32 devices in a mesh: dp: 8 (over z, y), mp: 4 (over x, core).
Axes of the slice: x: 2, y: 2, z: 4, core: 2. Of those that a mesh axis runs over, the one named last changes fastest.
Arguments:
- queries: bfloat16 [3072, 4096], P('dp', 'mp'), may hold values from -16 to 16
- states: bfloat16 [64, 128, 896], P('dp', 'mp'), may hold values from -6 to 6
- key_weight: bfloat16 [896, 4096], P(None, 'mp'), may hold values from -0.1875 to 0.1875
- value_weight: bfloat16 [896, 4096], P(None, 'mp'), may hold values from -0.1875 to 0.1875
- nbr_shard: int32 [48, 2], P('dp'), may hold values from 0 to 7, all different within a row; in each aligned block of 6 rows (0 to 5, 6 to 11, ...) at most 2 rows name the same one
- nbr_row: int32 [48, 2], P('dp'), may hold values from 0 to 7
- out_grad: bfloat16 [3072, 4096], P('dp', 'mp'), may hold values from -6 to 6
Outputs:
- attended: bfloat16 [3072, 4096], P('dp', 'mp')
- query_grad: bfloat16 [3072, 4096], P('dp', 'mp')
- state_grad: float32 [64, 128, 896], P('dp', 'mp')
- key_weight_grad: float32 [896, 4096], P(None, 'mp')
- value_weight_grad: float32 [896, 4096], P(None, 'mp')
The draws below stay inside these ranges and needn't reach their ends.
Inputs may be any that keep to these rules, and one draw needn't show every extreme that they name: `nbr_shard`: the 2 neighbours of a span lie on different shards; among the 6 spans of one device at most 2 neighbours lie on one shard, and some shard takes exactly 2 of them.
All inputs are finite; a program needn't handle non-finite values.
Results may differ from the reference program's by a relative error of at most 0.02.
Values may be sent and summed in bfloat16 or wider, within the bound.
No kernel may reach another device: no remote copies, remote signals or barrier semaphores. Data moves between devices by JAX's collectives and lax.ppermute only.
A program may use at most 128 MiB of HBM per device.

```python
import math
import jax
import jax.numpy as jnp
import numpy as np
from jax import lax

D = 4096
H = 32
E = 896
HD = 128
SPAN = 64
NLEN = 128
K = 2
C_DEV = 6
NB_DEV = 8
CAP = 2
SHARDS = 8
SPANS = 48
TOKENS = 3072
NBRS = 64
N_MP = 4


def draw_queries(key, part):
    key = jax.random.fold_in(key, 7)
    first = jax.random.fold_in(key, 0)
    values = jax.random.truncated_normal(first, -4.0, 4.0, (TOKENS, D), jnp.float32)
    return values.astype(jnp.bfloat16)


def with_ends(result, key, least, top_value):
    shape = result.shape
    place = [jax.random.randint(jax.random.fold_in(key, axis), (), 0, shape[axis]) for axis in range(len(shape))]
    result = result.at[tuple(place)].set(least)
    longest = shape.index(max(shape))
    place[longest] = (place[longest] + 1) % shape[longest]
    return result.at[tuple(place)].set(top_value)


def block_scale(key, dims, cuts, smallest, top_value):
    def one(position, blocks):
        steps = jax.random.uniform(jax.random.fold_in(jax.random.fold_in(key, 6), position), (blocks,), jnp.float32, smallest / len(cuts), top_value / len(cuts))
        return jnp.repeat(jnp.exp(steps), dims[position] // blocks).reshape((-1,) + (1,) * (len(dims) - position - 1))

    gain = one(*cuts[0])
    for cut in cuts[1:]:
        gain = gain * one(*cut)
    return gain


def routed_block(rng, own, number, rows, amount, top, most, lean):
    ranking = jax.random.permutation(rng, amount)
    heavy_load, usual = shares(amount, rows * top, most, lean, True), shares(amount, rows * top, most, lean, False)
    places = jnp.arange(amount)

    def named(lengths, turn):
        used = int((lengths > 0).sum())
        fixed = max(1, used // 4)
        shifted = fixed + (places - fixed + turn * (used - fixed)) % max(1, amount - fixed)
        return jnp.zeros((amount,), jnp.int32).at[ranking[jnp.where(places < fixed, places, shifted)]].set(jnp.asarray(lengths, jnp.int32))

    lengths = jnp.where(number % 4 == 0, named(heavy_load, number // 4), named(usual, number - number // 4 - 1))
    mixed = jax.random.permutation(jax.random.fold_in(own, 3), amount)
    donor, sink = mixed[0:amount // 2 * 2:2], mixed[1:amount // 2 * 2:2]
    margin = jnp.minimum(lengths[donor] - 1, most - lengths[sink]) // 2
    margin = jnp.where((donor == ranking[0]) | (sink == ranking[0]) | (lengths[sink] == 0), 0, jnp.maximum(margin, 0))
    shifted = jax.random.randint(jax.random.fold_in(own, 4), (amount // 2,), 0, 1 << 20) % (margin + 1)
    lengths = lengths.at[donor].add(-shifted).at[sink].add(shifted)
    items = jnp.searchsorted(jnp.cumsum(lengths), jnp.arange(rows * top), side="right").astype(jnp.int32)
    listing = items.reshape(top, rows).T
    listing = listing[jax.random.permutation(jax.random.fold_in(own, 1), rows)]
    turn = jax.random.randint(jax.random.fold_in(own, 2), (rows, 1), 0, top)
    return jnp.take_along_axis(listing, (jnp.arange(top)[None, :] + turn) % top, axis=1)


def shares(count, total, bound, lean, full):
    loads = [(1 << 20) // math.isqrt(standing ** lean) + 1 for standing in range(1, count + 1)]
    largest = bound if full else min(bound, max(-(-total // count), total * loads[0] // sum(loads)))
    least = 1 if total - largest >= count - 1 else 0
    given, rest = [largest] + [least] * (count - 1), total - largest - least * (count - 1)
    while rest > 0:
        free = [i for i in range(1, count) if given[i] < largest] or [i for i in range(1, count) if given[i] < bound]
        whole, left = sum([loads[i] for i in free]), rest
        for i in free:
            extra = min(bound - given[i], max(1, left * loads[i] // whole), rest)
            given[i] = given[i] + extra
            rest = rest - extra
    return np.array(given)


def gaussian(rng, dims, scale, reach, cuts=(), held_as=jnp.bfloat16):
    array = jax.random.normal(rng, dims, jnp.float32) * scale
    if len(cuts) > 0:
        array = block_scale(rng, dims, cuts, -0.22, 0.18) * array
    return jnp.clip(array, min=-reach, max=reach).astype(held_as)


def setup_inputs(seed: int = 0) -> dict:
    streams_of = jax.random.split(jax.random.key(seed), 8)
    queries = draw_queries(jax.random.fold_in(streams_of[7], 71), 0)
    states = gaussian(streams_of[1], (NBRS, NLEN, E), 1.0, 6.0, ((0, 8), (1, 4)))
    key_weight = gaussian(streams_of[2], (E, D), E ** -0.5, 0.1875, ((1, 4),))
    value_weight = gaussian(streams_of[3], (E, D), E ** -0.5, 0.1875, ((1, 4),))
    nbr_shard_keys = jax.random.split(jax.random.fold_in(streams_of[4], 1), SPANS // C_DEV)
    nbr_shard_turns = jax.random.permutation(jax.random.fold_in(streams_of[4], 3), SPANS // C_DEV)
    nbr_shard = jax.vmap(lambda own, number: routed_block(jax.random.fold_in(streams_of[4], 2), own, number, C_DEV, SHARDS, K, CAP, 2))(nbr_shard_keys, nbr_shard_turns).reshape((SPANS, K))
    nbr_row = with_ends(jax.random.randint(streams_of[5], (SPANS, K), 0, NB_DEV), jax.random.fold_in(streams_of[5], 1), 0, NB_DEV - 1).astype(jnp.int32)
    out_grad = gaussian(streams_of[6], (TOKENS, D), 1.0, 6.0, ((0, 8), (1, 4)))
    return dict(queries=queries, states=states, key_weight=key_weight, value_weight=value_weight, nbr_shard=nbr_shard, nbr_row=nbr_row, out_grad=out_grad)


def reference(queries, states, key_weight, value_weight, nbr_shard, nbr_row, out_grad):
    score_scale = 1.0 / (HD ** 0.5)
    group_cols = D // N_MP
    neighbour_ids = (nbr_shard * NB_DEV + nbr_row).astype(jnp.int32)
    query_heads = queries.reshape(SPANS, SPAN, H, HD)
    grad_heads = out_grad.reshape(SPANS, SPAN, H, HD)
    key_groups = key_weight.astype(jnp.float32).reshape(E, N_MP, group_cols)
    value_groups = value_weight.astype(jnp.float32).reshape(E, N_MP, group_cols)

    def one_span(carry, inputs):
        key_wgrad, value_wgrad, state_total = carry
        span_ids, query_span, grad_span = inputs
        rows_flat = states[span_ids].reshape(K * NLEN, E)
        key_rows = jnp.dot(rows_flat, key_weight, preferred_element_type=jnp.float32).astype(jnp.bfloat16)
        value_rows = jnp.dot(rows_flat, value_weight, preferred_element_type=jnp.float32).astype(jnp.bfloat16)
        key_heads = key_rows.reshape(K * NLEN, H, HD).astype(jnp.float32)
        value_heads = value_rows.reshape(K * NLEN, H, HD).astype(jnp.float32)
        query_f = query_span.astype(jnp.float32)
        grad_f = grad_span.astype(jnp.float32)
        scores = jnp.einsum('qhd,khd->hqk', query_f, key_heads) * score_scale
        probs = jax.nn.softmax(scores, axis=-1)
        probs_low = probs.astype(jnp.bfloat16)
        attended = jnp.einsum('hqk,khd->qhd', probs_low.astype(jnp.float32), value_heads).astype(jnp.bfloat16)
        prob_grad = jnp.einsum('qhd,khd->hqk', grad_f, value_heads)
        row_dot = jnp.sum(probs * prob_grad, axis=-1, keepdims=True)
        score_grad = (score_scale * probs * (prob_grad - row_dot)).astype(jnp.bfloat16)
        score_f = score_grad.astype(jnp.float32)
        query_grad = jnp.einsum('hqk,khd->qhd', score_f, key_heads).astype(jnp.bfloat16)
        key_grad = jnp.einsum('hqk,qhd->khd', score_f, query_f).astype(jnp.bfloat16).reshape(K * NLEN, D)
        value_grad = jnp.einsum('hqk,qhd->khd', probs_low.astype(jnp.float32), grad_f).astype(jnp.bfloat16).reshape(K * NLEN, D)
        key_wgrad = key_wgrad + jnp.dot(rows_flat.T, key_grad, preferred_element_type=jnp.float32)
        value_wgrad = value_wgrad + jnp.dot(rows_flat.T, value_grad, preferred_element_type=jnp.float32)
        key_split = key_grad.astype(jnp.float32).reshape(K * NLEN, N_MP, group_cols)
        value_split = value_grad.astype(jnp.float32).reshape(K * NLEN, N_MP, group_cols)
        head_part = jnp.einsum('tgd,egd->gte', key_split, key_groups) + jnp.einsum('tgd,egd->gte', value_split, value_groups)
        head_low = lax.optimization_barrier(head_part.astype(jnp.bfloat16))
        pair_grad = jnp.sum(head_low.astype(jnp.float32), axis=0).astype(jnp.bfloat16)
        state_total = state_total.at[span_ids].add(pair_grad.reshape(K, NLEN, E).astype(jnp.float32))
        return (key_wgrad, value_wgrad, state_total), (attended, query_grad)

    start = (jnp.zeros((E, D), jnp.float32), jnp.zeros((E, D), jnp.float32), jnp.zeros((NBRS, NLEN, E), jnp.float32))
    finals, outputs = lax.scan(one_span, start, (neighbour_ids, query_heads, grad_heads))
    key_wgrad, value_wgrad, state_total = finals
    attended = outputs[0].reshape(TOKENS, D)
    query_grad = outputs[1].reshape(TOKENS, D)
    return (attended, query_grad, state_total, key_wgrad, value_wgrad)
```

```python
import functools

import jax
import jax.numpy as jnp
from jax import lax
from jax.experimental import pallas as pl
from jax.experimental.pallas import tpu as pltpu
from jax.sharding import PartitionSpec as P

D = 4096
H = 32
VMEM_GRANT = 28 * 1024 * 1024
SMALL_GRANT = 12 * 1024 * 1024
CHEAP = pl.CostEstimate(flops=1, bytes_accessed=1, transcendentals=0)


def bits_of(count):
    return count.bit_length() - 1


def swap(value, axis, bit):
    count = lax.axis_size(axis)
    return lax.ppermute(value, axis, [(i, i ^ (1 << bit)) for i in range(count)])


def any_spec():
    return pl.BlockSpec(memory_space=pl.ANY)


def hbm_spec():
    return pl.BlockSpec(memory_space=pltpu.HBM)


def head_kernel(groups, spans, head_dim, start, extra, *refs):
    flag_ref = refs[0]
    slabs = refs[1 : 1 + groups]
    wk_hbm, wv_hbm, q_hbm, g_hbm = refs[1 + groups : 5 + groups]
    att_hbm, dq_hbm, dk_hbm, dv_hbm, keep_ref, send_ref = refs[5 + groups + extra : 11 + groups + extra]
    rows, wk, wv, q_ref, g_ref, keys, values, att_ref, dq_ref, dk_ref, dv_ref, grads, sems = refs[11 + groups + extra :]
    tokens, width = q_ref.shape
    span_len = tokens // spans
    block = rows.shape[0] // groups
    part = block // spans
    scale = 1.0 / head_dim**0.5
    columns = pl.ds(start, width)

    def begin(source, target, sem):
        copy = pltpu.make_async_copy(source, target, sems.at[sem])
        copy.start()
        return copy

    weights_in = [begin(wk_hbm.at[:, columns], wk, groups), begin(wv_hbm.at[:, columns], wv, groups + 1)]
    rows_in = [begin(slabs[r], rows.at[pl.ds(r * block, block)], r) for r in range(groups)]
    tokens_in = [begin(q_hbm.at[:, columns], q_ref, groups + 2), begin(g_hbm.at[:, columns], g_ref, groups + 3)]
    for copy in weights_in:
        copy.wait()
    for r in range(groups):
        rows_in[r].wait()
        at = pl.ds(r * block, block)
        keys[at, :] = jnp.dot(rows[at, :], wk[...], preferred_element_type=jnp.float32).astype(jnp.bfloat16)
        values[at, :] = jnp.dot(rows[at, :], wv[...], preferred_element_type=jnp.float32).astype(jnp.bfloat16)
    for copy in tokens_in:
        copy.wait()

    def spread(x):
        heads = x.shape[1] // head_dim
        lane_head = lax.broadcasted_iota(jnp.int32, x.shape, 1) // head_dim
        zero = jnp.zeros_like(x)
        return jnp.concatenate([jnp.where(lane_head == h, x, zero) for h in range(heads)], axis=0)

    def collect(x):
        out = x[0:span_len]
        lane_head = lax.broadcasted_iota(jnp.int32, out.shape, 1) // head_dim
        for h in range(1, x.shape[1] // head_dim):
            out = jnp.where(lane_head == h, x[h * span_len : (h + 1) * span_len], out)
        return out

    def span_rows(ref, c, cols):
        return jnp.concatenate([ref[pl.ds(r * block + c * part, part), cols] for r in range(groups)], axis=0)

    contract_last = (((1,), (1,)), ((), ()))
    contract_first = (((0,), (0,)), ((), ()))
    at = [pl.ds(c * span_len, span_len) for c in range(spans)]
    swapped = flag_ref[0] == 1
    pair = 2 * head_dim
    for first in range(0, width, pair):
        cols = slice(first, min(first + pair, width))
        send_cols = slice(width + cols.start, width + cols.stop)
        every = range(spans)
        scores = [
            lax.dot_general(
                span_rows(keys, c, cols), spread(q_ref[at[c], cols]), contract_last,
                preferred_element_type=jnp.float32,
            )
            * scale
            for c in every
        ]
        prob_grad = [
            lax.dot_general(
                span_rows(values, c, cols), spread(g_ref[at[c], cols]), contract_last,
                preferred_element_type=jnp.float32,
            )
            for c in every
        ]
        weights = [jnp.exp(x - jnp.max(x, axis=0, keepdims=True)) for x in scores]
        probs = [x * (1.0 / jnp.sum(x, axis=0, keepdims=True)) for x in weights]
        low = [x.astype(jnp.bfloat16) for x in probs]
        row_dot = [jnp.sum(p * d, axis=0, keepdims=True) for p, d in zip(probs, prob_grad)]
        score_grad = [(scale * p * (d - t)).astype(jnp.bfloat16) for p, d, t in zip(probs, prob_grad, row_dot)]
        for c in every:
            dk = jnp.dot(score_grad[c], spread(q_ref[at[c], cols]), preferred_element_type=jnp.float32)
            dv = jnp.dot(low[c], spread(g_ref[at[c], cols]), preferred_element_type=jnp.float32)
            dk, dv = dk.astype(jnp.bfloat16), dv.astype(jnp.bfloat16)
            for r in range(groups):
                to = pl.ds(r * block + c * part, part)
                piece = slice(r * part, (r + 1) * part)
                dk_ref[to, cols] = dk[piece]
                dv_ref[to, cols] = dv[piece]
                grads[to, cols] = jnp.where(swapped, dv[piece], dk[piece])
                grads[to, send_cols] = jnp.where(swapped, dk[piece], dv[piece])
        for c in every:
            att = lax.dot_general(
                low[c], span_rows(values, c, cols), contract_first, preferred_element_type=jnp.float32
            )
            att_ref[at[c], cols] = collect(att).astype(jnp.bfloat16)
            dq = lax.dot_general(
                score_grad[c], span_rows(keys, c, cols), contract_first, preferred_element_type=jnp.float32
            )
            dq_ref[at[c], cols] = collect(dq).astype(jnp.bfloat16)
    results = [
        begin(att_ref, att_hbm.at[:, columns], 0),
        begin(dq_ref, dq_hbm.at[:, columns], 1),
        begin(dk_ref, dk_hbm, 2),
        begin(dv_ref, dv_hbm, 3),
    ]
    both = lax.dot_general(rows[...], grads[...], contract_first, preferred_element_type=jnp.float32)
    keep_ref[...] = both[:, :width]
    send_ref[...] = both[:, width:].astype(jnp.bfloat16)
    for copy in results:
        copy.wait()


def run_heads(start, chunk, flag, slabs, key_weight, value_weight, queries, out_grad, chain, after, spans, head_dim):
    groups = len(slabs)
    tokens, local_width = queries.shape
    block, enc = slabs[0].shape
    total = groups * block
    bf = jnp.bfloat16
    extra = list(chain) + list(after)
    outs = pl.pallas_call(
        functools.partial(head_kernel, groups, spans, head_dim, start, len(extra)),
        out_shape=[
            jax.ShapeDtypeStruct((tokens, local_width), bf),
            jax.ShapeDtypeStruct((tokens, local_width), bf),
            jax.ShapeDtypeStruct((total, chunk), bf),
            jax.ShapeDtypeStruct((total, chunk), bf),
            jax.ShapeDtypeStruct((enc, chunk), jnp.float32),
            jax.ShapeDtypeStruct((enc, chunk), bf),
        ],
        in_specs=[pl.BlockSpec(memory_space=pltpu.SMEM)]
        + [any_spec()] * groups
        + [hbm_spec()] * (4 + len(chain))
        + [any_spec()] * len(after),
        out_specs=[hbm_spec()] * 4 + [pl.BlockSpec(memory_space=pltpu.VMEM)] * 2,
        scratch_shapes=[
            pltpu.VMEM((total, enc), bf),
            pltpu.VMEM((enc, chunk), bf),
            pltpu.VMEM((enc, chunk), bf),
            pltpu.VMEM((tokens, chunk), bf),
            pltpu.VMEM((tokens, chunk), bf),
            pltpu.VMEM((total, chunk), bf),
            pltpu.VMEM((total, chunk), bf),
            pltpu.VMEM((tokens, chunk), bf),
            pltpu.VMEM((tokens, chunk), bf),
            pltpu.VMEM((total, chunk), bf),
            pltpu.VMEM((total, chunk), bf),
            pltpu.VMEM((total, 2 * chunk), bf),
            pltpu.SemaphoreType.DMA((groups + 4,)),
        ],
        input_output_aliases={5 + groups + i: i for i in range(len(chain))},
        compiler_params=pltpu.CompilerParams(vmem_limit_bytes=VMEM_GRANT),
        cost_estimate=pl.CostEstimate(
            flops=2 * total * enc * chunk * 8, bytes_accessed=4 * total * enc, transcendentals=total * tokens
        ),
        name="heads",
    )(flag, *slabs, key_weight, value_weight, queries, out_grad, *extra)
    return outs[:2], outs[2], outs[3], outs[4:]


def state_kernel(groups, widths, extra, *refs):
    count = len(widths)
    dk_hbm, dv_hbm = refs[:count], refs[count : 2 * count]
    wk_hbm, wv_hbm = refs[2 * count : 2 * count + 2]
    keep_ref, send_ref, grads, weights, sems = refs[2 * count + 2 + extra :]
    half = weights.shape[1] // 2
    block = grads.shape[0] // groups

    copies = [
        pltpu.make_async_copy(wk_hbm, weights.at[:, pl.ds(0, half)], sems.at[0, 0]),
        pltpu.make_async_copy(wv_hbm, weights.at[:, pl.ds(half, half)], sems.at[0, 1]),
    ]
    blocks = []
    for r in range(groups):
        rows = pl.ds(r * block, block)
        parts = []
        for j in range(count):
            first = sum(widths[:j])
            for k, source in enumerate((dk_hbm[j], dv_hbm[j])):
                target = grads.at[rows, pl.ds(k * half + first, widths[j])]
                parts.append(pltpu.make_async_copy(source.at[rows, :], target, sems.at[1 + r, 2 * j + k]))
        blocks.append(parts)
    for copy in copies:
        copy.start()
    for parts in blocks:
        for copy in parts:
            copy.start()
    for copy in copies:
        copy.wait()
    for r in range(groups):
        for copy in blocks[r]:
            copy.wait()
        term = lax.dot_general(
            grads[pl.ds(r * block, block), :], weights[...], (((1,), (1,)), ((), ())),
            preferred_element_type=jnp.float32,
        )
        to = pl.ds((r // 2) * block, block)
        if r % 2:
            send_ref[to, :] = term.astype(jnp.bfloat16)
        else:
            keep_ref[to, :] = term


def run_state(groups, dk, dv, key_weight, value_weight, after):
    total = dk[0].shape[0]
    enc, local_width = key_weight.shape
    widths = [x.shape[1] for x in dk]
    vmem = pl.BlockSpec(memory_space=pltpu.VMEM)
    return pl.pallas_call(
        functools.partial(state_kernel, groups, widths, len(after)),
        out_shape=[
            jax.ShapeDtypeStruct((total // 2, enc), jnp.float32),
            jax.ShapeDtypeStruct((total // 2, enc), jnp.bfloat16),
        ],
        in_specs=[hbm_spec()] * (2 * len(dk) + 2) + [any_spec()] * len(after),
        out_specs=[vmem, vmem],
        scratch_shapes=[
            pltpu.VMEM((total, 2 * local_width), jnp.bfloat16),
            pltpu.VMEM((enc, 2 * local_width), jnp.bfloat16),
            pltpu.SemaphoreType.DMA((groups + 1, max(2, 2 * len(dk)))),
        ],
        compiler_params=pltpu.CompilerParams(vmem_limit_bytes=VMEM_GRANT),
        cost_estimate=pl.CostEstimate(
            flops=8 * total * enc * local_width, bytes_accessed=8 * total * enc, transcendentals=0
        ),
        name="state_terms",
    )(*dk, *dv, key_weight, value_weight, *after)


def fold_kernel(rows_ref, returned_ref, *refs):
    out_ref = refs[-1]
    out_ref[...] = jnp.zeros_like(out_ref)
    count = out_ref.shape[0]
    for s in range(returned_ref.shape[0]):
        row = rows_ref[s]

        @pl.when(row < count)
        def _():
            out_ref[row] += returned_ref[s].astype(jnp.float32)


def halve_kernel(choice_ref, keep_ref, recv_ref, *refs):
    stay_ref, send_ref = refs[-2:]
    total = keep_ref[...] + recv_ref[...].astype(jnp.float32)
    half = stay_ref.shape[0]
    upper = choice_ref[0] == 1
    stay_ref[...] = jnp.where(upper, total[half:], total[:half])
    send_ref[...] = jnp.where(upper, total[:half], total[half:]).astype(jnp.bfloat16)


def split_kernel(keep_ref, recv_ref, *refs):
    stay_ref, send_ref = refs[-2:]
    half = stay_ref.shape[0]
    stay_ref[...] = keep_ref[:half] + recv_ref[:half].astype(jnp.float32)
    send_ref[...] = (keep_ref[half:] + recv_ref[half:].astype(jnp.float32)).astype(jnp.bfloat16)


def add_kernel(keep_ref, recv_ref, *refs):
    refs[-1][...] = (keep_ref[...] + recv_ref[...].astype(jnp.float32)).astype(refs[-1].dtype)


def join_kernel(choice_ref, own_ref, recv_ref, *refs):
    out_ref = refs[-1]
    upper = choice_ref[0] == 1
    own, recv = own_ref[...], recv_ref[...]
    rows = own.shape[0]
    if rows % 16:
        own, recv = own.astype(jnp.float32), recv.astype(jnp.float32)
        out = jnp.concatenate([jnp.where(upper, recv, own), jnp.where(upper, own, recv)], axis=0)
        out_ref[...] = out.astype(out_ref.dtype)
    else:
        out_ref[:rows] = jnp.where(upper, recv, own)
        out_ref[rows:] = jnp.where(upper, own, recv)


def place_kernel(start, choice_ref, own_ref, recv_ref, *refs):
    key_hbm, value_hbm, token_ref, key_ref, value_ref, sems = refs[-6:]
    token_ref[...] = jnp.zeros_like(token_ref)
    swapped = choice_ref[0] == 1
    own, recv = own_ref[...].astype(jnp.float32), recv_ref[...].astype(jnp.float32)
    columns = pl.ds(start, own.shape[1])
    key_ref[...] = jnp.where(swapped, recv, own)
    key_out = pltpu.make_async_copy(key_ref, key_hbm.at[:, columns], sems.at[0])
    key_out.start()
    value_ref[...] = jnp.where(swapped, own, recv)
    value_out = pltpu.make_async_copy(value_ref, value_hbm.at[:, columns], sems.at[1])
    value_out.start()
    key_out.wait()
    value_out.wait()


def small(kernel, name, scalars, arrays, outs, after, alias_in=(), out_specs=None, scratch=()):
    vmem = pl.BlockSpec(memory_space=pltpu.VMEM)
    extra = list(alias_in) + list(after)
    first = len(scalars) + len(arrays)
    return pl.pallas_call(
        kernel,
        out_shape=outs,
        in_specs=[pl.BlockSpec(memory_space=pltpu.SMEM)] * len(scalars)
        + [vmem] * len(arrays)
        + [hbm_spec()] * len(alias_in)
        + [any_spec()] * len(after),
        out_specs=out_specs or [vmem] * len(outs),
        scratch_shapes=list(scratch),
        input_output_aliases={first + i: i for i in range(len(alias_in))},
        compiler_params=pltpu.CompilerParams(vmem_limit_bytes=SMALL_GRANT),
        cost_estimate=CHEAP,
        name=name,
    )(*scalars, *arrays, *extra)


class Sum:
    def __init__(self, order, choices, start, enc, width):
        self.choices, self.start, self.enc, self.width = choices, start, enc, width
        self.count = len(order)
        self.steps = list(order) + list(reversed(order))
        self.at = 0

    def begin(self, keep, send):
        self.keep = keep
        self.moving = swap(send, "dp", self.steps[0])

    def load(self, step):
        return self.enc >> (step if step < self.count else 2 * self.count - 1 - step)

    def advance(self, after, outs):
        count, at = self.count, self.at
        self.at += 1
        rows = self.load(at)
        shape = lambda rows, dtype: jax.ShapeDtypeStruct((rows, self.width), dtype)
        if at < count - 1:
            choice = self.choices[self.steps[at + 1]]
            self.keep, send = small(
                halve_kernel, "halve", [choice], [self.keep, self.moving],
                [shape(rows // 2, jnp.float32), shape(rows // 2, jnp.bfloat16)], after,
            )
        elif at == count - 1:
            (send,) = small(add_kernel, "add", [], [self.keep, self.moving], [shape(rows, jnp.bfloat16)], after)
        elif at < 2 * count - 1:
            choice = self.choices[self.steps[at]]
            (send,) = small(
                join_kernel, "join", [choice], [self.own, self.moving], [shape(2 * rows, jnp.bfloat16)], after
            )
        else:
            choice = self.choices[self.steps[at]]
            full = jax.ShapeDtypeStruct(self.full, jnp.float32)
            block = pltpu.VMEM((self.enc, self.width), jnp.float32)
            token = jax.ShapeDtypeStruct((8, 128), jnp.float32)
            *outs, done = small(
                functools.partial(place_kernel, self.start), "place", [choice], [self.own, self.moving],
                [full, full, token], after, alias_in=outs,
                out_specs=[hbm_spec()] * 2 + [pl.BlockSpec(memory_space=pltpu.VMEM)],
                scratch=[block, block, pltpu.SemaphoreType.DMA((2,))],
            )
            return done, outs
        self.own = send
        self.moving = swap(send, "dp", self.steps[at + 1])
        return send, outs


def wavefront(chunks, steps, rest):
    order, period = [], 0
    done = [0] * chunks
    rest_done = 0
    while min(done) < steps or rest_done < rest:
        begun = min(period, chunks)
        if period < chunks:
            order.append(f"heads{period}")
        elif period == chunks:
            order.append("state")
        for j in range(begun):
            if done[j] < steps:
                order.append(f"sum{j}")
                done[j] += 1
        if period > chunks and rest_done < rest and (rest_done < rest - 2 or min(done) >= steps - 1):
            order.append("rest")
            rest_done += 1
        period += 1
    return order


def body(queries, states, key_weight, value_weight, nbr_shard, nbr_row, out_grad):
    shards = lax.axis_size("dp")
    groups = lax.axis_size("mp")
    dp_bits, mp_bits = bits_of(shards), bits_of(groups)
    dp_index = lax.axis_index("dp")
    spans, neighbours = nbr_shard.shape
    pair_count = spans * neighbours
    tokens, local_width = queries.shape
    stored, slab_len, enc_width = states.shape
    head_dim = D // H
    capacity = max(2, (pair_count + shards - 1) // shards)
    slot_count = shards * capacity

    owners = nbr_shard.reshape(pair_count)
    row_index = nbr_row.reshape(pair_count)
    pair_ids = jnp.arange(pair_count, dtype=jnp.int32)
    before = (owners[:, None] == owners[None, :]) & (pair_ids[None, :] < pair_ids[:, None])
    slot_index = owners * capacity + jnp.sum(before.astype(jnp.int32), axis=1)
    matched = slot_index[:, None] == jnp.arange(slot_count, dtype=jnp.int32)[None, :]
    asked = stored + jnp.sum(jnp.where(matched, row_index[:, None] - stored, 0), axis=0)
    slot_pair = jnp.sum(jnp.where(matched, pair_ids[:, None], 0), axis=0)
    incoming = lax.all_to_all(
        asked.reshape(shards, capacity), "dp", split_axis=0, concat_axis=0, tiled=True
    ).reshape(slot_count)
    slab_rows = jnp.take(states, jnp.minimum(incoming, stored - 1), axis=0, mode="clip")
    sent_back = lax.all_to_all(
        slab_rows.reshape(shards, capacity, slab_len, enc_width), "dp", split_axis=0, concat_axis=0, tiled=True
    ).reshape(slot_count, slab_len, enc_width)
    picked = jnp.take(sent_back, slot_index, axis=0, mode="clip").reshape(pair_count * slab_len, enc_width)

    blocks = {0: picked}
    for bit in reversed(range(mp_bits)):
        for r in list(blocks):
            blocks[r | (1 << bit)] = swap(blocks[r], "mp", bit)
    slabs = [blocks[r] for r in range(groups)]

    heads = local_width // head_dim
    counts = [min(2, heads - first) for first in range(0, heads, 2)]
    bits = list(range(dp_bits))
    choices = [((dp_index >> bit) & 1).astype(jnp.int32).reshape(1) for bit in bits]
    sums = []
    for j, count in enumerate(counts):
        sums.append(Sum(bits, choices, sum(counts[:j]) * head_dim, enc_width, count * head_dim))
        sums[j].full = key_weight.shape

    after, chain, outs, dk, dv = [], [], [], [], []
    rest_bit = 0
    for name in wavefront(len(sums), 2 * dp_bits, mp_bits + 1):
        kind = name.rstrip("0123456789")
        number = int(name[len(kind) :] or 0)
        if kind == "heads":
            part = sums[number]
            chain, dk_part, dv_part, (keep, send) = run_heads(
                part.start, part.width, choices[part.steps[0]], slabs, key_weight, value_weight, queries, out_grad,
                chain, after, spans, head_dim,
            )
            dk.append(dk_part)
            dv.append(dv_part)
            part.begin(keep, send)
            after = [send]
        elif kind == "sum":
            done, outs = sums[number].advance(after, outs)
            after = [done]
        elif kind == "state":
            keep, send = run_state(groups, dk, dv, key_weight, value_weight, after)
            moving = swap(send, "mp", 0)
            after = [send]
        elif rest_bit < mp_bits - 1:
            half = keep.shape[0] // 2
            keep, send = small(
                split_kernel, "split", [], [keep, moving],
                [jax.ShapeDtypeStruct((half, enc_width), t) for t in (jnp.float32, jnp.bfloat16)], after,
            )
            moving = swap(send, "mp", mp_bits - 1 - rest_bit)
            after = [send]
            rest_bit += 1
        elif rest_bit == mp_bits - 1:
            (pair_grad,) = small(
                add_kernel, "add", [], [keep, moving], [jax.ShapeDtypeStruct(keep.shape, jnp.bfloat16)], after
            )
            after = [pair_grad]
            outgoing = jnp.take(
                pair_grad.reshape(pair_count, slab_len, enc_width), slot_pair, axis=0, mode="clip"
            ).reshape(shards, capacity, slab_len, enc_width)
            returned = lax.all_to_all(outgoing, "dp", split_axis=0, concat_axis=0, tiled=True)
            rest_bit += 1
        else:
            (state_total,) = small(
                fold_kernel, "fold", [incoming], [returned.reshape(slot_count, slab_len, enc_width)],
                [jax.ShapeDtypeStruct(states.shape, jnp.float32)], after,
            )
    return (chain[0], chain[1], state_total, outs[0], outs[1])


def solution(mesh):
    placed = (
        P("dp", "mp"),
        P("dp", "mp", None),
        P(None, "mp"),
        P(None, "mp"),
        P("dp", None),
        P("dp", None),
        P("dp", "mp"),
    )
    return jax.shard_map(
        body,
        mesh=mesh,
        in_specs=placed,
        out_specs=(P("dp", "mp"), P("dp", "mp"), P("dp", "mp", None), P(None, "mp"), P(None, "mp")),
        check_vma=False,
    )
```

```python
import functools

import jax
import jax.numpy as jnp
from jax import lax
from jax.experimental import pallas as pl
from jax.experimental.pallas import tpu as pltpu
from jax.sharding import PartitionSpec as P

D = 4096
H = 32
VMEM_GRANT = 28 * 1024 * 1024
SMALL_GRANT = 12 * 1024 * 1024
CHEAP = pl.CostEstimate(flops=1, bytes_accessed=1, transcendentals=0)


def bits_of(count):
    return count.bit_length() - 1


def swap(value, axis, bit):
    count = lax.axis_size(axis)
    return lax.ppermute(value, axis, [(i, i ^ (1 << bit)) for i in range(count)])


def any_spec():
    return pl.BlockSpec(memory_space=pl.ANY)


def in_hbm(arrays):
    return [pltpu.with_memory_space_constraint(x, pltpu.HBM) for x in arrays]


def hbm_spec():
    return pl.BlockSpec(memory_space=pltpu.HBM)


def turn_kernel(wk, wv, out_ref, held, sem):
    half = held.shape[0] // 2
    held[:half] = wk[...].T
    held[half:] = wv[...].T
    copy = pltpu.make_async_copy(held, out_ref, sem)
    copy.start()
    copy.wait()


def run_turn(key_weight, value_weight):
    enc, width = key_weight.shape
    vmem = pl.BlockSpec(memory_space=pltpu.VMEM)
    return pl.pallas_call(
        turn_kernel,
        out_shape=pltpu.HBM((2 * width, enc), key_weight.dtype),
        in_specs=[vmem, vmem],
        out_specs=hbm_spec(),
        scratch_shapes=[pltpu.VMEM((2 * width, enc), key_weight.dtype), pltpu.SemaphoreType.DMA],
        compiler_params=pltpu.CompilerParams(vmem_limit_bytes=VMEM_GRANT),
        cost_estimate=pl.CostEstimate(flops=enc * width * 2000, bytes_accessed=8 * enc * width, transcendentals=0),
        name="turn",
    )(key_weight, value_weight)


def project_kernel(count, *refs):
    slabs = refs[:count]
    wk, wv = refs[count : count + 2]
    outs, (keys, values, turned, sems) = refs[-7:-4], refs[-4:]

    def store(i, held, value):
        held[...] = value.astype(jnp.bfloat16)
        copy = pltpu.make_async_copy(held, outs[i], sems.at[i])
        copy.start()
        return copy

    rows = slabs[0][...] if count == 1 else jnp.concatenate([slab[...] for slab in slabs], axis=0)
    copies = [
        store(0, keys, jnp.dot(rows, wk[...], preferred_element_type=jnp.float32)),
        store(1, values, jnp.dot(rows, wv[...], preferred_element_type=jnp.float32)),
        store(2, turned, rows.T),
    ]
    for copy in copies:
        copy.wait()


def run_project(slabs, key_weight, value_weight, after):
    enc, width = key_weight.shape
    rows = sum(slab.shape[0] for slab in slabs)
    vmem = pl.BlockSpec(memory_space=pltpu.VMEM)
    shapes = [(rows, width), (rows, width), (enc, rows)]
    return pl.pallas_call(
        functools.partial(project_kernel, len(slabs)),
        out_shape=[pltpu.HBM(shape, jnp.bfloat16) for shape in shapes],
        in_specs=[vmem] * (len(slabs) + 2) + [hbm_spec()] * len(after),
        out_specs=[hbm_spec()] * 3,
        scratch_shapes=[pltpu.VMEM(shape, jnp.bfloat16) for shape in shapes] + [pltpu.SemaphoreType.DMA((3,))],
        compiler_params=pltpu.CompilerParams(vmem_limit_bytes=VMEM_GRANT),
        cost_estimate=pl.CostEstimate(
            flops=4 * rows * enc * width, bytes_accessed=4 * (rows + enc) * width, transcendentals=0
        ),
        name="project",
    )(*slabs, key_weight, value_weight, *in_hbm(after))


def head_kernel(groups, spans, head_dim, start, parts, extra, *refs):
    flag_ref = refs[0]
    count = len(parts)
    keys_hbm, values_hbm, turned_hbm = refs[1 : 1 + count], refs[1 + count : 1 + 2 * count], refs[1 + 2 * count : 1 + 3 * count]
    q_hbm, g_hbm = refs[1 + 3 * count : 3 + 3 * count]
    refs = refs[3 + 3 * count + extra :]
    att_hbm, dq_hbm, dk_hbm, dv_hbm, keep_ref, send_ref = refs[:6]
    turned, q_ref, g_ref, keys, values, att_ref, dq_ref, dk_ref, dv_ref, grads, sems = refs[6:]
    tokens, width = q_ref.shape
    span_len = tokens // spans
    block = keys.shape[0] // groups
    part = block // spans
    scale = 1.0 / head_dim**0.5
    columns = pl.ds(start, width)

    def begin(source, target, sem):
        copy = pltpu.make_async_copy(source, target, sems.at[sem])
        copy.start()
        return copy

    copies = [begin(q_hbm.at[:, columns], q_ref, 0), begin(g_hbm.at[:, columns], g_ref, 1)]
    first = 0
    for i, size in enumerate(parts):
        to = pl.ds(first, size)
        copies.append(begin(keys_hbm[i].at[:, columns], keys.at[to], 2 + 3 * i))
        copies.append(begin(values_hbm[i].at[:, columns], values.at[to], 3 + 3 * i))
        first += size
    later, first = [], 0
    for i, size in enumerate(parts):
        later.append(begin(turned_hbm[i], turned.at[:, pl.ds(first, size)], 4 + 3 * i))
        first += size
    for copy in copies:
        copy.wait()

    def spread(x):
        heads = x.shape[1] // head_dim
        lane_head = lax.broadcasted_iota(jnp.int32, x.shape, 1) // head_dim
        zero = jnp.zeros_like(x)
        return jnp.concatenate([jnp.where(lane_head == h, x, zero) for h in range(heads)], axis=0)

    def collect(x):
        out = x[0:span_len]
        lane_head = lax.broadcasted_iota(jnp.int32, out.shape, 1) // head_dim
        for h in range(1, x.shape[1] // head_dim):
            out = jnp.where(lane_head == h, x[h * span_len : (h + 1) * span_len], out)
        return out

    def span_rows(ref, c):
        return jnp.concatenate([ref[pl.ds(r * block + c * part, part), :] for r in range(groups)], axis=0)

    contract_last = (((1,), (1,)), ((), ()))
    contract_first = (((0,), (0,)), ((), ()))
    at = [pl.ds(c * span_len, span_len) for c in range(spans)]
    swapped = flag_ref[0] == 1
    every = range(spans)
    scores = [
        lax.dot_general(
            span_rows(keys, c), spread(q_ref[at[c], :]), contract_last, preferred_element_type=jnp.float32
        )
        * scale
        for c in every
    ]
    prob_grad = [
        lax.dot_general(
            span_rows(values, c), spread(g_ref[at[c], :]), contract_last, preferred_element_type=jnp.float32
        )
        for c in every
    ]
    weights = [jnp.exp(x - jnp.max(x, axis=0, keepdims=True)) for x in scores]
    probs = [x * (1.0 / jnp.sum(x, axis=0, keepdims=True)) for x in weights]
    low = [x.astype(jnp.bfloat16) for x in probs]
    row_dot = [jnp.sum(p * d, axis=0, keepdims=True) for p, d in zip(probs, prob_grad)]
    score_grad = [(scale * p * (d - t)).astype(jnp.bfloat16) for p, d, t in zip(probs, prob_grad, row_dot)]
    for c in every:
        dk = jnp.dot(score_grad[c], spread(q_ref[at[c], :]), preferred_element_type=jnp.float32)
        dv = jnp.dot(low[c], spread(g_ref[at[c], :]), preferred_element_type=jnp.float32)
        dk, dv = dk.astype(jnp.bfloat16), dv.astype(jnp.bfloat16)
        for r in range(groups):
            to = pl.ds(r * block + c * part, part)
            piece = slice(r * part, (r + 1) * part)
            dk_ref[to, :] = dk[piece]
            dv_ref[to, :] = dv[piece]
            grads[to, :width] = jnp.where(swapped, dv[piece], dk[piece])
            grads[to, width:] = jnp.where(swapped, dk[piece], dv[piece])
    for c in every:
        att = lax.dot_general(low[c], span_rows(values, c), contract_first, preferred_element_type=jnp.float32)
        att_ref[at[c], :] = collect(att).astype(jnp.bfloat16)
        dq = lax.dot_general(score_grad[c], span_rows(keys, c), contract_first, preferred_element_type=jnp.float32)
        dq_ref[at[c], :] = collect(dq).astype(jnp.bfloat16)
    results = [
        begin(att_ref, att_hbm.at[:, columns], 0),
        begin(dq_ref, dq_hbm.at[:, columns], 1),
        begin(dk_ref, dk_hbm, 2),
        begin(dv_ref, dv_hbm, 3),
    ]
    for copy in later:
        copy.wait()
    both = jnp.dot(turned[...], grads[...], preferred_element_type=jnp.float32)
    keep_ref[...] = both[:, :width]
    send_ref[...] = both[:, width:].astype(jnp.bfloat16)
    for copy in results:
        copy.wait()


def run_heads(start, chunk, flag, parts, groups, queries, out_grad, chain, after, spans, head_dim):
    tokens, local_width = queries.shape
    keys, values, turned = zip(*parts)
    sizes = [k.shape[0] for k in keys]
    total, enc = sum(sizes), turned[0].shape[0]
    bf = jnp.bfloat16
    extra = list(chain) + list(after)
    first = 3 + 3 * len(parts)
    outs = pl.pallas_call(
        functools.partial(head_kernel, groups, spans, head_dim, start, sizes, len(extra)),
        out_shape=[
            pltpu.HBM((tokens, local_width), bf),
            pltpu.HBM((tokens, local_width), bf),
            pltpu.HBM((total, chunk), bf),
            pltpu.HBM((total, chunk), bf),
            jax.ShapeDtypeStruct((enc, chunk), jnp.float32),
            jax.ShapeDtypeStruct((enc, chunk), bf),
        ],
        in_specs=[pl.BlockSpec(memory_space=pltpu.SMEM)]
        + [hbm_spec()] * (3 * len(parts) + 2 + len(chain))
        + [any_spec()] * len(after),
        out_specs=[hbm_spec()] * 4 + [pl.BlockSpec(memory_space=pltpu.VMEM)] * 2,
        scratch_shapes=[
            pltpu.VMEM((enc, total), bf),
            pltpu.VMEM((tokens, chunk), bf),
            pltpu.VMEM((tokens, chunk), bf),
            pltpu.VMEM((total, chunk), bf),
            pltpu.VMEM((total, chunk), bf),
            pltpu.VMEM((tokens, chunk), bf),
            pltpu.VMEM((tokens, chunk), bf),
            pltpu.VMEM((total, chunk), bf),
            pltpu.VMEM((total, chunk), bf),
            pltpu.VMEM((total, 2 * chunk), bf),
            pltpu.SemaphoreType.DMA((2 + 3 * len(parts),)),
        ],
        input_output_aliases={first + i: i for i in range(len(chain))},
        compiler_params=pltpu.CompilerParams(vmem_limit_bytes=VMEM_GRANT),
        cost_estimate=pl.CostEstimate(
            flops=2 * total * enc * chunk * 6, bytes_accessed=4 * total * enc, transcendentals=total * tokens
        ),
        name="heads",
    )(flag, *in_hbm([*keys, *values, *turned, queries, out_grad, *chain]), *after)
    return outs[:2], outs[2], outs[3], outs[4:]


def state_kernel(groups, widths, extra, *refs):
    count = len(widths)
    dk_hbm, dv_hbm, weights_hbm = refs[:count], refs[count : 2 * count], refs[2 * count]
    keep_ref, send_ref, grads, weights, sems = refs[2 * count + 1 + extra :]
    half = weights.shape[0] // 2
    block = grads.shape[0] // groups

    load = pltpu.make_async_copy(weights_hbm, weights, sems.at[0, 0])
    load.start()
    blocks = []
    for r in range(groups):
        rows = pl.ds(r * block, block)
        parts = []
        for j in range(count):
            first = sum(widths[:j])
            for k, source in enumerate((dk_hbm[j], dv_hbm[j])):
                target = grads.at[rows, pl.ds(k * half + first, widths[j])]
                parts.append(pltpu.make_async_copy(source.at[rows, :], target, sems.at[1 + r, 2 * j + k]))
        blocks.append(parts)
    for parts in blocks:
        for copy in parts:
            copy.start()
    load.wait()
    for r in range(groups):
        for copy in blocks[r]:
            copy.wait()
        term = jnp.dot(grads[pl.ds(r * block, block), :], weights[...], preferred_element_type=jnp.float32)
        to = pl.ds((r // 2) * block, block)
        (send_ref if r % 2 else keep_ref)[to, :] = term.astype(jnp.bfloat16)


def run_state(groups, dk, dv, weights, after):
    total = dk[0].shape[0]
    enc = weights.shape[1]
    widths = [x.shape[1] for x in dk]
    vmem = pl.BlockSpec(memory_space=pltpu.VMEM)
    return pl.pallas_call(
        functools.partial(state_kernel, groups, widths, len(after)),
        out_shape=[
            jax.ShapeDtypeStruct((total // 2, enc), jnp.bfloat16),
            jax.ShapeDtypeStruct((total // 2, enc), jnp.bfloat16),
        ],
        in_specs=[hbm_spec()] * (2 * len(dk) + 1) + [any_spec()] * len(after),
        out_specs=[vmem, vmem],
        scratch_shapes=[
            pltpu.VMEM((total, weights.shape[0]), jnp.bfloat16),
            pltpu.VMEM(weights.shape, jnp.bfloat16),
            pltpu.SemaphoreType.DMA((groups + 1, 2 * len(dk))),
        ],
        compiler_params=pltpu.CompilerParams(vmem_limit_bytes=VMEM_GRANT),
        cost_estimate=pl.CostEstimate(
            flops=2 * total * enc * weights.shape[0], bytes_accessed=8 * total * enc, transcendentals=0
        ),
        name="state_terms",
    )(*in_hbm([*dk, *dv, weights]), *after)


def fold_kernel(rows_ref, returned_ref, *refs):
    out_hbm, out_ref, sem = refs[-3:]
    out_ref[...] = jnp.zeros_like(out_ref)
    count = out_ref.shape[0]
    for s in range(returned_ref.shape[0]):
        row = rows_ref[s]

        @pl.when(row < count)
        def _():
            out_ref[row] += returned_ref[s].astype(jnp.float32)

    copy = pltpu.make_async_copy(out_ref, out_hbm, sem)
    copy.start()
    copy.wait()


def halve_kernel(choice_ref, keep_ref, recv_ref, *refs):
    stay_ref, send_ref = refs[-2:]
    total = keep_ref[...] + recv_ref[...].astype(jnp.float32)
    half = stay_ref.shape[0]
    upper = choice_ref[0] == 1
    stay_ref[...] = jnp.where(upper, total[half:], total[:half])
    send_ref[...] = jnp.where(upper, total[:half], total[half:]).astype(jnp.bfloat16)


def split_kernel(keep_ref, recv_ref, *refs):
    stay_ref, send_ref = refs[-2:]
    half = stay_ref.shape[0]
    total = keep_ref[...].astype(jnp.float32) + recv_ref[...].astype(jnp.float32)
    stay_ref[...] = total[:half]
    send_ref[...] = total[half:].astype(jnp.bfloat16)


def add_kernel(keep_ref, recv_ref, *refs):
    total = keep_ref[...].astype(jnp.float32) + recv_ref[...].astype(jnp.float32)
    refs[-1][...] = total.astype(refs[-1].dtype)


def join_kernel(choice_ref, own_ref, recv_ref, *refs):
    out_ref = refs[-1]
    upper = choice_ref[0] == 1
    own, recv = own_ref[...], recv_ref[...]
    rows = own.shape[0]
    if rows % 16:
        own, recv = own.astype(jnp.float32), recv.astype(jnp.float32)
        out = jnp.concatenate([jnp.where(upper, recv, own), jnp.where(upper, own, recv)], axis=0)
        out_ref[...] = out.astype(out_ref.dtype)
    else:
        out_ref[:rows] = jnp.where(upper, recv, own)
        out_ref[rows:] = jnp.where(upper, own, recv)


def place_kernel(start, choice_ref, own_ref, recv_ref, *refs):
    key_hbm, value_hbm, token_ref, key_ref, value_ref, sems = refs[-6:]
    token_ref[...] = jnp.zeros_like(token_ref)
    swapped = choice_ref[0] == 1
    own, recv = own_ref[...].astype(jnp.float32), recv_ref[...].astype(jnp.float32)
    columns = pl.ds(start, own.shape[1])
    key_ref[...] = jnp.where(swapped, recv, own)
    key_out = pltpu.make_async_copy(key_ref, key_hbm.at[:, columns], sems.at[0])
    key_out.start()
    value_ref[...] = jnp.where(swapped, own, recv)
    value_out = pltpu.make_async_copy(value_ref, value_hbm.at[:, columns], sems.at[1])
    value_out.start()
    key_out.wait()
    value_out.wait()


def small(kernel, name, scalars, arrays, outs, after, alias_in=(), out_specs=None, scratch=()):
    vmem = pl.BlockSpec(memory_space=pltpu.VMEM)
    extra = list(alias_in) + list(after)
    first = len(scalars) + len(arrays)
    return pl.pallas_call(
        kernel,
        out_shape=outs,
        in_specs=[pl.BlockSpec(memory_space=pltpu.SMEM)] * len(scalars)
        + [vmem] * len(arrays)
        + [hbm_spec()] * len(alias_in)
        + [any_spec()] * len(after),
        out_specs=out_specs or [vmem] * len(outs),
        scratch_shapes=list(scratch),
        input_output_aliases={first + i: i for i in range(len(alias_in))},
        compiler_params=pltpu.CompilerParams(vmem_limit_bytes=SMALL_GRANT),
        cost_estimate=CHEAP,
        name=name,
    )(*scalars, *arrays, *extra)


class Sum:
    def __init__(self, order, choices, start, enc, width):
        self.choices, self.start, self.enc, self.width = choices, start, enc, width
        self.count = len(order)
        self.steps = list(order) + list(reversed(order))
        self.at = 0

    def begin(self, keep, send):
        self.keep = keep
        self.moving = swap(send, "dp", self.steps[0])

    def load(self, step):
        return self.enc >> (step if step < self.count else 2 * self.count - 1 - step)

    def advance(self, after, outs):
        count, at = self.count, self.at
        self.at += 1
        rows = self.load(at)
        shape = lambda rows, dtype: jax.ShapeDtypeStruct((rows, self.width), dtype)
        if at < count - 1:
            choice = self.choices[self.steps[at + 1]]
            self.keep, send = small(
                halve_kernel, "halve", [choice], [self.keep, self.moving],
                [shape(rows // 2, jnp.float32), shape(rows // 2, jnp.bfloat16)], after,
            )
        elif at == count - 1:
            (send,) = small(add_kernel, "add", [], [self.keep, self.moving], [shape(rows, jnp.bfloat16)], after)
        elif at < 2 * count - 1:
            choice = self.choices[self.steps[at]]
            (send,) = small(
                join_kernel, "join", [choice], [self.own, self.moving], [shape(2 * rows, jnp.bfloat16)], after
            )
        else:
            choice = self.choices[self.steps[at]]
            full = pltpu.HBM(self.full, jnp.float32)
            block = pltpu.VMEM((self.enc, self.width), jnp.float32)
            token = jax.ShapeDtypeStruct((8, 128), jnp.float32)
            *outs, done = small(
                functools.partial(place_kernel, self.start), "place", [choice], [self.own, self.moving],
                [full, full, token], after, alias_in=outs,
                out_specs=[hbm_spec()] * 2 + [pl.BlockSpec(memory_space=pltpu.VMEM)],
                scratch=[block, block, pltpu.SemaphoreType.DMA((2,))],
            )
            return done, outs
        self.own = send
        self.moving = swap(send, "dp", self.steps[at + 1])
        return send, outs


def wavefront(chunks, steps, rest):
    order = [f"heads{j}" for j in range(chunks)] + ["sum0", "state"] + ["sum1"] * (chunks > 1)
    done = [1, 1][:chunks] + [0] * (chunks - 2)
    rest_done, period = 0, 1
    while min(done) < steps or rest_done < rest:
        for j in range(min(period + 1, chunks)):
            if done[j] < steps and (period, j) != (1, 1):
                order.append(f"sum{j}")
                done[j] += 1
        if period > 2 and rest_done < rest and (rest_done < rest - 2 or min(done) >= steps - 1):
            order.append("rest")
            rest_done += 1
        period += 1
    return order


def body(queries, states, key_weight, value_weight, nbr_shard, nbr_row, out_grad):
    shards = lax.axis_size("dp")
    groups = lax.axis_size("mp")
    dp_bits, mp_bits = bits_of(shards), bits_of(groups)
    dp_index = lax.axis_index("dp")
    spans, neighbours = nbr_shard.shape
    pair_count = spans * neighbours
    tokens, local_width = queries.shape
    stored, slab_len, enc_width = states.shape
    head_dim = D // H
    capacity = max(2, (pair_count + shards - 1) // shards)
    slot_count = shards * capacity

    owners = nbr_shard.reshape(pair_count)
    row_index = nbr_row.reshape(pair_count)
    pair_ids = jnp.arange(pair_count, dtype=jnp.int32)
    before = (owners[:, None] == owners[None, :]) & (pair_ids[None, :] < pair_ids[:, None])
    slot_index = owners * capacity + jnp.sum(before.astype(jnp.int32), axis=1)
    matched = slot_index[:, None] == jnp.arange(slot_count, dtype=jnp.int32)[None, :]
    asked = stored + jnp.sum(jnp.where(matched, row_index[:, None] - stored, 0), axis=0)
    slot_pair = jnp.sum(jnp.where(matched, pair_ids[:, None], 0), axis=0)
    incoming = lax.all_to_all(
        asked.reshape(shards, capacity), "dp", split_axis=0, concat_axis=0, tiled=True
    ).reshape(slot_count)
    slab_rows = jnp.take(states, jnp.minimum(incoming, stored - 1), axis=0, mode="clip")
    sent_back = lax.all_to_all(
        slab_rows.reshape(shards, capacity, slab_len, enc_width), "dp", split_axis=0, concat_axis=0, tiled=True
    ).reshape(slot_count, slab_len, enc_width)
    picked = jnp.take(sent_back, slot_index, axis=0, mode="clip").reshape(pair_count * slab_len, enc_width)

    turned_weights = run_turn(key_weight, value_weight)
    blocks = {0: picked}
    parts = []
    for bit in reversed(range(mp_bits)):
        across = {r | (1 << bit): swap(blocks[r], "mp", bit) for r in blocks}
        if bit == mp_bits - 1 and groups > 2:
            near = [picked, swap(picked, "mp", 0)]
            parts.append(run_project(near, key_weight, value_weight, [turned_weights]))
            across, parts[0] = lax.optimization_barrier((across, parts[0]))
        blocks.update(across)
    if groups > 2:
        blocks[1] = near[1]
    rest = [blocks[r] for r in range(2 * len(parts), groups)]
    cuts = [rest[: len(rest) // 2], rest[len(rest) // 2 :]] if groups == 4 else [rest]
    parts += [run_project(cut, key_weight, value_weight, [turned_weights]) for cut in cuts]

    heads = local_width // head_dim
    counts = [min(2, heads - first) for first in range(0, heads, 2)]
    bits = list(range(dp_bits))
    choices = [((dp_index >> bit) & 1).astype(jnp.int32).reshape(1) for bit in bits]
    sums = []
    for j, count in enumerate(counts):
        sums.append(Sum(bits, choices, sum(counts[:j]) * head_dim, enc_width, count * head_dim))
        sums[j].full = key_weight.shape

    after, chain, outs, dk, dv = [], [], [], [], []
    rest_bit, pending = 0, None
    for name in wavefront(len(sums), 2 * dp_bits, mp_bits + 1):
        kind = name.rstrip("0123456789")
        number = int(name[len(kind) :] or 0)
        if kind == "heads":
            part = sums[number]
            chain, dk_part, dv_part, (keep, send) = run_heads(
                part.start, part.width, choices[part.steps[0]], parts, groups, queries, out_grad,
                chain, after, spans, head_dim,
            )
            dk.append(dk_part)
            dv.append(dv_part)
            part.begin(keep, send)
            after = [send]
        elif kind == "sum":
            done, outs = sums[number].advance(after, outs)
            after = [done]
            if pending is not None:
                pending, _ = lax.optimization_barrier((pending, done))
                moving, pending = swap(pending, "mp", 0), None
        elif kind == "state":
            keep, send = run_state(groups, dk, dv, turned_weights, after)
            pending, after = send, [send]
        elif rest_bit < mp_bits - 1:
            half = keep.shape[0] // 2
            keep, send = small(
                split_kernel, "split", [], [keep, moving],
                [jax.ShapeDtypeStruct((half, enc_width), t) for t in (jnp.float32, jnp.bfloat16)], after,
            )
            moving = swap(send, "mp", mp_bits - 1 - rest_bit)
            after = [send]
            rest_bit += 1
        elif rest_bit == mp_bits - 1:
            (pair_grad,) = small(
                add_kernel, "add", [], [keep, moving], [jax.ShapeDtypeStruct(keep.shape, jnp.bfloat16)], after
            )
            after = [pair_grad]
            outgoing = jnp.take(
                pair_grad.reshape(pair_count, slab_len, enc_width), slot_pair, axis=0, mode="clip"
            ).reshape(shards, capacity, slab_len, enc_width)
            returned = lax.all_to_all(outgoing, "dp", split_axis=0, concat_axis=0, tiled=True)
            rest_bit += 1
        else:
            (state_total,) = small(
                fold_kernel, "fold", [incoming], [returned.reshape(slot_count, slab_len, enc_width)],
                [pltpu.HBM(states.shape, jnp.float32)], after, out_specs=[hbm_spec()],
                scratch=[pltpu.VMEM(states.shape, jnp.float32), pltpu.SemaphoreType.DMA],
            )
    return (chain[0], chain[1], state_total, outs[0], outs[1])


def solution(mesh):
    placed = (
        P("dp", "mp"),
        P("dp", "mp", None),
        P(None, "mp"),
        P(None, "mp"),
        P("dp", None),
        P("dp", None),
        P("dp", "mp"),
    )
    return jax.shard_map(
        body,
        mesh=mesh,
        in_specs=placed,
        out_specs=(P("dp", "mp"), P("dp", "mp"), P("dp", "mp", None), P(None, "mp"), P(None, "mp")),
        check_vma=False,
    )
```

```python
import functools

import jax
import jax.numpy as jnp
from jax import lax
from jax.experimental import pallas as pl
from jax.experimental.pallas import tpu as pltpu
from jax.sharding import PartitionSpec as P

D = 4096
H = 32
VMEM_GRANT = 28 * 1024 * 1024
SMALL_GRANT = 12 * 1024 * 1024
CHEAP = pl.CostEstimate(flops=1, bytes_accessed=1, transcendentals=0)


def bits_of(count):
    return count.bit_length() - 1


def swap(value, axis, bit):
    count = lax.axis_size(axis)
    return lax.ppermute(value, axis, [(i, i ^ (1 << bit)) for i in range(count)])


def any_spec():
    return pl.BlockSpec(memory_space=pl.ANY)


def in_hbm(arrays):
    return [pltpu.with_memory_space_constraint(x, pltpu.HBM) for x in arrays]


def hbm_spec():
    return pl.BlockSpec(memory_space=pltpu.HBM)


def head_kernel(groups, spans, head_dim, start, extra, *refs):
    flag_ref = refs[0]
    slabs = refs[1 : 1 + groups]
    wk_hbm, wv_hbm, q_hbm, g_hbm = refs[1 + groups : 5 + groups]
    att_hbm, dq_hbm, dk_hbm, dv_hbm, keep_ref, send_ref = refs[5 + groups + extra : 11 + groups + extra]
    rows, wk, wv, q_ref, g_ref, keys, values, att_ref, dq_ref, dk_ref, dv_ref, grads, sems = refs[11 + groups + extra :]
    tokens, width = q_ref.shape
    span_len = tokens // spans
    block = rows.shape[0] // groups
    part = block // spans
    scale = 1.0 / head_dim**0.5
    columns = pl.ds(start, width)

    def begin(source, target, sem):
        copy = pltpu.make_async_copy(source, target, sems.at[sem])
        copy.start()
        return copy

    weights_in = [begin(wk_hbm.at[:, columns], wk, groups), begin(wv_hbm.at[:, columns], wv, groups + 1)]
    rows_in = [begin(slabs[r], rows.at[pl.ds(r * block, block)], r) for r in range(groups)]
    tokens_in = [begin(q_hbm.at[:, columns], q_ref, groups + 2), begin(g_hbm.at[:, columns], g_ref, groups + 3)]
    for copy in weights_in:
        copy.wait()
    for r in range(groups):
        rows_in[r].wait()
        at = pl.ds(r * block, block)
        keys[at, :] = jnp.dot(rows[at, :], wk[...], preferred_element_type=jnp.float32).astype(jnp.bfloat16)
        values[at, :] = jnp.dot(rows[at, :], wv[...], preferred_element_type=jnp.float32).astype(jnp.bfloat16)
    for copy in tokens_in:
        copy.wait()

    def spread(x):
        heads = x.shape[1] // head_dim
        lane_head = lax.broadcasted_iota(jnp.int32, x.shape, 1) // head_dim
        zero = jnp.zeros_like(x)
        return jnp.concatenate([jnp.where(lane_head == h, x, zero) for h in range(heads)], axis=0)

    def collect(x):
        out = x[0:span_len]
        lane_head = lax.broadcasted_iota(jnp.int32, out.shape, 1) // head_dim
        for h in range(1, x.shape[1] // head_dim):
            out = jnp.where(lane_head == h, x[h * span_len : (h + 1) * span_len], out)
        return out

    def span_rows(ref, c, cols):
        return jnp.concatenate([ref[pl.ds(r * block + c * part, part), cols] for r in range(groups)], axis=0)

    contract_last = (((1,), (1,)), ((), ()))
    contract_first = (((0,), (0,)), ((), ()))
    at = [pl.ds(c * span_len, span_len) for c in range(spans)]
    swapped = flag_ref[0] == 1
    pair = 2 * head_dim
    for first in range(0, width, pair):
        cols = slice(first, min(first + pair, width))
        send_cols = slice(width + cols.start, width + cols.stop)
        every = range(spans)
        scores = [
            lax.dot_general(
                span_rows(keys, c, cols), spread(q_ref[at[c], cols]), contract_last,
                preferred_element_type=jnp.float32,
            )
            * scale
            for c in every
        ]
        prob_grad = [
            lax.dot_general(
                span_rows(values, c, cols), spread(g_ref[at[c], cols]), contract_last,
                preferred_element_type=jnp.float32,
            )
            for c in every
        ]
        weights = [jnp.exp(x - jnp.max(x, axis=0, keepdims=True)) for x in scores]
        probs = [x * (1.0 / jnp.sum(x, axis=0, keepdims=True)) for x in weights]
        low = [x.astype(jnp.bfloat16) for x in probs]
        row_dot = [jnp.sum(p * d, axis=0, keepdims=True) for p, d in zip(probs, prob_grad)]
        score_grad = [(scale * p * (d - t)).astype(jnp.bfloat16) for p, d, t in zip(probs, prob_grad, row_dot)]
        for c in every:
            dk = jnp.dot(score_grad[c], spread(q_ref[at[c], cols]), preferred_element_type=jnp.float32)
            dv = jnp.dot(low[c], spread(g_ref[at[c], cols]), preferred_element_type=jnp.float32)
            dk, dv = dk.astype(jnp.bfloat16), dv.astype(jnp.bfloat16)
            for r in range(groups):
                to = pl.ds(r * block + c * part, part)
                piece = slice(r * part, (r + 1) * part)
                dk_ref[to, cols] = dk[piece]
                dv_ref[to, cols] = dv[piece]
                grads[to, cols] = jnp.where(swapped, dv[piece], dk[piece])
                grads[to, send_cols] = jnp.where(swapped, dk[piece], dv[piece])
        for c in every:
            att = lax.dot_general(
                low[c], span_rows(values, c, cols), contract_first, preferred_element_type=jnp.float32
            )
            att_ref[at[c], cols] = collect(att).astype(jnp.bfloat16)
            dq = lax.dot_general(
                score_grad[c], span_rows(keys, c, cols), contract_first, preferred_element_type=jnp.float32
            )
            dq_ref[at[c], cols] = collect(dq).astype(jnp.bfloat16)
    results = [
        begin(att_ref, att_hbm.at[:, columns], 0),
        begin(dq_ref, dq_hbm.at[:, columns], 1),
        begin(dk_ref, dk_hbm, 2),
        begin(dv_ref, dv_hbm, 3),
    ]
    tile = 128
    for first in range(0, rows.shape[1], tile):
        to = slice(first, first + tile)
        both = lax.dot_general(rows[:, to], grads[...], contract_first, preferred_element_type=jnp.float32)
        keep_ref[to, :] = both[:, :width]
        send_ref[to, :] = both[:, width:].astype(jnp.bfloat16)
    for copy in results:
        copy.wait()


def run_heads(start, chunk, flag, slabs, key_weight, value_weight, queries, out_grad, chain, after, spans, head_dim):
    groups = len(slabs)
    tokens, local_width = queries.shape
    block, enc = slabs[0].shape
    total = groups * block
    bf = jnp.bfloat16
    extra = list(chain) + list(after)
    outs = pl.pallas_call(
        functools.partial(head_kernel, groups, spans, head_dim, start, len(extra)),
        out_shape=[
            pltpu.HBM((tokens, local_width), bf),
            pltpu.HBM((tokens, local_width), bf),
            pltpu.HBM((total, chunk), bf),
            pltpu.HBM((total, chunk), bf),
            jax.ShapeDtypeStruct((enc, chunk), jnp.float32),
            jax.ShapeDtypeStruct((enc, chunk), bf),
        ],
        in_specs=[pl.BlockSpec(memory_space=pltpu.SMEM)]
        + [any_spec()] * groups
        + [hbm_spec()] * (4 + len(chain))
        + [any_spec()] * len(after),
        out_specs=[hbm_spec()] * 4 + [pl.BlockSpec(memory_space=pltpu.VMEM)] * 2,
        scratch_shapes=[
            pltpu.VMEM((total, enc), bf),
            pltpu.VMEM((enc, chunk), bf),
            pltpu.VMEM((enc, chunk), bf),
            pltpu.VMEM((tokens, chunk), bf),
            pltpu.VMEM((tokens, chunk), bf),
            pltpu.VMEM((total, chunk), bf),
            pltpu.VMEM((total, chunk), bf),
            pltpu.VMEM((tokens, chunk), bf),
            pltpu.VMEM((tokens, chunk), bf),
            pltpu.VMEM((total, chunk), bf),
            pltpu.VMEM((total, chunk), bf),
            pltpu.VMEM((total, 2 * chunk), bf),
            pltpu.SemaphoreType.DMA((groups + 4,)),
        ],
        input_output_aliases={5 + groups + i: i for i in range(len(chain))},
        compiler_params=pltpu.CompilerParams(vmem_limit_bytes=VMEM_GRANT),
        cost_estimate=pl.CostEstimate(
            flops=2 * total * enc * chunk * 8, bytes_accessed=4 * total * enc, transcendentals=total * tokens
        ),
        name="heads",
    )(flag, *slabs, *in_hbm([key_weight, value_weight, queries, out_grad, *chain]), *after)
    return outs[:2], outs[2], outs[3], outs[4:]


def state_kernel(groups, widths, extra, *refs):
    count = len(widths)
    dk_hbm, dv_hbm = refs[:count], refs[count : 2 * count]
    wk_hbm, wv_hbm = refs[2 * count : 2 * count + 2]
    keep_ref, send_ref, grads, weights, sems = refs[2 * count + 2 + extra :]
    half = weights.shape[1] // 2
    block = grads.shape[0] // groups

    copies = [
        pltpu.make_async_copy(wk_hbm, weights.at[:, pl.ds(0, half)], sems.at[0, 0]),
        pltpu.make_async_copy(wv_hbm, weights.at[:, pl.ds(half, half)], sems.at[0, 1]),
    ]
    blocks = []
    for r in range(groups):
        rows = pl.ds(r * block, block)
        parts = []
        for j in range(count):
            first = sum(widths[:j])
            for k, source in enumerate((dk_hbm[j], dv_hbm[j])):
                target = grads.at[rows, pl.ds(k * half + first, widths[j])]
                parts.append(pltpu.make_async_copy(source.at[rows, :], target, sems.at[1 + r, 2 * j + k]))
        blocks.append(parts)
    for copy in copies:
        copy.start()
    for parts in blocks:
        for copy in parts:
            copy.start()
    for copy in copies:
        copy.wait()
    for r in range(groups):
        for copy in blocks[r]:
            copy.wait()
        to = pl.ds((r // 2) * block, block)
        for first in range(0, weights.shape[0], 256):
            cols = slice(first, min(first + 256, weights.shape[0]))
            term = lax.dot_general(
                grads[pl.ds(r * block, block), :], weights[cols, :], (((1,), (1,)), ((), ())),
                preferred_element_type=jnp.float32,
            )
            (send_ref if r % 2 else keep_ref)[to, cols] = term.astype(jnp.bfloat16)


def run_state(groups, dk, dv, key_weight, value_weight, after):
    total = dk[0].shape[0]
    enc, local_width = key_weight.shape
    widths = [x.shape[1] for x in dk]
    vmem = pl.BlockSpec(memory_space=pltpu.VMEM)
    return pl.pallas_call(
        functools.partial(state_kernel, groups, widths, len(after)),
        out_shape=[
            jax.ShapeDtypeStruct((total // 2, enc), jnp.bfloat16),
            jax.ShapeDtypeStruct((total // 2, enc), jnp.bfloat16),
        ],
        in_specs=[hbm_spec()] * (2 * len(dk) + 2) + [any_spec()] * len(after),
        out_specs=[vmem, vmem],
        scratch_shapes=[
            pltpu.VMEM((total, 2 * local_width), jnp.bfloat16),
            pltpu.VMEM((enc, 2 * local_width), jnp.bfloat16),
            pltpu.SemaphoreType.DMA((groups + 1, max(2, 2 * len(dk)))),
        ],
        compiler_params=pltpu.CompilerParams(vmem_limit_bytes=VMEM_GRANT),
        cost_estimate=pl.CostEstimate(
            flops=8 * total * enc * local_width, bytes_accessed=8 * total * enc, transcendentals=0
        ),
        name="state_terms",
    )(*in_hbm([*dk, *dv, key_weight, value_weight]), *after)


def fold_kernel(rows_ref, returned_ref, *refs):
    out_hbm, out_ref, sem = refs[-3:]
    out_ref[...] = jnp.zeros_like(out_ref)
    count = out_ref.shape[0]
    for s in range(returned_ref.shape[0]):
        row = rows_ref[s]

        @pl.when(row < count)
        def _():
            out_ref[row] += returned_ref[s].astype(jnp.float32)

    copy = pltpu.make_async_copy(out_ref, out_hbm, sem)
    copy.start()
    copy.wait()


def halve_kernel(choice_ref, keep_ref, recv_ref, *refs):
    stay_ref, send_ref = refs[-2:]
    total = keep_ref[...] + recv_ref[...].astype(jnp.float32)
    half = stay_ref.shape[0]
    upper = choice_ref[0] == 1
    stay_ref[...] = jnp.where(upper, total[half:], total[:half])
    send_ref[...] = jnp.where(upper, total[:half], total[half:]).astype(jnp.bfloat16)


def split_kernel(keep_ref, recv_ref, *refs):
    stay_ref, send_ref = refs[-2:]
    half = stay_ref.shape[0]
    total = keep_ref[...].astype(jnp.float32) + recv_ref[...].astype(jnp.float32)
    stay_ref[...] = total[:half]
    send_ref[...] = total[half:].astype(jnp.bfloat16)


def add_kernel(keep_ref, recv_ref, *refs):
    total = keep_ref[...].astype(jnp.float32) + recv_ref[...].astype(jnp.float32)
    refs[-1][...] = total.astype(refs[-1].dtype)


def join_kernel(choice_ref, own_ref, recv_ref, *refs):
    out_ref = refs[-1]
    upper = choice_ref[0] == 1
    own, recv = own_ref[...], recv_ref[...]
    rows = own.shape[0]
    if rows % 16:
        own, recv = own.astype(jnp.float32), recv.astype(jnp.float32)
        out = jnp.concatenate([jnp.where(upper, recv, own), jnp.where(upper, own, recv)], axis=0)
        out_ref[...] = out.astype(out_ref.dtype)
    else:
        out_ref[:rows] = jnp.where(upper, recv, own)
        out_ref[rows:] = jnp.where(upper, own, recv)


def place_kernel(start, choice_ref, own_ref, recv_ref, *refs):
    key_hbm, value_hbm, token_ref, key_ref, value_ref, sems = refs[-6:]
    token_ref[...] = jnp.zeros_like(token_ref)
    swapped = choice_ref[0] == 1
    own, recv = own_ref[...].astype(jnp.float32), recv_ref[...].astype(jnp.float32)
    columns = pl.ds(start, own.shape[1])
    key_ref[...] = jnp.where(swapped, recv, own)
    key_out = pltpu.make_async_copy(key_ref, key_hbm.at[:, columns], sems.at[0])
    key_out.start()
    value_ref[...] = jnp.where(swapped, own, recv)
    value_out = pltpu.make_async_copy(value_ref, value_hbm.at[:, columns], sems.at[1])
    value_out.start()
    key_out.wait()
    value_out.wait()


def small(kernel, name, scalars, arrays, outs, after, alias_in=(), out_specs=None, scratch=()):
    vmem = pl.BlockSpec(memory_space=pltpu.VMEM)
    extra = list(alias_in) + list(after)
    first = len(scalars) + len(arrays)
    return pl.pallas_call(
        kernel,
        out_shape=outs,
        in_specs=[pl.BlockSpec(memory_space=pltpu.SMEM)] * len(scalars)
        + [vmem] * len(arrays)
        + [hbm_spec()] * len(alias_in)
        + [any_spec()] * len(after),
        out_specs=out_specs or [vmem] * len(outs),
        scratch_shapes=list(scratch),
        input_output_aliases={first + i: i for i in range(len(alias_in))},
        compiler_params=pltpu.CompilerParams(vmem_limit_bytes=SMALL_GRANT),
        cost_estimate=CHEAP,
        name=name,
    )(*scalars, *arrays, *extra)


class Sum:
    def __init__(self, order, choices, start, enc, width):
        self.choices, self.start, self.enc, self.width = choices, start, enc, width
        self.count = len(order)
        self.steps = list(order) + list(reversed(order))
        self.at = 0

    def begin(self, keep, send):
        self.keep = keep
        self.moving = swap(send, "dp", self.steps[0])

    def load(self, step):
        return self.enc >> (step if step < self.count else 2 * self.count - 1 - step)

    def advance(self, after, outs):
        count, at = self.count, self.at
        self.at += 1
        rows = self.load(at)
        shape = lambda rows, dtype: jax.ShapeDtypeStruct((rows, self.width), dtype)
        if at < count - 1:
            choice = self.choices[self.steps[at + 1]]
            self.keep, send = small(
                halve_kernel, "halve", [choice], [self.keep, self.moving],
                [shape(rows // 2, jnp.float32), shape(rows // 2, jnp.bfloat16)], after,
            )
        elif at == count - 1:
            (send,) = small(add_kernel, "add", [], [self.keep, self.moving], [shape(rows, jnp.bfloat16)], after)
        elif at < 2 * count - 1:
            choice = self.choices[self.steps[at]]
            (send,) = small(
                join_kernel, "join", [choice], [self.own, self.moving], [shape(2 * rows, jnp.bfloat16)], after
            )
        else:
            choice = self.choices[self.steps[at]]
            full = pltpu.HBM(self.full, jnp.float32)
            block = pltpu.VMEM((self.enc, self.width), jnp.float32)
            token = jax.ShapeDtypeStruct((8, 128), jnp.float32)
            *outs, done = small(
                functools.partial(place_kernel, self.start), "place", [choice], [self.own, self.moving],
                [full, full, token], after, alias_in=outs,
                out_specs=[hbm_spec()] * 2 + [pl.BlockSpec(memory_space=pltpu.VMEM)],
                scratch=[block, block, pltpu.SemaphoreType.DMA((2,))],
            )
            return done, outs
        self.own = send
        self.moving = swap(send, "dp", self.steps[at + 1])
        return send, outs


def plan(sums, rest):
    rate, event, start, lag = 84e3, 1.0, 1.5, 1.5
    chains = {}
    for j, s in enumerate(sums):
        chains[f"sum{j}"] = []
        for k, bit in enumerate(s.steps):
            time = 4 * s.load(k) * s.width / rate
            chains[f"sum{j}"].append({"y": time} if bit == 0 else {"ends": time, "middle": time * (1 + (bit > 1))})
    chains["rest"] = [{"core": 3.0}] + [{"x": 17.0}] * (rest - 2) + [{"y": 9.0, "ends": 14.0, "middle": 18.0}]
    last = f"sum{len(sums) - 1}"
    heavy = [(f"heads{j}", 1.0 + 2.75 * s.width / 128, f"sum{j}") for j, s in enumerate(sums)]
    heavy.append(("state", 9.5, "rest"))
    left = {name: len(steps) for name, steps in chains.items()}
    free, waiting, order, now = {}, {}, [], 0.0

    def send(name):
        nonlocal now
        now += start
        loads = chains[name][-left[name]]
        begin = max([now] + [free.get(link, 0.0) for link in loads])
        for link, time in loads.items():
            free[link] = max(free.get(link, 0.0), now) + time
        waiting[name] = max([begin + max(loads.values())] + [free[link] for link in loads]) + lag

    def step(name):
        nonlocal now
        now = max(now, waiting.pop(name)) + event
        order.append(name)
        left[name] -= 1
        if left[name]:
            send(name)

    for period, (name, time, begun) in enumerate(heavy):
        now += time
        order.append(name)
        if begun != "rest":
            send(begun)
        for name in [f"sum{j}" for j in range(period)] if begun != "rest" else sorted(waiting, key=waiting.get):
            step(name)
    send("rest")
    while waiting:
        open_now = [name for name in waiting if not (name == "rest" and left[name] == 2 and left[last] > 1)]
        ready = [name for name in open_now if waiting[name] <= now]
        moving = [name for name in ready if left[name] > 1]
        if moving:
            step(min(moving, key=lambda name: (-left[name], waiting[name])))
        elif ready:
            step(ready[0])
        else:
            step(min(open_now, key=lambda name: waiting[name]))
    return order


def body(queries, states, key_weight, value_weight, nbr_shard, nbr_row, out_grad):
    shards = lax.axis_size("dp")
    groups = lax.axis_size("mp")
    dp_bits, mp_bits = bits_of(shards), bits_of(groups)
    dp_index = lax.axis_index("dp")
    spans, neighbours = nbr_shard.shape
    pair_count = spans * neighbours
    tokens, local_width = queries.shape
    stored, slab_len, enc_width = states.shape
    head_dim = D // H
    capacity = max(2, (pair_count + shards - 1) // shards)
    slot_count = shards * capacity

    owners = nbr_shard.reshape(pair_count)
    row_index = nbr_row.reshape(pair_count)
    pair_ids = jnp.arange(pair_count, dtype=jnp.int32)
    before = (owners[:, None] == owners[None, :]) & (pair_ids[None, :] < pair_ids[:, None])
    slot_index = owners * capacity + jnp.sum(before.astype(jnp.int32), axis=1)
    matched = slot_index[:, None] == jnp.arange(slot_count, dtype=jnp.int32)[None, :]
    asked = stored + jnp.sum(jnp.where(matched, row_index[:, None] - stored, 0), axis=0)
    slot_pair = jnp.sum(jnp.where(matched, pair_ids[:, None], 0), axis=0)
    incoming = lax.all_to_all(
        asked.reshape(shards, capacity), "dp", split_axis=0, concat_axis=0, tiled=True
    ).reshape(slot_count)
    slab_rows = jnp.take(states, jnp.minimum(incoming, stored - 1), axis=0, mode="clip")
    sent_back = lax.all_to_all(
        slab_rows.reshape(shards, capacity, slab_len, enc_width), "dp", split_axis=0, concat_axis=0, tiled=True
    ).reshape(slot_count, slab_len, enc_width)
    picked = jnp.take(sent_back, slot_index, axis=0, mode="clip").reshape(pair_count * slab_len, enc_width)

    blocks = {0: picked}
    for bit in reversed(range(mp_bits)):
        for r in list(blocks):
            blocks[r | (1 << bit)] = swap(blocks[r], "mp", bit)
    slabs = [blocks[r] for r in range(groups)]

    heads = local_width // head_dim
    counts = [min(2, heads - first) for first in range(0, heads, 2)]
    bits = list(range(dp_bits))
    choices = [((dp_index >> bit) & 1).astype(jnp.int32).reshape(1) for bit in bits]
    sums = []
    for j, count in enumerate(counts):
        sums.append(Sum(bits, choices, sum(counts[:j]) * head_dim, enc_width, count * head_dim))
        sums[j].full = key_weight.shape

    after, chain, outs, dk, dv = [], [], [], [], []
    rest_bit, pending, held_for = 0, None, 0
    for name in plan(sums, mp_bits + 1):
        kind = name.rstrip("0123456789")
        number = int(name[len(kind) :] or 0)
        if kind == "heads":
            part = sums[number]
            chain, dk_part, dv_part, (keep, send) = run_heads(
                part.start, part.width, choices[0], slabs, key_weight, value_weight, queries, out_grad,
                chain, after, spans, head_dim,
            )
            dk.append(dk_part)
            dv.append(dv_part)
            part.begin(keep, send)
            after = [send]
        elif kind == "sum":
            done, outs = sums[number].advance(after, outs)
            after = [done]
            held_for -= 1
            if pending is not None and not held_for:
                pending, _ = lax.optimization_barrier((pending, done))
                moving, pending = swap(pending, "mp", 0), None
        elif kind == "state":
            keep, send = run_state(groups, dk, dv, key_weight, value_weight, after)
            pending, after, held_for = send, [send], len(sums)
        elif rest_bit < mp_bits - 1:
            half = keep.shape[0] // 2
            keep, send = small(
                split_kernel, "split", [], [keep, moving],
                [jax.ShapeDtypeStruct((half, enc_width), t) for t in (jnp.float32, jnp.bfloat16)], after,
            )
            moving = swap(send, "mp", mp_bits - 1 - rest_bit)
            after = [send]
            rest_bit += 1
        elif rest_bit == mp_bits - 1:
            (pair_grad,) = small(
                add_kernel, "add", [], [keep, moving], [jax.ShapeDtypeStruct(keep.shape, jnp.bfloat16)], after
            )
            after = [pair_grad]
            outgoing = jnp.take(
                pair_grad.reshape(pair_count, slab_len, enc_width), slot_pair, axis=0, mode="clip"
            ).reshape(shards, capacity, slab_len, enc_width)
            returned = lax.all_to_all(outgoing, "dp", split_axis=0, concat_axis=0, tiled=True)
            rest_bit += 1
        else:
            (state_total,) = small(
                fold_kernel, "fold", [incoming], [returned.reshape(slot_count, slab_len, enc_width)],
                [pltpu.HBM(states.shape, jnp.float32)], after, out_specs=[hbm_spec()],
                scratch=[pltpu.VMEM(states.shape, jnp.float32), pltpu.SemaphoreType.DMA],
            )
    return (chain[0], chain[1], state_total, outs[0], outs[1])


def solution(mesh):
    placed = (
        P("dp", "mp"),
        P("dp", "mp", None),
        P(None, "mp"),
        P(None, "mp"),
        P("dp", None),
        P("dp", None),
        P("dp", "mp"),
    )
    return jax.shard_map(
        body,
        mesh=mesh,
        in_specs=placed,
        out_specs=(P("dp", "mp"), P("dp", "mp"), P("dp", "mp", None), P(None, "mp"), P(None, "mp")),
        check_vma=False,
    )
```

```python
import functools

import jax
import jax.numpy as jnp
from jax import lax
from jax.experimental import pallas as pl
from jax.experimental.pallas import tpu as pltpu
from jax.sharding import PartitionSpec as P

D = 4096
H = 32
VMEM_GRANT = 28 * 1024 * 1024
SMALL_GRANT = 12 * 1024 * 1024
CHEAP = pl.CostEstimate(flops=1, bytes_accessed=1, transcendentals=0)


def bits_of(count):
    return count.bit_length() - 1


def swap(value, axis, bit):
    count = lax.axis_size(axis)
    return lax.ppermute(value, axis, [(i, i ^ (1 << bit)) for i in range(count)])


def any_spec():
    return pl.BlockSpec(memory_space=pl.ANY)


def in_hbm(arrays):
    return [pltpu.with_memory_space_constraint(x, pltpu.HBM) for x in arrays]


def hbm_spec():
    return pl.BlockSpec(memory_space=pltpu.HBM)


def head_kernel(groups, spans, head_dim, start, extra, *refs):
    flag_ref = refs[0]
    slabs = refs[1 : 1 + groups]
    wk_hbm, wv_hbm, q_hbm, g_hbm = refs[1 + groups : 5 + groups]
    att_hbm, dq_hbm, dk_hbm, dv_hbm, keep_ref, send_ref = refs[5 + groups + extra : 11 + groups + extra]
    rows, wk, wv, q_ref, g_ref, keys, values, att_ref, dq_ref, dk_ref, dv_ref, grads, sems = refs[11 + groups + extra :]
    tokens, width = q_ref.shape
    span_len = tokens // spans
    block = rows.shape[0] // groups
    part = block // spans
    scale = 1.0 / head_dim**0.5
    columns = pl.ds(start, width)

    def begin(source, target, sem):
        copy = pltpu.make_async_copy(source, target, sems.at[sem])
        copy.start()
        return copy

    weights_in = [begin(wk_hbm.at[:, columns], wk, groups), begin(wv_hbm.at[:, columns], wv, groups + 1)]
    rows_in = [begin(slabs[r], rows.at[pl.ds(r * block, block)], r) for r in range(groups)]
    tokens_in = [begin(q_hbm.at[:, columns], q_ref, groups + 2), begin(g_hbm.at[:, columns], g_ref, groups + 3)]
    for copy in weights_in:
        copy.wait()
    for r in range(groups):
        rows_in[r].wait()
        at = pl.ds(r * block, block)
        keys[at, :] = jnp.dot(rows[at, :], wk[...], preferred_element_type=jnp.float32).astype(jnp.bfloat16)
        values[at, :] = jnp.dot(rows[at, :], wv[...], preferred_element_type=jnp.float32).astype(jnp.bfloat16)
    for copy in tokens_in:
        copy.wait()

    def spread(x):
        heads = x.shape[1] // head_dim
        lane_head = lax.broadcasted_iota(jnp.int32, x.shape, 1) // head_dim
        zero = jnp.zeros_like(x)
        return jnp.concatenate([jnp.where(lane_head == h, x, zero) for h in range(heads)], axis=0)

    def collect(x):
        out = x[0:span_len]
        lane_head = lax.broadcasted_iota(jnp.int32, out.shape, 1) // head_dim
        for h in range(1, x.shape[1] // head_dim):
            out = jnp.where(lane_head == h, x[h * span_len : (h + 1) * span_len], out)
        return out

    def span_rows(ref, c, cols):
        return jnp.concatenate([ref[pl.ds(r * block + c * part, part), cols] for r in range(groups)], axis=0)

    contract_last = (((1,), (1,)), ((), ()))
    contract_first = (((0,), (0,)), ((), ()))
    at = [pl.ds(c * span_len, span_len) for c in range(spans)]
    swapped = flag_ref[0] == 1
    pair = 2 * head_dim
    for first in range(0, width, pair):
        cols = slice(first, min(first + pair, width))
        send_cols = slice(width + cols.start, width + cols.stop)
        every = range(spans)
        scores = [
            lax.dot_general(
                span_rows(keys, c, cols), spread(q_ref[at[c], cols]), contract_last,
                preferred_element_type=jnp.float32,
            )
            * scale
            for c in every
        ]
        prob_grad = [
            lax.dot_general(
                span_rows(values, c, cols), spread(g_ref[at[c], cols]), contract_last,
                preferred_element_type=jnp.float32,
            )
            for c in every
        ]
        weights = [jnp.exp(x - jnp.max(x, axis=0, keepdims=True)) for x in scores]
        probs = [x * (1.0 / jnp.sum(x, axis=0, keepdims=True)) for x in weights]
        low = [x.astype(jnp.bfloat16) for x in probs]
        row_dot = [jnp.sum(p * d, axis=0, keepdims=True) for p, d in zip(probs, prob_grad)]
        score_grad = [(scale * p * (d - t)).astype(jnp.bfloat16) for p, d, t in zip(probs, prob_grad, row_dot)]
        for c in every:
            dk = jnp.dot(score_grad[c], spread(q_ref[at[c], cols]), preferred_element_type=jnp.float32)
            dv = jnp.dot(low[c], spread(g_ref[at[c], cols]), preferred_element_type=jnp.float32)
            dk, dv = dk.astype(jnp.bfloat16), dv.astype(jnp.bfloat16)
            for r in range(groups):
                to = pl.ds(r * block + c * part, part)
                piece = slice(r * part, (r + 1) * part)
                dk_ref[to, cols] = dk[piece]
                dv_ref[to, cols] = dv[piece]
                grads[to, cols] = jnp.where(swapped, dv[piece], dk[piece])
                grads[to, send_cols] = jnp.where(swapped, dk[piece], dv[piece])
        for c in every:
            att = lax.dot_general(
                low[c], span_rows(values, c, cols), contract_first, preferred_element_type=jnp.float32
            )
            att_ref[at[c], cols] = collect(att).astype(jnp.bfloat16)
            dq = lax.dot_general(
                score_grad[c], span_rows(keys, c, cols), contract_first, preferred_element_type=jnp.float32
            )
            dq_ref[at[c], cols] = collect(dq).astype(jnp.bfloat16)
    results = [
        begin(att_ref, att_hbm.at[:, columns], 0),
        begin(dq_ref, dq_hbm.at[:, columns], 1),
        begin(dk_ref, dk_hbm, 2),
        begin(dv_ref, dv_hbm, 3),
    ]
    tile = 128
    for first in range(0, rows.shape[1], tile):
        to = slice(first, first + tile)
        both = lax.dot_general(rows[:, to], grads[...], contract_first, preferred_element_type=jnp.float32)
        keep_ref[to, :] = both[:, :width]
        send_ref[to, :] = both[:, width:].astype(jnp.bfloat16)
    for copy in results:
        copy.wait()


def run_heads(start, chunk, flag, slabs, key_weight, value_weight, queries, out_grad, chain, after, spans, head_dim):
    groups = len(slabs)
    tokens, local_width = queries.shape
    block, enc = slabs[0].shape
    total = groups * block
    bf = jnp.bfloat16
    extra = list(chain) + list(after)
    outs = pl.pallas_call(
        functools.partial(head_kernel, groups, spans, head_dim, start, len(extra)),
        out_shape=[
            pltpu.HBM((tokens, local_width), bf),
            pltpu.HBM((tokens, local_width), bf),
            pltpu.HBM((total, chunk), bf),
            pltpu.HBM((total, chunk), bf),
            jax.ShapeDtypeStruct((enc, chunk), jnp.float32),
            jax.ShapeDtypeStruct((enc, chunk), bf),
        ],
        in_specs=[pl.BlockSpec(memory_space=pltpu.SMEM)]
        + [any_spec()] * groups
        + [hbm_spec()] * (4 + len(chain))
        + [any_spec()] * len(after),
        out_specs=[hbm_spec()] * 4 + [pl.BlockSpec(memory_space=pltpu.VMEM)] * 2,
        scratch_shapes=[
            pltpu.VMEM((total, enc), bf),
            pltpu.VMEM((enc, chunk), bf),
            pltpu.VMEM((enc, chunk), bf),
            pltpu.VMEM((tokens, chunk), bf),
            pltpu.VMEM((tokens, chunk), bf),
            pltpu.VMEM((total, chunk), bf),
            pltpu.VMEM((total, chunk), bf),
            pltpu.VMEM((tokens, chunk), bf),
            pltpu.VMEM((tokens, chunk), bf),
            pltpu.VMEM((total, chunk), bf),
            pltpu.VMEM((total, chunk), bf),
            pltpu.VMEM((total, 2 * chunk), bf),
            pltpu.SemaphoreType.DMA((groups + 4,)),
        ],
        input_output_aliases={5 + groups + i: i for i in range(len(chain))},
        compiler_params=pltpu.CompilerParams(vmem_limit_bytes=VMEM_GRANT),
        cost_estimate=pl.CostEstimate(
            flops=2 * total * enc * chunk * 8, bytes_accessed=4 * total * enc, transcendentals=total * tokens
        ),
        name="heads",
    )(flag, *slabs, *in_hbm([key_weight, value_weight, queries, out_grad, *chain]), *after)
    return outs[:2], outs[2], outs[3], outs[4:]


def state_kernel(groups, widths, extra, *refs):
    count = len(widths)
    dk_hbm, dv_hbm = refs[:count], refs[count : 2 * count]
    wk_hbm, wv_hbm = refs[2 * count : 2 * count + 2]
    keep_ref, send_ref, grads, weights, sems = refs[2 * count + 2 + extra :]
    half = weights.shape[1] // 2
    block = grads.shape[0] // groups

    copies = [
        pltpu.make_async_copy(wk_hbm, weights.at[:, pl.ds(0, half)], sems.at[0, 0]),
        pltpu.make_async_copy(wv_hbm, weights.at[:, pl.ds(half, half)], sems.at[0, 1]),
    ]
    blocks = []
    for r in range(groups):
        rows = pl.ds(r * block, block)
        parts = []
        for j in range(count):
            first = sum(widths[:j])
            for k, source in enumerate((dk_hbm[j], dv_hbm[j])):
                target = grads.at[rows, pl.ds(k * half + first, widths[j])]
                parts.append(pltpu.make_async_copy(source.at[rows, :], target, sems.at[1 + r, 2 * j + k]))
        blocks.append(parts)
    for copy in copies:
        copy.start()
    for parts in blocks:
        for copy in parts:
            copy.start()
    for copy in copies:
        copy.wait()
    for r in range(groups):
        for copy in blocks[r]:
            copy.wait()
        to = pl.ds((r // 2) * block, block)
        for first in range(0, weights.shape[0], 256):
            cols = slice(first, min(first + 256, weights.shape[0]))
            term = lax.dot_general(
                grads[pl.ds(r * block, block), :], weights[cols, :], (((1,), (1,)), ((), ())),
                preferred_element_type=jnp.float32,
            )
            (send_ref if r % 2 else keep_ref)[to, cols] = term.astype(jnp.bfloat16)


def run_state(groups, dk, dv, key_weight, value_weight, after):
    total = dk[0].shape[0]
    enc, local_width = key_weight.shape
    widths = [x.shape[1] for x in dk]
    vmem = pl.BlockSpec(memory_space=pltpu.VMEM)
    return pl.pallas_call(
        functools.partial(state_kernel, groups, widths, len(after)),
        out_shape=[
            jax.ShapeDtypeStruct((total // 2, enc), jnp.bfloat16),
            jax.ShapeDtypeStruct((total // 2, enc), jnp.bfloat16),
        ],
        in_specs=[hbm_spec()] * (2 * len(dk) + 2) + [any_spec()] * len(after),
        out_specs=[vmem, vmem],
        scratch_shapes=[
            pltpu.VMEM((total, 2 * local_width), jnp.bfloat16),
            pltpu.VMEM((enc, 2 * local_width), jnp.bfloat16),
            pltpu.SemaphoreType.DMA((groups + 1, max(2, 2 * len(dk)))),
        ],
        compiler_params=pltpu.CompilerParams(vmem_limit_bytes=VMEM_GRANT),
        cost_estimate=pl.CostEstimate(
            flops=8 * total * enc * local_width, bytes_accessed=8 * total * enc, transcendentals=0
        ),
        name="state_terms",
    )(*in_hbm([*dk, *dv, key_weight, value_weight]), *after)


def fold_kernel(rows_ref, returned_ref, *refs):
    out_hbm, out_ref, sem = refs[-3:]
    out_ref[...] = jnp.zeros_like(out_ref)
    count = out_ref.shape[0]
    for s in range(returned_ref.shape[0]):
        row = rows_ref[s]

        @pl.when(row < count)
        def _():
            out_ref[row] += returned_ref[s].astype(jnp.float32)

    copy = pltpu.make_async_copy(out_ref, out_hbm, sem)
    copy.start()
    copy.wait()


def halve_kernel(choice_ref, keep_ref, recv_ref, *refs):
    stay_ref, send_ref = refs[-2:]
    total = keep_ref[...] + recv_ref[...].astype(jnp.float32)
    half = stay_ref.shape[0]
    upper = choice_ref[0] == 1
    stay_ref[...] = jnp.where(upper, total[half:], total[:half])
    send_ref[...] = jnp.where(upper, total[:half], total[half:]).astype(jnp.bfloat16)


def split_kernel(keep_ref, recv_ref, *refs):
    stay_ref, send_ref = refs[-2:]
    half = stay_ref.shape[0]
    total = keep_ref[...].astype(jnp.float32) + recv_ref[...].astype(jnp.float32)
    stay_ref[...] = total[:half]
    send_ref[...] = total[half:].astype(jnp.bfloat16)


def add_kernel(keep_ref, recv_ref, *refs):
    total = keep_ref[...].astype(jnp.float32) + recv_ref[...].astype(jnp.float32)
    refs[-1][...] = total.astype(refs[-1].dtype)


def order_kernel(halves, pairs, keep_ref, recv_ref, *refs):
    total = keep_ref[...].astype(jnp.float32) + recv_ref[...].astype(jnp.float32)
    piece = total.shape[0] // (halves * pairs)
    parts = [total[(h * pairs + p) * piece :][:piece] for p in range(pairs) for h in range(halves)]
    refs[-1][...] = jnp.concatenate(parts, axis=0).astype(refs[-1].dtype)


def join_kernel(choice_ref, own_ref, recv_ref, *refs):
    out_ref = refs[-1]
    upper = choice_ref[0] == 1
    own, recv = own_ref[...], recv_ref[...]
    rows = own.shape[0]
    if rows % 16:
        own, recv = own.astype(jnp.float32), recv.astype(jnp.float32)
        out = jnp.concatenate([jnp.where(upper, recv, own), jnp.where(upper, own, recv)], axis=0)
        out_ref[...] = out.astype(out_ref.dtype)
    else:
        out_ref[:rows] = jnp.where(upper, recv, own)
        out_ref[rows:] = jnp.where(upper, own, recv)


def place_kernel(start, choice_ref, own_ref, recv_ref, *refs):
    key_hbm, value_hbm, token_ref, key_ref, value_ref, sems = refs[-6:]
    token_ref[...] = jnp.zeros_like(token_ref)
    swapped = choice_ref[0] == 1
    own, recv = own_ref[...].astype(jnp.float32), recv_ref[...].astype(jnp.float32)
    columns = pl.ds(start, own.shape[1])
    key_ref[...] = jnp.where(swapped, recv, own)
    key_out = pltpu.make_async_copy(key_ref, key_hbm.at[:, columns], sems.at[0])
    key_out.start()
    value_ref[...] = jnp.where(swapped, own, recv)
    value_out = pltpu.make_async_copy(value_ref, value_hbm.at[:, columns], sems.at[1])
    value_out.start()
    key_out.wait()
    value_out.wait()


def small(kernel, name, scalars, arrays, outs, after, alias_in=(), out_specs=None, scratch=()):
    vmem = pl.BlockSpec(memory_space=pltpu.VMEM)
    extra = list(alias_in) + list(after)
    first = len(scalars) + len(arrays)
    return pl.pallas_call(
        kernel,
        out_shape=outs,
        in_specs=[pl.BlockSpec(memory_space=pltpu.SMEM)] * len(scalars)
        + [vmem] * len(arrays)
        + [hbm_spec()] * len(alias_in)
        + [any_spec()] * len(after),
        out_specs=out_specs or [vmem] * len(outs),
        scratch_shapes=list(scratch),
        input_output_aliases={first + i: i for i in range(len(alias_in))},
        compiler_params=pltpu.CompilerParams(vmem_limit_bytes=SMALL_GRANT),
        cost_estimate=CHEAP,
        name=name,
    )(*scalars, *arrays, *extra)


class Sum:
    def __init__(self, order, choices, start, enc, width):
        self.choices, self.start, self.enc, self.width = choices, start, enc, width
        self.count = len(order)
        self.steps = list(order) + list(reversed(order))
        self.at = 0

    def begin(self, keep, send):
        self.keep = keep
        self.moving = swap(send, "dp", self.steps[0])

    def load(self, step):
        return self.enc >> (step if step < self.count else 2 * self.count - 1 - step)

    def advance(self, after, outs):
        count, at = self.count, self.at
        self.at += 1
        rows = self.load(at)
        shape = lambda rows, dtype: jax.ShapeDtypeStruct((rows, self.width), dtype)
        if at < count - 1:
            choice = self.choices[self.steps[at + 1]]
            self.keep, send = small(
                halve_kernel, "halve", [choice], [self.keep, self.moving],
                [shape(rows // 2, jnp.float32), shape(rows // 2, jnp.bfloat16)], after,
            )
        elif at == count - 1:
            (send,) = small(add_kernel, "add", [], [self.keep, self.moving], [shape(rows, jnp.bfloat16)], after)
        elif at < 2 * count - 1:
            choice = self.choices[self.steps[at]]
            (send,) = small(
                join_kernel, "join", [choice], [self.own, self.moving], [shape(2 * rows, jnp.bfloat16)], after
            )
        else:
            choice = self.choices[self.steps[at]]
            full = pltpu.HBM(self.full, jnp.float32)
            block = pltpu.VMEM((self.enc, self.width), jnp.float32)
            token = jax.ShapeDtypeStruct((8, 128), jnp.float32)
            *outs, done = small(
                functools.partial(place_kernel, self.start), "place", [choice], [self.own, self.moving],
                [full, full, token], after, alias_in=outs,
                out_specs=[hbm_spec()] * 2 + [pl.BlockSpec(memory_space=pltpu.VMEM)],
                scratch=[block, block, pltpu.SemaphoreType.DMA((2,))],
            )
            return done, outs
        self.own = send
        self.moving = swap(send, "dp", self.steps[at + 1])
        return send, outs


def wavefront(chunks, steps, rest):
    order, done = [], [0] * chunks

    def step(j):
        order.append(f"sum{j}")
        done[j] += 1

    for j in range(chunks):
        order.append(f"heads{j}")
        for earlier in range(j):
            if done[earlier] < steps - 1:
                step(earlier)
    order.append("state")
    for j in [0] + list(range(chunks - 1, 0, -1)):
        step(j)
    period, left, launched = 0, rest, False
    while min(done) < steps or left:
        turn = list(done)
        for j in range(chunks):
            if turn[j] < steps - 1:
                step(j)
        if left > 1 and period != 1:
            order.append("rest")
            left -= 1
        for j in range(chunks):
            if turn[j] == steps - 1:
                step(j)
        if left == 1 and not launched and min(done) >= steps - 1:
            order.append("launch")
            launched = True
        if left == 1 and launched and min(done) == steps:
            order.append("rest")
            left = 0
        period += 1
    return order


def body(queries, states, key_weight, value_weight, nbr_shard, nbr_row, out_grad):
    shards = lax.axis_size("dp")
    groups = lax.axis_size("mp")
    dp_bits, mp_bits = bits_of(shards), bits_of(groups)
    dp_index = lax.axis_index("dp")
    spans, neighbours = nbr_shard.shape
    pair_count = spans * neighbours
    tokens, local_width = queries.shape
    stored, slab_len, enc_width = states.shape
    head_dim = D // H
    capacity = max(2, (pair_count + shards - 1) // shards)
    slot_count = shards * capacity

    owners = nbr_shard.reshape(pair_count)
    row_index = nbr_row.reshape(pair_count)
    pair_ids = jnp.arange(pair_count, dtype=jnp.int32)
    before = (owners[:, None] == owners[None, :]) & (pair_ids[None, :] < pair_ids[:, None])
    slot_index = owners * capacity + jnp.sum(before.astype(jnp.int32), axis=1)
    matched = slot_index[:, None] == jnp.arange(slot_count, dtype=jnp.int32)[None, :]
    asked = stored + jnp.sum(jnp.where(matched, row_index[:, None] - stored, 0), axis=0)
    slot_pair = jnp.sum(jnp.where(matched, pair_ids[:, None], 0), axis=0)
    incoming = lax.all_to_all(
        asked.reshape(shards, capacity), "dp", split_axis=0, concat_axis=0, tiled=True
    ).reshape(slot_count)
    slab_rows = jnp.take(states, jnp.minimum(incoming, stored - 1), axis=0, mode="clip")
    halves = 2
    piece = slab_len // halves
    came = []
    for h in range(halves):
        out = slab_rows[:, h * piece : (h + 1) * piece].reshape(shards, capacity, piece, enc_width)
        came.append(lax.all_to_all(out, "dp", split_axis=0, concat_axis=0, tiled=True))
    blocks = {}
    for h in range(halves):
        back = came[h].reshape(slot_count, piece, enc_width)
        picked = jnp.take(back, slot_index, axis=0, mode="clip").reshape(pair_count * piece, enc_width)
        blocks[0, h] = picked
        for bit in reversed(range(mp_bits)):
            for r in [r for r, k in blocks if k == h]:
                blocks[r | (1 << bit), h] = swap(blocks[r, h], "mp", bit)
    slabs = [blocks[r, h] for r in range(groups) for h in range(halves)]

    heads = local_width // head_dim
    counts = [min(2, heads - first) for first in range(0, heads, 2)]
    bits = list(range(dp_bits))
    choices = [((dp_index >> bit) & 1).astype(jnp.int32).reshape(1) for bit in bits]
    sums = []
    for j, count in enumerate(counts):
        sums.append(Sum(bits, choices, sum(counts[:j]) * head_dim, enc_width, count * head_dim))
        sums[j].full = key_weight.shape

    after, chain, outs, dk, dv = [], [], [], [], []
    rest_bit, pending, held_for = 0, None, 0
    for name in wavefront(len(sums), len(sums[0].steps), mp_bits + 1):
        kind = name.rstrip("0123456789")
        number = int(name[len(kind) :] or 0)
        if kind == "heads":
            part = sums[number]
            chain, dk_part, dv_part, (keep, send) = run_heads(
                part.start, part.width, choices[0], slabs, key_weight, value_weight, queries, out_grad,
                chain, after, spans, head_dim,
            )
            dk.append(dk_part)
            dv.append(dv_part)
            part.begin(keep, send)
            after = [send]
        elif kind == "sum":
            done, outs = sums[number].advance(after, outs)
            after = [done]
            held_for -= 1
            if pending is not None and not held_for:
                pending, _ = lax.optimization_barrier((pending, done))
                moving, pending = swap(pending, "mp", 0), None
        elif kind == "state":
            keep, send = run_state(groups, dk, dv, key_weight, value_weight, after)
            pending, after, held_for = send, [send], len(sums)
        elif kind == "launch":
            outgoing, _ = lax.optimization_barrier((outgoing, after))
            returned = lax.all_to_all(outgoing, "dp", split_axis=0, concat_axis=0, tiled=True)
        elif rest_bit < mp_bits - 1:
            half = keep.shape[0] // 2
            keep, send = small(
                split_kernel, "split", [], [keep, moving],
                [jax.ShapeDtypeStruct((half, enc_width), t) for t in (jnp.float32, jnp.bfloat16)], after,
            )
            moving = swap(send, "mp", mp_bits - 1 - rest_bit)
            after = [send]
            rest_bit += 1
        elif rest_bit == mp_bits - 1:
            (pair_grad,) = small(
                functools.partial(order_kernel, halves, pair_count), "add", [], [keep, moving],
                [jax.ShapeDtypeStruct(keep.shape, jnp.bfloat16)], after,
            )
            after = [pair_grad]
            outgoing = jnp.take(
                pair_grad.reshape(pair_count, slab_len, enc_width), slot_pair, axis=0, mode="clip"
            ).reshape(shards, capacity, slab_len, enc_width)
            rest_bit += 1
        else:
            (state_total,) = small(
                fold_kernel, "fold", [incoming], [returned.reshape(slot_count, slab_len, enc_width)],
                [pltpu.HBM(states.shape, jnp.float32)], after, out_specs=[hbm_spec()],
                scratch=[pltpu.VMEM(states.shape, jnp.float32), pltpu.SemaphoreType.DMA],
            )
    return (chain[0], chain[1], state_total, outs[0], outs[1])


def solution(mesh):
    placed = (
        P("dp", "mp"),
        P("dp", "mp", None),
        P(None, "mp"),
        P(None, "mp"),
        P("dp", None),
        P("dp", None),
        P("dp", "mp"),
    )
    return jax.shard_map(
        body,
        mesh=mesh,
        in_specs=placed,
        out_specs=(P("dp", "mp"), P("dp", "mp"), P("dp", "mp", None), P(None, "mp"), P(None, "mp")),
        check_vma=False,
    )
```

```python
import functools

import jax
import jax.numpy as jnp
from jax import lax
from jax.experimental import pallas as pl
from jax.experimental.pallas import tpu as pltpu
from jax.sharding import PartitionSpec as P

D = 4096
H = 32
VMEM_GRANT = 28 * 1024 * 1024
SMALL_GRANT = 12 * 1024 * 1024
CHEAP = pl.CostEstimate(flops=1, bytes_accessed=1, transcendentals=0)


def bits_of(count):
    return count.bit_length() - 1


def swap(value, axis, bit):
    count = lax.axis_size(axis)
    return lax.ppermute(value, axis, [(i, i ^ (1 << bit)) for i in range(count)])


def any_spec():
    return pl.BlockSpec(memory_space=pl.ANY)


def in_hbm(arrays):
    return [pltpu.with_memory_space_constraint(x, pltpu.HBM) for x in arrays]


def hbm_spec():
    return pl.BlockSpec(memory_space=pltpu.HBM)


def head_kernel(groups, spans, head_dim, start, extra, *refs):
    flag_ref = refs[0]
    slabs = refs[1 : 1 + groups]
    wk_hbm, wv_hbm, q_hbm, g_hbm = refs[1 + groups : 5 + groups]
    att_hbm, dq_hbm, dk_hbm, dv_hbm, keep_ref, send_ref = refs[5 + groups + extra : 11 + groups + extra]
    rows, wk, wv, q_ref, g_ref, keys, values, att_ref, dq_ref, dk_ref, dv_ref, grads, sems = refs[11 + groups + extra :]
    tokens, width = q_ref.shape
    span_len = tokens // spans
    block = rows.shape[0] // groups
    part = block // spans
    scale = 1.0 / head_dim**0.5
    columns = pl.ds(start, width)

    def begin(source, target, sem):
        copy = pltpu.make_async_copy(source, target, sems.at[sem])
        copy.start()
        return copy

    weights_in = [begin(wk_hbm.at[:, columns], wk, groups), begin(wv_hbm.at[:, columns], wv, groups + 1)]
    rows_in = [begin(slabs[r], rows.at[pl.ds(r * block, block)], r) for r in range(groups)]
    tokens_in = [begin(q_hbm.at[:, columns], q_ref, groups + 2), begin(g_hbm.at[:, columns], g_ref, groups + 3)]
    for copy in weights_in:
        copy.wait()
    for r in range(0, groups, 2):
        rows_in[r].wait()
        rows_in[r + 1].wait()
        at = pl.ds(r * block, 2 * block)
        keys[at, :] = jnp.dot(rows[at, :], wk[...], preferred_element_type=jnp.float32).astype(jnp.bfloat16)
        values[at, :] = jnp.dot(rows[at, :], wv[...], preferred_element_type=jnp.float32).astype(jnp.bfloat16)
    for copy in tokens_in:
        copy.wait()

    def spread(x):
        heads = x.shape[1] // head_dim
        lane_head = lax.broadcasted_iota(jnp.int32, x.shape, 1) // head_dim
        zero = jnp.zeros_like(x)
        return jnp.concatenate([jnp.where(lane_head == h, x, zero) for h in range(heads)], axis=0)

    def collect(x):
        out = x[0:span_len]
        lane_head = lax.broadcasted_iota(jnp.int32, out.shape, 1) // head_dim
        for h in range(1, x.shape[1] // head_dim):
            out = jnp.where(lane_head == h, x[h * span_len : (h + 1) * span_len], out)
        return out

    def span_rows(ref, c, cols):
        return jnp.concatenate([ref[pl.ds(r * block + c * part, part), cols] for r in range(groups)], axis=0)

    contract_last = (((1,), (1,)), ((), ()))
    contract_first = (((0,), (0,)), ((), ()))
    at = [pl.ds(c * span_len, span_len) for c in range(spans)]
    swapped = flag_ref[0] == 1
    pair = 2 * head_dim
    for first in range(0, width, pair):
        cols = slice(first, min(first + pair, width))
        send_cols = slice(width + cols.start, width + cols.stop)
        every = range(spans)
        scores = [
            lax.dot_general(
                span_rows(keys, c, cols), spread(q_ref[at[c], cols]), contract_last,
                preferred_element_type=jnp.float32,
            )
            * scale
            for c in every
        ]
        prob_grad = [
            lax.dot_general(
                span_rows(values, c, cols), spread(g_ref[at[c], cols]), contract_last,
                preferred_element_type=jnp.float32,
            )
            for c in every
        ]
        weights = [jnp.exp(x - jnp.max(x, axis=0, keepdims=True)) for x in scores]
        probs = [x * (1.0 / jnp.sum(x, axis=0, keepdims=True)) for x in weights]
        low = [x.astype(jnp.bfloat16) for x in probs]
        row_dot = [jnp.sum(p * d, axis=0, keepdims=True) for p, d in zip(probs, prob_grad)]
        score_grad = [(scale * p * (d - t)).astype(jnp.bfloat16) for p, d, t in zip(probs, prob_grad, row_dot)]
        for c in every:
            dk = jnp.dot(score_grad[c], spread(q_ref[at[c], cols]), preferred_element_type=jnp.float32)
            dv = jnp.dot(low[c], spread(g_ref[at[c], cols]), preferred_element_type=jnp.float32)
            dk, dv = dk.astype(jnp.bfloat16), dv.astype(jnp.bfloat16)
            for r in range(groups):
                to = pl.ds(r * block + c * part, part)
                piece = slice(r * part, (r + 1) * part)
                dk_ref[to, cols] = dk[piece]
                dv_ref[to, cols] = dv[piece]
                grads[to, cols] = jnp.where(swapped, dv[piece], dk[piece])
                grads[to, send_cols] = jnp.where(swapped, dk[piece], dv[piece])
        for c in every:
            att = lax.dot_general(
                low[c], span_rows(values, c, cols), contract_first, preferred_element_type=jnp.float32
            )
            att_ref[at[c], cols] = collect(att).astype(jnp.bfloat16)
            dq = lax.dot_general(
                score_grad[c], span_rows(keys, c, cols), contract_first, preferred_element_type=jnp.float32
            )
            dq_ref[at[c], cols] = collect(dq).astype(jnp.bfloat16)
    results = [
        begin(att_ref, att_hbm.at[:, columns], 0),
        begin(dq_ref, dq_hbm.at[:, columns], 1),
        begin(dk_ref, dk_hbm, 2),
        begin(dv_ref, dv_hbm, 3),
    ]
    tile = 128
    for first in range(0, rows.shape[1], tile):
        to = slice(first, first + tile)
        both = lax.dot_general(rows[:, to], grads[...], contract_first, preferred_element_type=jnp.float32)
        keep_ref[to, :] = both[:, :width]
        send_ref[to, :] = both[:, width:].astype(jnp.bfloat16)
    for copy in results:
        copy.wait()


def run_heads(start, chunk, flag, slabs, key_weight, value_weight, queries, out_grad, chain, after, spans, head_dim):
    groups = len(slabs)
    tokens, local_width = queries.shape
    block, enc = slabs[0].shape
    total = groups * block
    bf = jnp.bfloat16
    extra = list(chain) + list(after)
    outs = pl.pallas_call(
        functools.partial(head_kernel, groups, spans, head_dim, start, len(extra)),
        out_shape=[
            pltpu.HBM((tokens, local_width), bf),
            pltpu.HBM((tokens, local_width), bf),
            pltpu.HBM((total, chunk), bf),
            pltpu.HBM((total, chunk), bf),
            jax.ShapeDtypeStruct((enc, chunk), jnp.float32),
            jax.ShapeDtypeStruct((enc, chunk), bf),
        ],
        in_specs=[pl.BlockSpec(memory_space=pltpu.SMEM)]
        + [any_spec()] * groups
        + [hbm_spec()] * (4 + len(chain))
        + [any_spec()] * len(after),
        out_specs=[hbm_spec()] * 4 + [pl.BlockSpec(memory_space=pltpu.VMEM)] * 2,
        scratch_shapes=[
            pltpu.VMEM((total, enc), bf),
            pltpu.VMEM((enc, chunk), bf),
            pltpu.VMEM((enc, chunk), bf),
            pltpu.VMEM((tokens, chunk), bf),
            pltpu.VMEM((tokens, chunk), bf),
            pltpu.VMEM((total, chunk), bf),
            pltpu.VMEM((total, chunk), bf),
            pltpu.VMEM((tokens, chunk), bf),
            pltpu.VMEM((tokens, chunk), bf),
            pltpu.VMEM((total, chunk), bf),
            pltpu.VMEM((total, chunk), bf),
            pltpu.VMEM((total, 2 * chunk), bf),
            pltpu.SemaphoreType.DMA((groups + 4,)),
        ],
        input_output_aliases={5 + groups + i: i for i in range(len(chain))},
        compiler_params=pltpu.CompilerParams(vmem_limit_bytes=VMEM_GRANT),
        cost_estimate=pl.CostEstimate(
            flops=2 * total * enc * chunk * 8, bytes_accessed=4 * total * enc, transcendentals=total * tokens
        ),
        name="heads",
    )(flag, *slabs, *in_hbm([key_weight, value_weight, queries, out_grad, *chain]), *after)
    return outs[:2], outs[2], outs[3], outs[4:]


def state_kernel(groups, widths, extra, *refs):
    count = len(widths)
    dk_hbm, dv_hbm = refs[:count], refs[count : 2 * count]
    wk_hbm, wv_hbm = refs[2 * count : 2 * count + 2]
    keep_ref, send_ref, grads, weights, sems = refs[2 * count + 2 + extra :]
    half = weights.shape[1] // 2
    block = grads.shape[0] // groups

    copies = [
        pltpu.make_async_copy(wk_hbm, weights.at[:, pl.ds(0, half)], sems.at[0, 0]),
        pltpu.make_async_copy(wv_hbm, weights.at[:, pl.ds(half, half)], sems.at[0, 1]),
    ]
    blocks = []
    for r in range(groups):
        rows = pl.ds(r * block, block)
        parts = []
        for j in range(count):
            first = sum(widths[:j])
            for k, source in enumerate((dk_hbm[j], dv_hbm[j])):
                target = grads.at[rows, pl.ds(k * half + first, widths[j])]
                parts.append(pltpu.make_async_copy(source.at[rows, :], target, sems.at[1 + r, 2 * j + k]))
        blocks.append(parts)
    for copy in copies:
        copy.start()
    for parts in blocks:
        for copy in parts:
            copy.start()
    for copy in copies:
        copy.wait()
    for r in range(groups):
        for copy in blocks[r]:
            copy.wait()
        to = pl.ds((r // 2) * block, block)
        for first in range(0, weights.shape[0], 256):
            cols = slice(first, min(first + 256, weights.shape[0]))
            term = lax.dot_general(
                grads[pl.ds(r * block, block), :], weights[cols, :], (((1,), (1,)), ((), ())),
                preferred_element_type=jnp.float32,
            )
            (send_ref if r % 2 else keep_ref)[to, cols] = term.astype(jnp.bfloat16)


def run_state(groups, dk, dv, key_weight, value_weight, after):
    total = dk[0].shape[0]
    enc, local_width = key_weight.shape
    widths = [x.shape[1] for x in dk]
    vmem = pl.BlockSpec(memory_space=pltpu.VMEM)
    return pl.pallas_call(
        functools.partial(state_kernel, groups, widths, len(after)),
        out_shape=[
            jax.ShapeDtypeStruct((total // 2, enc), jnp.bfloat16),
            jax.ShapeDtypeStruct((total // 2, enc), jnp.bfloat16),
        ],
        in_specs=[hbm_spec()] * (2 * len(dk) + 2) + [any_spec()] * len(after),
        out_specs=[vmem, vmem],
        scratch_shapes=[
            pltpu.VMEM((total, 2 * local_width), jnp.bfloat16),
            pltpu.VMEM((enc, 2 * local_width), jnp.bfloat16),
            pltpu.SemaphoreType.DMA((groups + 1, max(2, 2 * len(dk)))),
        ],
        compiler_params=pltpu.CompilerParams(vmem_limit_bytes=VMEM_GRANT),
        cost_estimate=pl.CostEstimate(
            flops=8 * total * enc * local_width, bytes_accessed=8 * total * enc, transcendentals=0
        ),
        name="state_terms",
    )(*in_hbm([*dk, *dv, key_weight, value_weight]), *after)


def fold_kernel(rows_ref, returned_ref, *refs):
    out_hbm, out_ref, sem = refs[-3:]
    out_ref[...] = jnp.zeros_like(out_ref)
    count = out_ref.shape[0]
    for s in range(returned_ref.shape[0]):
        row = rows_ref[s]

        @pl.when(row < count)
        def _():
            out_ref[row] += returned_ref[s].astype(jnp.float32)

    copy = pltpu.make_async_copy(out_ref, out_hbm, sem)
    copy.start()
    copy.wait()


def halve_kernel(choice_ref, keep_ref, recv_ref, *refs):
    stay_ref, send_ref = refs[-2:]
    total = keep_ref[...] + recv_ref[...].astype(jnp.float32)
    half = stay_ref.shape[0]
    upper = choice_ref[0] == 1
    stay_ref[...] = jnp.where(upper, total[half:], total[:half])
    send_ref[...] = jnp.where(upper, total[:half], total[half:]).astype(jnp.bfloat16)


def split_kernel(keep_ref, recv_ref, *refs):
    stay_ref, send_ref = refs[-2:]
    half = stay_ref.shape[0]
    total = keep_ref[...].astype(jnp.float32) + recv_ref[...].astype(jnp.float32)
    stay_ref[...] = total[:half]
    send_ref[...] = total[half:].astype(jnp.bfloat16)


def add_kernel(keep_ref, recv_ref, *refs):
    total = keep_ref[...].astype(jnp.float32) + recv_ref[...].astype(jnp.float32)
    refs[-1][...] = total.astype(refs[-1].dtype)


def order_kernel(halves, pairs, keep_ref, recv_ref, *refs):
    total = keep_ref[...].astype(jnp.float32) + recv_ref[...].astype(jnp.float32)
    piece = total.shape[0] // (halves * pairs)
    parts = [total[(h * pairs + p) * piece :][:piece] for p in range(pairs) for h in range(halves)]
    refs[-1][...] = jnp.concatenate(parts, axis=0).astype(refs[-1].dtype)


def join_kernel(choice_ref, own_ref, recv_ref, *refs):
    out_ref = refs[-1]
    upper = choice_ref[0] == 1
    own, recv = own_ref[...], recv_ref[...]
    rows = own.shape[0]
    if rows % 16:
        own, recv = own.astype(jnp.float32), recv.astype(jnp.float32)
        out = jnp.concatenate([jnp.where(upper, recv, own), jnp.where(upper, own, recv)], axis=0)
        out_ref[...] = out.astype(out_ref.dtype)
    else:
        out_ref[:rows] = jnp.where(upper, recv, own)
        out_ref[rows:] = jnp.where(upper, own, recv)


def place_kernel(start, choice_ref, own_ref, recv_ref, *refs):
    key_hbm, value_hbm, token_ref, key_ref, value_ref, sems = refs[-6:]
    token_ref[...] = jnp.zeros_like(token_ref)
    swapped = choice_ref[0] == 1
    own, recv = own_ref[...].astype(jnp.float32), recv_ref[...].astype(jnp.float32)
    columns = pl.ds(start, own.shape[1])
    key_ref[...] = jnp.where(swapped, recv, own)
    key_out = pltpu.make_async_copy(key_ref, key_hbm.at[:, columns], sems.at[0])
    key_out.start()
    value_ref[...] = jnp.where(swapped, own, recv)
    value_out = pltpu.make_async_copy(value_ref, value_hbm.at[:, columns], sems.at[1])
    value_out.start()
    key_out.wait()
    value_out.wait()


def small(kernel, name, scalars, arrays, outs, after, alias_in=(), out_specs=None, scratch=()):
    vmem = pl.BlockSpec(memory_space=pltpu.VMEM)
    extra = list(alias_in) + list(after)
    first = len(scalars) + len(arrays)
    return pl.pallas_call(
        kernel,
        out_shape=outs,
        in_specs=[pl.BlockSpec(memory_space=pltpu.SMEM)] * len(scalars)
        + [vmem] * len(arrays)
        + [hbm_spec()] * len(alias_in)
        + [any_spec()] * len(after),
        out_specs=out_specs or [vmem] * len(outs),
        scratch_shapes=list(scratch),
        input_output_aliases={first + i: i for i in range(len(alias_in))},
        compiler_params=pltpu.CompilerParams(vmem_limit_bytes=SMALL_GRANT),
        cost_estimate=CHEAP,
        name=name,
    )(*scalars, *arrays, *extra)


class Sum:
    def __init__(self, order, choices, start, enc, width):
        self.choices, self.start, self.enc, self.width = choices, start, enc, width
        self.count = len(order)
        self.steps = list(order) + list(reversed(order))
        self.at = 0

    def begin(self, keep, send):
        self.keep = keep
        self.moving = swap(send, "dp", self.steps[0])

    def load(self, step):
        return self.enc >> (step if step < self.count else 2 * self.count - 1 - step)

    def advance(self, after, outs):
        count, at = self.count, self.at
        self.at += 1
        rows = self.load(at)
        shape = lambda rows, dtype: jax.ShapeDtypeStruct((rows, self.width), dtype)
        if at < count - 1:
            choice = self.choices[self.steps[at + 1]]
            self.keep, send = small(
                halve_kernel, "halve", [choice], [self.keep, self.moving],
                [shape(rows // 2, jnp.float32), shape(rows // 2, jnp.bfloat16)], after,
            )
        elif at == count - 1:
            (send,) = small(add_kernel, "add", [], [self.keep, self.moving], [shape(rows, jnp.bfloat16)], after)
        elif at < 2 * count - 1:
            choice = self.choices[self.steps[at]]
            (send,) = small(
                join_kernel, "join", [choice], [self.own, self.moving], [shape(2 * rows, jnp.bfloat16)], after
            )
        else:
            choice = self.choices[self.steps[at]]
            full = pltpu.HBM(self.full, jnp.float32)
            block = pltpu.VMEM((self.enc, self.width), jnp.float32)
            token = jax.ShapeDtypeStruct((8, 128), jnp.float32)
            *outs, done = small(
                functools.partial(place_kernel, self.start), "place", [choice], [self.own, self.moving],
                [full, full, token], after, alias_in=outs,
                out_specs=[hbm_spec()] * 2 + [pl.BlockSpec(memory_space=pltpu.VMEM)],
                scratch=[block, block, pltpu.SemaphoreType.DMA((2,))],
            )
            return done, outs
        self.own = send
        self.moving = swap(send, "dp", self.steps[at + 1])
        return send, outs


def wavefront(chunks, steps, rest):
    order, done = [], [0] * chunks

    def step(j):
        order.append(f"sum{j}")
        done[j] += 1

    for j in range(chunks):
        order.append(f"heads{j}")
        for earlier in range(j):
            if done[earlier] < steps - 1:
                step(earlier)
    order.append("state")
    for j in [0] + list(range(chunks - 1, 0, -1)):
        step(j)
    period, left, launched = 0, rest, False
    while min(done) < steps or left:
        turn = list(done)
        for j in range(chunks):
            if turn[j] < steps - 1:
                step(j)
        if left > 1 and period != 1:
            order.append("rest")
            left -= 1
        for j in range(chunks):
            if turn[j] == steps - 1:
                step(j)
        if left == 1 and not launched and min(done) >= steps - 2:
            order.append("launch")
            launched = True
        if left == 1 and launched and min(done) == steps:
            order.append("rest")
            left = 0
        period += 1
    return order


def body(queries, states, key_weight, value_weight, nbr_shard, nbr_row, out_grad):
    shards = lax.axis_size("dp")
    groups = lax.axis_size("mp")
    dp_bits, mp_bits = bits_of(shards), bits_of(groups)
    dp_index = lax.axis_index("dp")
    spans, neighbours = nbr_shard.shape
    pair_count = spans * neighbours
    tokens, local_width = queries.shape
    stored, slab_len, enc_width = states.shape
    head_dim = D // H
    capacity = max(2, (pair_count + shards - 1) // shards)
    slot_count = shards * capacity

    owners = nbr_shard.reshape(pair_count)
    row_index = nbr_row.reshape(pair_count)
    pair_ids = jnp.arange(pair_count, dtype=jnp.int32)
    before = (owners[:, None] == owners[None, :]) & (pair_ids[None, :] < pair_ids[:, None])
    slot_index = owners * capacity + jnp.sum(before.astype(jnp.int32), axis=1)
    matched = slot_index[:, None] == jnp.arange(slot_count, dtype=jnp.int32)[None, :]
    asked = stored + jnp.sum(jnp.where(matched, row_index[:, None] - stored, 0), axis=0)
    slot_pair = jnp.sum(jnp.where(matched, pair_ids[:, None], 0), axis=0)
    incoming = lax.all_to_all(
        asked.reshape(shards, capacity), "dp", split_axis=0, concat_axis=0, tiled=True
    ).reshape(slot_count)
    slab_rows = jnp.take(states, jnp.minimum(incoming, stored - 1), axis=0, mode="clip")
    halves = 2
    piece = slab_len // halves
    came = []
    for h in range(halves):
        out = slab_rows[:, h * piece : (h + 1) * piece].reshape(shards, capacity, piece, enc_width)
        came.append(lax.all_to_all(out, "dp", split_axis=0, concat_axis=0, tiled=True))
    blocks = {}
    for h in range(halves):
        back = came[h].reshape(slot_count, piece, enc_width)
        picked = jnp.take(back, slot_index, axis=0, mode="clip").reshape(pair_count * piece, enc_width)
        blocks[0, h] = picked
        for bit in reversed(range(mp_bits)):
            for r in [r for r, k in blocks if k == h]:
                blocks[r | (1 << bit), h] = swap(blocks[r, h], "mp", bit)
    slabs = [blocks[r, h] for r in range(groups) for h in range(halves)]

    heads = local_width // head_dim
    counts = [min(2, heads - first) for first in range(0, heads, 2)]
    bits = list(range(dp_bits))
    choices = [((dp_index >> bit) & 1).astype(jnp.int32).reshape(1) for bit in bits]
    sums = []
    for j, count in enumerate(counts):
        sums.append(Sum(bits, choices, sum(counts[:j]) * head_dim, enc_width, count * head_dim))
        sums[j].full = key_weight.shape

    after, chain, outs, dk, dv = [], [], [], [], []
    rest_bit, pending, held_for = 0, None, 0
    for name in wavefront(len(sums), len(sums[0].steps), mp_bits + 1):
        kind = name.rstrip("0123456789")
        number = int(name[len(kind) :] or 0)
        if kind == "heads":
            part = sums[number]
            chain, dk_part, dv_part, (keep, send) = run_heads(
                part.start, part.width, choices[0], slabs, key_weight, value_weight, queries, out_grad,
                chain, after, spans, head_dim,
            )
            dk.append(dk_part)
            dv.append(dv_part)
            part.begin(keep, send)
            after = [send]
        elif kind == "sum":
            done, outs = sums[number].advance(after, outs)
            after = [done]
            held_for -= 1
            if pending is not None and not held_for:
                pending, _ = lax.optimization_barrier((pending, done))
                moving, pending = swap(pending, "mp", 0), None
        elif kind == "state":
            keep, send = run_state(groups, dk, dv, key_weight, value_weight, after)
            pending, after, held_for = send, [send], len(sums)
        elif kind == "launch":
            outgoing, _ = lax.optimization_barrier((outgoing, after))
            returned = lax.all_to_all(outgoing, "dp", split_axis=0, concat_axis=0, tiled=True)
        elif rest_bit < mp_bits - 1:
            half = keep.shape[0] // 2
            keep, send = small(
                split_kernel, "split", [], [keep, moving],
                [jax.ShapeDtypeStruct((half, enc_width), t) for t in (jnp.float32, jnp.bfloat16)], after,
            )
            moving = swap(send, "mp", mp_bits - 1 - rest_bit)
            after = [send]
            rest_bit += 1
        elif rest_bit == mp_bits - 1:
            (pair_grad,) = small(
                functools.partial(order_kernel, halves, pair_count), "add", [], [keep, moving],
                [jax.ShapeDtypeStruct(keep.shape, jnp.bfloat16)], after,
            )
            after = [pair_grad]
            outgoing = jnp.take(
                pair_grad.reshape(pair_count, slab_len, enc_width), slot_pair, axis=0, mode="clip"
            ).reshape(shards, capacity, slab_len, enc_width)
            after = [outgoing]
            rest_bit += 1
        else:
            (state_total,) = small(
                fold_kernel, "fold", [incoming], [returned.reshape(slot_count, slab_len, enc_width)],
                [pltpu.HBM(states.shape, jnp.float32)], after, out_specs=[hbm_spec()],
                scratch=[pltpu.VMEM(states.shape, jnp.float32), pltpu.SemaphoreType.DMA],
            )
    return (chain[0], chain[1], state_total, outs[0], outs[1])


def solution(mesh):
    placed = (
        P("dp", "mp"),
        P("dp", "mp", None),
        P(None, "mp"),
        P(None, "mp"),
        P("dp", None),
        P("dp", None),
        P("dp", "mp"),
    )
    return jax.shard_map(
        body,
        mesh=mesh,
        in_specs=placed,
        out_specs=(P("dp", "mp"), P("dp", "mp"), P("dp", "mp", None), P(None, "mp"), P(None, "mp")),
        check_vma=False,
    )
```

```python
import functools

import jax
import jax.numpy as jnp
from jax import lax
from jax.experimental import pallas as pl
from jax.experimental.pallas import tpu as pltpu
from jax.sharding import PartitionSpec as P

D = 4096
H = 32
VMEM_GRANT = 28 * 1024 * 1024
SMALL_GRANT = 12 * 1024 * 1024
CHEAP = pl.CostEstimate(flops=1, bytes_accessed=1, transcendentals=0)


def bits_of(count):
    return count.bit_length() - 1


def swap(value, axis, bit):
    count = lax.axis_size(axis)
    return lax.ppermute(value, axis, [(i, i ^ (1 << bit)) for i in range(count)])


def any_spec():
    return pl.BlockSpec(memory_space=pl.ANY)


def in_hbm(arrays):
    return [pltpu.with_memory_space_constraint(x, pltpu.HBM) for x in arrays]


def hbm_spec():
    return pl.BlockSpec(memory_space=pltpu.HBM)


def head_kernel(groups, spans, head_dim, start, extra, *refs):
    flag_ref = refs[0]
    slabs = refs[1 : 1 + groups]
    wk_hbm, wv_hbm, q_hbm, g_hbm = refs[1 + groups : 5 + groups]
    att_hbm, dq_hbm, dk_hbm, dv_hbm, keep_ref, send_ref = refs[5 + groups + extra : 11 + groups + extra]
    rows, wk, wv, q_ref, g_ref, keys, values, att_ref, dq_ref, dk_ref, dv_ref, grads, sems = refs[11 + groups + extra :]
    tokens, width = q_ref.shape
    span_len = tokens // spans
    block = rows.shape[0] // groups
    part = block // spans
    scale = 1.0 / head_dim**0.5
    columns = pl.ds(start, width)

    def begin(source, target, sem):
        copy = pltpu.make_async_copy(source, target, sems.at[sem])
        copy.start()
        return copy

    weights_in = [begin(wk_hbm.at[:, columns], wk, groups), begin(wv_hbm.at[:, columns], wv, groups + 1)]
    rows_in = [begin(slabs[r], rows.at[pl.ds(r * block, block)], r) for r in range(groups)]
    tokens_in = [begin(q_hbm.at[:, columns], q_ref, groups + 2), begin(g_hbm.at[:, columns], g_ref, groups + 3)]
    for copy in weights_in:
        copy.wait()
    for r in range(0, groups, 2):
        rows_in[r].wait()
        rows_in[r + 1].wait()
        at = pl.ds(r * block, 2 * block)
        keys[at, :] = jnp.dot(rows[at, :], wk[...], preferred_element_type=jnp.float32).astype(jnp.bfloat16)
        values[at, :] = jnp.dot(rows[at, :], wv[...], preferred_element_type=jnp.float32).astype(jnp.bfloat16)
    for copy in tokens_in:
        copy.wait()

    def spread(x):
        heads = x.shape[1] // head_dim
        lane_head = lax.broadcasted_iota(jnp.int32, x.shape, 1) // head_dim
        zero = jnp.zeros_like(x)
        return jnp.concatenate([jnp.where(lane_head == h, x, zero) for h in range(heads)], axis=0)

    def collect(x):
        out = x[0:span_len]
        lane_head = lax.broadcasted_iota(jnp.int32, out.shape, 1) // head_dim
        for h in range(1, x.shape[1] // head_dim):
            out = jnp.where(lane_head == h, x[h * span_len : (h + 1) * span_len], out)
        return out

    def span_rows(ref, c, cols):
        return jnp.concatenate([ref[pl.ds(r * block + c * part, part), cols] for r in range(groups)], axis=0)

    contract_last = (((1,), (1,)), ((), ()))
    contract_first = (((0,), (0,)), ((), ()))
    at = [pl.ds(c * span_len, span_len) for c in range(spans)]
    swapped = flag_ref[0] == 1
    pair = 2 * head_dim
    for first in range(0, width, pair):
        cols = slice(first, min(first + pair, width))
        send_cols = slice(width + cols.start, width + cols.stop)
        every = range(spans)
        scores = [
            lax.dot_general(
                span_rows(keys, c, cols), spread(q_ref[at[c], cols]), contract_last,
                preferred_element_type=jnp.float32,
            )
            * scale
            for c in every
        ]
        prob_grad = [
            lax.dot_general(
                span_rows(values, c, cols), spread(g_ref[at[c], cols]), contract_last,
                preferred_element_type=jnp.float32,
            )
            for c in every
        ]
        weights = [jnp.exp(x - jnp.max(x, axis=0, keepdims=True)) for x in scores]
        probs = [x * (1.0 / jnp.sum(x, axis=0, keepdims=True)) for x in weights]
        low = [x.astype(jnp.bfloat16) for x in probs]
        row_dot = [jnp.sum(p * d, axis=0, keepdims=True) for p, d in zip(probs, prob_grad)]
        score_grad = [(scale * p * (d - t)).astype(jnp.bfloat16) for p, d, t in zip(probs, prob_grad, row_dot)]
        for c in every:
            dk = jnp.dot(score_grad[c], spread(q_ref[at[c], cols]), preferred_element_type=jnp.float32)
            dv = jnp.dot(low[c], spread(g_ref[at[c], cols]), preferred_element_type=jnp.float32)
            dk, dv = dk.astype(jnp.bfloat16), dv.astype(jnp.bfloat16)
            for r in range(groups):
                to = pl.ds(r * block + c * part, part)
                piece = slice(r * part, (r + 1) * part)
                dk_ref[to, cols] = dk[piece]
                dv_ref[to, cols] = dv[piece]
                grads[to, cols] = jnp.where(swapped, dv[piece], dk[piece])
                grads[to, send_cols] = jnp.where(swapped, dk[piece], dv[piece])
        for c in every:
            att = lax.dot_general(
                low[c], span_rows(values, c, cols), contract_first, preferred_element_type=jnp.float32
            )
            att_ref[at[c], cols] = collect(att).astype(jnp.bfloat16)
            dq = lax.dot_general(
                score_grad[c], span_rows(keys, c, cols), contract_first, preferred_element_type=jnp.float32
            )
            dq_ref[at[c], cols] = collect(dq).astype(jnp.bfloat16)
    results = [
        begin(att_ref, att_hbm.at[:, columns], 0),
        begin(dq_ref, dq_hbm.at[:, columns], 1),
        begin(dk_ref, dk_hbm, 2),
        begin(dv_ref, dv_hbm, 3),
    ]
    tile = 128
    for first in range(0, rows.shape[1], tile):
        to = slice(first, first + tile)
        both = lax.dot_general(rows[:, to], grads[...], contract_first, preferred_element_type=jnp.float32)
        keep_ref[to, :] = both[:, :width]
        send_ref[to, :] = both[:, width:].astype(jnp.bfloat16)
    for copy in results:
        copy.wait()


def run_heads(start, chunk, flag, slabs, key_weight, value_weight, queries, out_grad, chain, after, spans, head_dim):
    groups = len(slabs)
    tokens, local_width = queries.shape
    block, enc = slabs[0].shape
    total = groups * block
    bf = jnp.bfloat16
    extra = list(chain) + list(after)
    outs = pl.pallas_call(
        functools.partial(head_kernel, groups, spans, head_dim, start, len(extra)),
        out_shape=[
            pltpu.HBM((tokens, local_width), bf),
            pltpu.HBM((tokens, local_width), bf),
            pltpu.HBM((total, chunk), bf),
            pltpu.HBM((total, chunk), bf),
            jax.ShapeDtypeStruct((enc, chunk), jnp.float32),
            jax.ShapeDtypeStruct((enc, chunk), bf),
        ],
        in_specs=[pl.BlockSpec(memory_space=pltpu.SMEM)]
        + [any_spec()] * groups
        + [hbm_spec()] * (4 + len(chain))
        + [any_spec()] * len(after),
        out_specs=[hbm_spec()] * 4 + [pl.BlockSpec(memory_space=pltpu.VMEM)] * 2,
        scratch_shapes=[
            pltpu.VMEM((total, enc), bf),
            pltpu.VMEM((enc, chunk), bf),
            pltpu.VMEM((enc, chunk), bf),
            pltpu.VMEM((tokens, chunk), bf),
            pltpu.VMEM((tokens, chunk), bf),
            pltpu.VMEM((total, chunk), bf),
            pltpu.VMEM((total, chunk), bf),
            pltpu.VMEM((tokens, chunk), bf),
            pltpu.VMEM((tokens, chunk), bf),
            pltpu.VMEM((total, chunk), bf),
            pltpu.VMEM((total, chunk), bf),
            pltpu.VMEM((total, 2 * chunk), bf),
            pltpu.SemaphoreType.DMA((groups + 4,)),
        ],
        input_output_aliases={5 + groups + i: i for i in range(len(chain))},
        compiler_params=pltpu.CompilerParams(vmem_limit_bytes=VMEM_GRANT),
        cost_estimate=pl.CostEstimate(
            flops=2 * total * enc * chunk * 8, bytes_accessed=4 * total * enc, transcendentals=total * tokens
        ),
        name="heads",
    )(flag, *slabs, *in_hbm([key_weight, value_weight, queries, out_grad, *chain]), *after)
    return outs[:2], outs[2], outs[3], outs[4:]


def state_kernel(groups, widths, extra, *refs):
    count = len(widths)
    dk_hbm, dv_hbm = refs[:count], refs[count : 2 * count]
    wk_hbm, wv_hbm = refs[2 * count : 2 * count + 2]
    keep_ref, send_ref, grads, weights, sems = refs[2 * count + 2 + extra :]
    half = weights.shape[1] // 2
    block = grads.shape[0] // groups

    copies = [
        pltpu.make_async_copy(wk_hbm, weights.at[:, pl.ds(0, half)], sems.at[0, 0]),
        pltpu.make_async_copy(wv_hbm, weights.at[:, pl.ds(half, half)], sems.at[0, 1]),
    ]
    blocks = []
    for r in range(groups):
        rows = pl.ds(r * block, block)
        parts = []
        for j in range(count):
            first = sum(widths[:j])
            for k, source in enumerate((dk_hbm[j], dv_hbm[j])):
                target = grads.at[rows, pl.ds(k * half + first, widths[j])]
                parts.append(pltpu.make_async_copy(source.at[rows, :], target, sems.at[1 + r, 2 * j + k]))
        blocks.append(parts)
    for copy in copies:
        copy.start()
    for parts in blocks:
        for copy in parts:
            copy.start()
    for copy in copies:
        copy.wait()
    for r in range(groups):
        for copy in blocks[r]:
            copy.wait()
        to = pl.ds((r // 2) * block, block)
        for first in range(0, weights.shape[0], 256):
            cols = slice(first, min(first + 256, weights.shape[0]))
            term = lax.dot_general(
                grads[pl.ds(r * block, block), :], weights[cols, :], (((1,), (1,)), ((), ())),
                preferred_element_type=jnp.float32,
            )
            (send_ref if r % 2 else keep_ref)[to, cols] = term.astype(jnp.bfloat16)


def run_state(groups, dk, dv, key_weight, value_weight, after):
    total = dk[0].shape[0]
    enc, local_width = key_weight.shape
    widths = [x.shape[1] for x in dk]
    vmem = pl.BlockSpec(memory_space=pltpu.VMEM)
    return pl.pallas_call(
        functools.partial(state_kernel, groups, widths, len(after)),
        out_shape=[
            jax.ShapeDtypeStruct((total // 2, enc), jnp.bfloat16),
            jax.ShapeDtypeStruct((total // 2, enc), jnp.bfloat16),
        ],
        in_specs=[hbm_spec()] * (2 * len(dk) + 2) + [any_spec()] * len(after),
        out_specs=[vmem, vmem],
        scratch_shapes=[
            pltpu.VMEM((total, 2 * local_width), jnp.bfloat16),
            pltpu.VMEM((enc, 2 * local_width), jnp.bfloat16),
            pltpu.SemaphoreType.DMA((groups + 1, max(2, 2 * len(dk)))),
        ],
        compiler_params=pltpu.CompilerParams(vmem_limit_bytes=VMEM_GRANT),
        cost_estimate=pl.CostEstimate(
            flops=8 * total * enc * local_width, bytes_accessed=8 * total * enc, transcendentals=0
        ),
        name="state_terms",
    )(*in_hbm([*dk, *dv, key_weight, value_weight]), *after)


def fold_kernel(rows_ref, returned_ref, *refs):
    out_hbm, out_ref, sem = refs[-3:]
    out_ref[...] = jnp.zeros_like(out_ref)
    count = out_ref.shape[0]
    for s in range(returned_ref.shape[0]):
        row = rows_ref[s]

        @pl.when(row < count)
        def _():
            out_ref[row] += returned_ref[s].astype(jnp.float32)

    copy = pltpu.make_async_copy(out_ref, out_hbm, sem)
    copy.start()
    copy.wait()


def halve_kernel(choice_ref, keep_ref, recv_ref, *refs):
    stay_ref, send_ref = refs[-2:]
    total = keep_ref[...] + recv_ref[...].astype(jnp.float32)
    half = stay_ref.shape[0]
    upper = choice_ref[0] == 1
    stay_ref[...] = jnp.where(upper, total[half:], total[:half])
    send_ref[...] = jnp.where(upper, total[:half], total[half:]).astype(jnp.bfloat16)


def split_kernel(keep_ref, recv_ref, *refs):
    stay_ref, send_ref = refs[-2:]
    half = stay_ref.shape[0]
    total = keep_ref[...].astype(jnp.float32) + recv_ref[...].astype(jnp.float32)
    stay_ref[...] = total[:half]
    send_ref[...] = total[half:].astype(jnp.bfloat16)


def add_kernel(keep_ref, recv_ref, *refs):
    total = keep_ref[...].astype(jnp.float32) + recv_ref[...].astype(jnp.float32)
    refs[-1][...] = total.astype(refs[-1].dtype)


def order_kernel(halves, pairs, keep_ref, recv_ref, *refs):
    total = keep_ref[...].astype(jnp.float32) + recv_ref[...].astype(jnp.float32)
    piece = total.shape[0] // (halves * pairs)
    parts = [total[(h * pairs + p) * piece :][:piece] for p in range(pairs) for h in range(halves)]
    refs[-1][...] = jnp.concatenate(parts, axis=0).astype(refs[-1].dtype)


def join_kernel(choice_ref, own_ref, recv_ref, *refs):
    out_ref = refs[-1]
    upper = choice_ref[0] == 1
    own, recv = own_ref[...], recv_ref[...]
    rows = own.shape[0]
    if rows % 16:
        own, recv = own.astype(jnp.float32), recv.astype(jnp.float32)
        out = jnp.concatenate([jnp.where(upper, recv, own), jnp.where(upper, own, recv)], axis=0)
        out_ref[...] = out.astype(out_ref.dtype)
    else:
        out_ref[:rows] = jnp.where(upper, recv, own)
        out_ref[rows:] = jnp.where(upper, own, recv)


def place_kernel(start, choice_ref, own_ref, recv_ref, *refs):
    key_hbm, value_hbm, token_ref, key_ref, value_ref, sems = refs[-6:]
    token_ref[...] = jnp.zeros_like(token_ref)
    swapped = choice_ref[0] == 1
    own, recv = own_ref[...].astype(jnp.float32), recv_ref[...].astype(jnp.float32)
    columns = pl.ds(start, own.shape[1])
    key_ref[...] = jnp.where(swapped, recv, own)
    key_out = pltpu.make_async_copy(key_ref, key_hbm.at[:, columns], sems.at[0])
    key_out.start()
    value_ref[...] = jnp.where(swapped, own, recv)
    value_out = pltpu.make_async_copy(value_ref, value_hbm.at[:, columns], sems.at[1])
    value_out.start()
    key_out.wait()
    value_out.wait()


def small(kernel, name, scalars, arrays, outs, after, alias_in=(), out_specs=None, scratch=()):
    vmem = pl.BlockSpec(memory_space=pltpu.VMEM)
    extra = list(alias_in) + list(after)
    first = len(scalars) + len(arrays)
    return pl.pallas_call(
        kernel,
        out_shape=outs,
        in_specs=[pl.BlockSpec(memory_space=pltpu.SMEM)] * len(scalars)
        + [vmem] * len(arrays)
        + [hbm_spec()] * len(alias_in)
        + [any_spec()] * len(after),
        out_specs=out_specs or [vmem] * len(outs),
        scratch_shapes=list(scratch),
        input_output_aliases={first + i: i for i in range(len(alias_in))},
        compiler_params=pltpu.CompilerParams(vmem_limit_bytes=SMALL_GRANT),
        cost_estimate=CHEAP,
        name=name,
    )(*scalars, *arrays, *extra)


class Sum:
    def __init__(self, order, choices, start, enc, width):
        self.choices, self.start, self.enc, self.width = choices, start, enc, width
        self.count = len(order)
        self.steps = list(order) + list(reversed(order))
        self.at = 0

    def begin(self, keep, send):
        self.keep = keep
        self.moving = swap(send, "dp", self.steps[0])

    def load(self, step):
        return self.enc >> (step if step < self.count else 2 * self.count - 1 - step)

    def advance(self, after, outs):
        count, at = self.count, self.at
        self.at += 1
        rows = self.load(at)
        shape = lambda rows, dtype: jax.ShapeDtypeStruct((rows, self.width), dtype)
        if at < count - 1:
            choice = self.choices[self.steps[at + 1]]
            self.keep, send = small(
                halve_kernel, "halve", [choice], [self.keep, self.moving],
                [shape(rows // 2, jnp.float32), shape(rows // 2, jnp.bfloat16)], after,
            )
        elif at == count - 1:
            (send,) = small(add_kernel, "add", [], [self.keep, self.moving], [shape(rows, jnp.bfloat16)], after)
        elif at < 2 * count - 1:
            choice = self.choices[self.steps[at]]
            (send,) = small(
                join_kernel, "join", [choice], [self.own, self.moving], [shape(2 * rows, jnp.bfloat16)], after
            )
        else:
            choice = self.choices[self.steps[at]]
            full = pltpu.HBM(self.full, jnp.float32)
            block = pltpu.VMEM((self.enc, self.width), jnp.float32)
            token = jax.ShapeDtypeStruct((8, 128), jnp.float32)
            *outs, done = small(
                functools.partial(place_kernel, self.start), "place", [choice], [self.own, self.moving],
                [full, full, token], after, alias_in=outs,
                out_specs=[hbm_spec()] * 2 + [pl.BlockSpec(memory_space=pltpu.VMEM)],
                scratch=[block, block, pltpu.SemaphoreType.DMA((2,))],
            )
            return done, outs
        self.own = send
        self.moving = swap(send, "dp", self.steps[at + 1])
        return send, outs


def wavefront(chunks, steps, rest):
    order, done = [], [0] * chunks

    def step(j):
        order.append(f"sum{j}")
        done[j] += 1

    for j in range(chunks):
        order.append(f"heads{j}")
        for earlier in range(j):
            if done[earlier] < steps - 1:
                step(earlier)
    order.append("state")
    for j in [0] + list(range(chunks - 1, 0, -1)):
        step(j)
    period, left, launched = 0, rest, False
    while min(done) < steps or left:
        turn = list(done)
        for j in [chunks - 1, *range(chunks - 1)]:
            if turn[j] < steps - 1 - (j == chunks - 1):
                step(j)
        if left > 1 and period != 1:
            order.append("rest")
            left -= 1
        for j in range(chunks):
            if turn[j] == steps - 1:
                step(j)
        if turn[-1] == steps - 2:
            step(chunks - 1)
        if left == 1 and not launched and done[-1] >= steps - 1:
            order.append("launch")
            launched = True
        if left == 1 and launched and min(done) == steps:
            order.append("rest")
            left = 0
        period += 1
    return order


def body(queries, states, key_weight, value_weight, nbr_shard, nbr_row, out_grad):
    shards = lax.axis_size("dp")
    groups = lax.axis_size("mp")
    dp_bits, mp_bits = bits_of(shards), bits_of(groups)
    dp_index = lax.axis_index("dp")
    spans, neighbours = nbr_shard.shape
    pair_count = spans * neighbours
    tokens, local_width = queries.shape
    stored, slab_len, enc_width = states.shape
    head_dim = D // H
    capacity = max(2, (pair_count + shards - 1) // shards)
    slot_count = shards * capacity

    owners = nbr_shard.reshape(pair_count)
    row_index = nbr_row.reshape(pair_count)
    pair_ids = jnp.arange(pair_count, dtype=jnp.int32)
    before = (owners[:, None] == owners[None, :]) & (pair_ids[None, :] < pair_ids[:, None])
    slot_index = owners * capacity + jnp.sum(before.astype(jnp.int32), axis=1)
    matched = slot_index[:, None] == jnp.arange(slot_count, dtype=jnp.int32)[None, :]
    asked = stored + jnp.sum(jnp.where(matched, row_index[:, None] - stored, 0), axis=0)
    slot_pair = jnp.sum(jnp.where(matched, pair_ids[:, None], 0), axis=0)
    incoming = lax.all_to_all(
        asked.reshape(shards, capacity), "dp", split_axis=0, concat_axis=0, tiled=True
    ).reshape(slot_count)
    slab_rows = jnp.take(states, jnp.minimum(incoming, stored - 1), axis=0, mode="clip")
    halves = 2
    piece = slab_len // halves
    came = []
    for h in range(halves):
        out = slab_rows[:, h * piece : (h + 1) * piece].reshape(shards, capacity, piece, enc_width)
        came.append(lax.all_to_all(out, "dp", split_axis=0, concat_axis=0, tiled=True))
    blocks = {}
    for h in range(halves):
        back = came[h].reshape(slot_count, piece, enc_width)
        picked = jnp.take(back, slot_index, axis=0, mode="clip").reshape(pair_count * piece, enc_width)
        blocks[0, h] = picked
        for bit in reversed(range(mp_bits)):
            for r in [r for r, k in blocks if k == h]:
                blocks[r | (1 << bit), h] = swap(blocks[r, h], "mp", bit)
    slabs = [blocks[r, h] for r in range(groups) for h in range(halves)]

    heads = local_width // head_dim
    counts = [min(2, heads - first) for first in range(0, heads, 2)]
    bits = list(range(dp_bits))
    choices = [((dp_index >> bit) & 1).astype(jnp.int32).reshape(1) for bit in bits]
    sums = []
    for j, count in enumerate(counts):
        sums.append(Sum(bits, choices, sum(counts[:j]) * head_dim, enc_width, count * head_dim))
        sums[j].full = key_weight.shape

    after, chain, outs, dk, dv = [], [], [], [], []
    rest_bit, pending, held_for = 0, None, 0
    for name in wavefront(len(sums), len(sums[0].steps), mp_bits + 1):
        kind = name.rstrip("0123456789")
        number = int(name[len(kind) :] or 0)
        if kind == "heads":
            part = sums[number]
            chain, dk_part, dv_part, (keep, send) = run_heads(
                part.start, part.width, choices[0], slabs, key_weight, value_weight, queries, out_grad,
                chain, after, spans, head_dim,
            )
            dk.append(dk_part)
            dv.append(dv_part)
            part.begin(keep, send)
            after = [send]
        elif kind == "sum":
            done, outs = sums[number].advance(after, outs)
            after = [done]
            held_for -= 1
            if pending is not None and not held_for:
                pending, _ = lax.optimization_barrier((pending, done))
                moving, pending = swap(pending, "mp", 0), None
        elif kind == "state":
            keep, send = run_state(groups, dk, dv, key_weight, value_weight, after)
            pending, after, held_for = send, [send], len(sums)
        elif kind == "launch":
            outgoing, _ = lax.optimization_barrier((outgoing, after))
            returned = lax.all_to_all(outgoing, "dp", split_axis=0, concat_axis=0, tiled=True)
        elif rest_bit < mp_bits - 1:
            half = keep.shape[0] // 2
            keep, send = small(
                split_kernel, "split", [], [keep, moving],
                [jax.ShapeDtypeStruct((half, enc_width), t) for t in (jnp.float32, jnp.bfloat16)], after,
            )
            moving = swap(send, "mp", mp_bits - 1 - rest_bit)
            after = [send]
            rest_bit += 1
        elif rest_bit == mp_bits - 1:
            (pair_grad,) = small(
                functools.partial(order_kernel, halves, pair_count), "add", [], [keep, moving],
                [jax.ShapeDtypeStruct(keep.shape, jnp.bfloat16)], after,
            )
            after = [pair_grad]
            outgoing = jnp.take(
                pair_grad.reshape(pair_count, slab_len, enc_width), slot_pair, axis=0, mode="clip"
            ).reshape(shards, capacity, slab_len, enc_width)
            after = [outgoing]
            rest_bit += 1
        else:
            (state_total,) = small(
                fold_kernel, "fold", [incoming], [returned.reshape(slot_count, slab_len, enc_width)],
                [pltpu.HBM(states.shape, jnp.float32)], after, out_specs=[hbm_spec()],
                scratch=[pltpu.VMEM(states.shape, jnp.float32), pltpu.SemaphoreType.DMA],
            )
    return (chain[0], chain[1], state_total, outs[0], outs[1])


def solution(mesh):
    placed = (
        P("dp", "mp"),
        P("dp", "mp", None),
        P(None, "mp"),
        P(None, "mp"),
        P("dp", None),
        P("dp", None),
        P("dp", "mp"),
    )
    return jax.shard_map(
        body,
        mesh=mesh,
        in_specs=placed,
        out_specs=(P("dp", "mp"), P("dp", "mp"), P("dp", "mp", None), P(None, "mp"), P(None, "mp")),
        check_vma=False,
    )
```

```python
import functools

import jax
import jax.numpy as jnp
from jax import lax
from jax.experimental import pallas as pl
from jax.experimental.pallas import tpu as pltpu
from jax.sharding import PartitionSpec as P

D = 4096
H = 32
VMEM_GRANT = 28 * 1024 * 1024
SMALL_GRANT = 12 * 1024 * 1024
CHEAP = pl.CostEstimate(flops=1, bytes_accessed=1, transcendentals=0)


def bits_of(count):
    return count.bit_length() - 1


def swap(value, axis, bit):
    count = lax.axis_size(axis)
    return lax.ppermute(value, axis, [(i, i ^ (1 << bit)) for i in range(count)])


def any_spec():
    return pl.BlockSpec(memory_space=pl.ANY)


def in_hbm(arrays):
    return [pltpu.with_memory_space_constraint(x, pltpu.HBM) for x in arrays]


def hbm_spec():
    return pl.BlockSpec(memory_space=pltpu.HBM)


def head_kernel(groups, spans, head_dim, start, extra, *refs):
    flag_ref = refs[0]
    slabs = refs[1 : 1 + groups]
    wk_hbm, wv_hbm, q_hbm, g_hbm = refs[1 + groups : 5 + groups]
    att_hbm, dq_hbm, dk_hbm, dv_hbm, keep_ref, send_ref = refs[5 + groups + extra : 11 + groups + extra]
    rows, wk, wv, q_ref, g_ref, keys, values, att_ref, dq_ref, dk_ref, dv_ref, grads, sems = refs[11 + groups + extra :]
    tokens, width = q_ref.shape
    span_len = tokens // spans
    block = rows.shape[0] // groups
    part = block // spans
    scale = 1.0 / head_dim**0.5
    columns = pl.ds(start, width)

    def begin(source, target, sem):
        copy = pltpu.make_async_copy(source, target, sems.at[sem])
        copy.start()
        return copy

    weights_in = [begin(wk_hbm.at[:, columns], wk, groups), begin(wv_hbm.at[:, columns], wv, groups + 1)]
    rows_in = [begin(slabs[r], rows.at[pl.ds(r * block, block)], r) for r in range(groups)]
    tokens_in = [begin(q_hbm.at[:, columns], q_ref, groups + 2), begin(g_hbm.at[:, columns], g_ref, groups + 3)]
    for copy in weights_in:
        copy.wait()
    for r in range(0, groups, 2):
        rows_in[r].wait()
        rows_in[r + 1].wait()
        at = pl.ds(r * block, 2 * block)
        keys[at, :] = jnp.dot(rows[at, :], wk[...], preferred_element_type=jnp.float32).astype(jnp.bfloat16)
        values[at, :] = jnp.dot(rows[at, :], wv[...], preferred_element_type=jnp.float32).astype(jnp.bfloat16)
    for copy in tokens_in:
        copy.wait()

    def spread(x):
        heads = x.shape[1] // head_dim
        lane_head = lax.broadcasted_iota(jnp.int32, x.shape, 1) // head_dim
        zero = jnp.zeros_like(x)
        return jnp.concatenate([jnp.where(lane_head == h, x, zero) for h in range(heads)], axis=0)

    def collect(x):
        out = x[0:span_len]
        lane_head = lax.broadcasted_iota(jnp.int32, out.shape, 1) // head_dim
        for h in range(1, x.shape[1] // head_dim):
            out = jnp.where(lane_head == h, x[h * span_len : (h + 1) * span_len], out)
        return out

    def span_rows(ref, c, cols):
        return jnp.concatenate([ref[pl.ds(r * block + c * part, part), cols] for r in range(groups)], axis=0)

    contract_last = (((1,), (1,)), ((), ()))
    contract_first = (((0,), (0,)), ((), ()))
    at = [pl.ds(c * span_len, span_len) for c in range(spans)]
    swapped = flag_ref[0] == 1
    pair = 2 * head_dim
    for first in range(0, width, pair):
        cols = slice(first, min(first + pair, width))
        send_cols = slice(width + cols.start, width + cols.stop)
        every = range(spans)
        scores = [
            lax.dot_general(
                span_rows(keys, c, cols), spread(q_ref[at[c], cols]), contract_last,
                preferred_element_type=jnp.float32,
            )
            * scale
            for c in every
        ]
        prob_grad = [
            lax.dot_general(
                span_rows(values, c, cols), spread(g_ref[at[c], cols]), contract_last,
                preferred_element_type=jnp.float32,
            )
            for c in every
        ]
        weights = [jnp.exp(x - jnp.max(x, axis=0, keepdims=True)) for x in scores]
        probs = [x * (1.0 / jnp.sum(x, axis=0, keepdims=True)) for x in weights]
        low = [x.astype(jnp.bfloat16) for x in probs]
        row_dot = [jnp.sum(p * d, axis=0, keepdims=True) for p, d in zip(probs, prob_grad)]
        score_grad = [(scale * p * (d - t)).astype(jnp.bfloat16) for p, d, t in zip(probs, prob_grad, row_dot)]
        for c in every:
            dk = jnp.dot(score_grad[c], spread(q_ref[at[c], cols]), preferred_element_type=jnp.float32)
            dv = jnp.dot(low[c], spread(g_ref[at[c], cols]), preferred_element_type=jnp.float32)
            dk, dv = dk.astype(jnp.bfloat16), dv.astype(jnp.bfloat16)
            for r in range(groups):
                to = pl.ds(r * block + c * part, part)
                piece = slice(r * part, (r + 1) * part)
                dk_ref[to, cols] = dk[piece]
                dv_ref[to, cols] = dv[piece]
                grads[to, cols] = jnp.where(swapped, dv[piece], dk[piece])
                grads[to, send_cols] = jnp.where(swapped, dk[piece], dv[piece])
        for c in every:
            att = lax.dot_general(
                low[c], span_rows(values, c, cols), contract_first, preferred_element_type=jnp.float32
            )
            att_ref[at[c], cols] = collect(att).astype(jnp.bfloat16)
            dq = lax.dot_general(
                score_grad[c], span_rows(keys, c, cols), contract_first, preferred_element_type=jnp.float32
            )
            dq_ref[at[c], cols] = collect(dq).astype(jnp.bfloat16)
    results = [
        begin(att_ref, att_hbm.at[:, columns], 0),
        begin(dq_ref, dq_hbm.at[:, columns], 1),
        begin(dk_ref, dk_hbm, 2),
        begin(dv_ref, dv_hbm, 3),
    ]
    tile = 128
    for first in range(0, rows.shape[1], tile):
        to = slice(first, first + tile)
        both = lax.dot_general(rows[:, to], grads[...], contract_first, preferred_element_type=jnp.float32)
        keep_ref[to, :] = both[:, :width]
        send_ref[to, :] = both[:, width:].astype(jnp.bfloat16)
    for copy in results:
        copy.wait()


def run_heads(start, chunk, flag, slabs, key_weight, value_weight, queries, out_grad, chain, after, spans, head_dim):
    groups = len(slabs)
    tokens, local_width = queries.shape
    block, enc = slabs[0].shape
    total = groups * block
    bf = jnp.bfloat16
    extra = list(chain) + list(after)
    outs = pl.pallas_call(
        functools.partial(head_kernel, groups, spans, head_dim, start, len(extra)),
        out_shape=[
            pltpu.HBM((tokens, local_width), bf),
            pltpu.HBM((tokens, local_width), bf),
            pltpu.HBM((total, chunk), bf),
            pltpu.HBM((total, chunk), bf),
            jax.ShapeDtypeStruct((enc, chunk), jnp.float32),
            jax.ShapeDtypeStruct((enc, chunk), bf),
        ],
        in_specs=[pl.BlockSpec(memory_space=pltpu.SMEM)]
        + [any_spec()] * groups
        + [hbm_spec()] * (4 + len(chain))
        + [any_spec()] * len(after),
        out_specs=[hbm_spec()] * 4 + [pl.BlockSpec(memory_space=pltpu.VMEM)] * 2,
        scratch_shapes=[
            pltpu.VMEM((total, enc), bf),
            pltpu.VMEM((enc, chunk), bf),
            pltpu.VMEM((enc, chunk), bf),
            pltpu.VMEM((tokens, chunk), bf),
            pltpu.VMEM((tokens, chunk), bf),
            pltpu.VMEM((total, chunk), bf),
            pltpu.VMEM((total, chunk), bf),
            pltpu.VMEM((tokens, chunk), bf),
            pltpu.VMEM((tokens, chunk), bf),
            pltpu.VMEM((total, chunk), bf),
            pltpu.VMEM((total, chunk), bf),
            pltpu.VMEM((total, 2 * chunk), bf),
            pltpu.SemaphoreType.DMA((groups + 4,)),
        ],
        input_output_aliases={5 + groups + i: i for i in range(len(chain))},
        compiler_params=pltpu.CompilerParams(vmem_limit_bytes=VMEM_GRANT),
        cost_estimate=pl.CostEstimate(
            flops=2 * total * enc * chunk * 8, bytes_accessed=4 * total * enc, transcendentals=total * tokens
        ),
        name="heads",
    )(flag, *slabs, *in_hbm([key_weight, value_weight, queries, out_grad, *chain]), *after)
    return outs[:2], outs[2], outs[3], outs[4:]


def state_kernel(groups, widths, extra, *refs):
    count = len(widths)
    dk_hbm, dv_hbm = refs[:count], refs[count : 2 * count]
    wk_hbm, wv_hbm = refs[2 * count : 2 * count + 2]
    keep_ref, send_ref, grads, weights, sems = refs[2 * count + 2 + extra :]
    half = weights.shape[1] // 2
    block = grads.shape[0] // groups

    copies = [
        pltpu.make_async_copy(wk_hbm, weights.at[:, pl.ds(0, half)], sems.at[0, 0]),
        pltpu.make_async_copy(wv_hbm, weights.at[:, pl.ds(half, half)], sems.at[0, 1]),
    ]
    blocks = []
    for r in range(groups):
        rows = pl.ds(r * block, block)
        parts = []
        for j in range(count):
            first = sum(widths[:j])
            for k, source in enumerate((dk_hbm[j], dv_hbm[j])):
                target = grads.at[rows, pl.ds(k * half + first, widths[j])]
                parts.append(pltpu.make_async_copy(source.at[rows, :], target, sems.at[1 + r, 2 * j + k]))
        blocks.append(parts)
    for copy in copies:
        copy.start()
    for parts in blocks:
        for copy in parts:
            copy.start()
    for copy in copies:
        copy.wait()
    for r in range(groups):
        for copy in blocks[r]:
            copy.wait()
        to = pl.ds((r // 2) * block, block)
        for first in range(0, weights.shape[0], 256):
            cols = slice(first, min(first + 256, weights.shape[0]))
            term = lax.dot_general(
                grads[pl.ds(r * block, block), :], weights[cols, :], (((1,), (1,)), ((), ())),
                preferred_element_type=jnp.float32,
            )
            (send_ref if r % 2 else keep_ref)[to, cols] = term.astype(jnp.bfloat16)


def run_state(groups, dk, dv, key_weight, value_weight, after):
    total = dk[0].shape[0]
    enc, local_width = key_weight.shape
    widths = [x.shape[1] for x in dk]
    vmem = pl.BlockSpec(memory_space=pltpu.VMEM)
    return pl.pallas_call(
        functools.partial(state_kernel, groups, widths, len(after)),
        out_shape=[
            jax.ShapeDtypeStruct((total // 2, enc), jnp.bfloat16),
            jax.ShapeDtypeStruct((total // 2, enc), jnp.bfloat16),
        ],
        in_specs=[hbm_spec()] * (2 * len(dk) + 2) + [any_spec()] * len(after),
        out_specs=[vmem, vmem],
        scratch_shapes=[
            pltpu.VMEM((total, 2 * local_width), jnp.bfloat16),
            pltpu.VMEM((enc, 2 * local_width), jnp.bfloat16),
            pltpu.SemaphoreType.DMA((groups + 1, max(2, 2 * len(dk)))),
        ],
        compiler_params=pltpu.CompilerParams(vmem_limit_bytes=VMEM_GRANT),
        cost_estimate=pl.CostEstimate(
            flops=8 * total * enc * local_width, bytes_accessed=8 * total * enc, transcendentals=0
        ),
        name="state_terms",
    )(*in_hbm([*dk, *dv, key_weight, value_weight]), *after)


def fold_kernel(rows_ref, returned_ref, *refs):
    out_hbm, out_ref, sem = refs[-3:]
    out_ref[...] = jnp.zeros_like(out_ref)
    count = out_ref.shape[0]
    for s in range(returned_ref.shape[0]):
        row = rows_ref[s]

        @pl.when(row < count)
        def _():
            out_ref[row] += returned_ref[s].astype(jnp.float32)

    copy = pltpu.make_async_copy(out_ref, out_hbm, sem)
    copy.start()
    copy.wait()


def halve_kernel(choice_ref, keep_ref, recv_ref, *refs):
    stay_ref, send_ref = refs[-2:]
    total = keep_ref[...] + recv_ref[...].astype(jnp.float32)
    half = stay_ref.shape[0]
    upper = choice_ref[0] == 1
    stay_ref[...] = jnp.where(upper, total[half:], total[:half])
    send_ref[...] = jnp.where(upper, total[:half], total[half:]).astype(jnp.bfloat16)


def split_kernel(keep_ref, recv_ref, *refs):
    stay_ref, send_ref = refs[-2:]
    half = stay_ref.shape[0]
    total = keep_ref[...].astype(jnp.float32) + recv_ref[...].astype(jnp.float32)
    stay_ref[...] = total[:half]
    send_ref[...] = total[half:].astype(jnp.bfloat16)


def add_kernel(keep_ref, recv_ref, *refs):
    total = keep_ref[...].astype(jnp.float32) + recv_ref[...].astype(jnp.float32)
    refs[-1][...] = total.astype(refs[-1].dtype)


def order_kernel(halves, pairs, keep_ref, recv_ref, *refs):
    total = keep_ref[...].astype(jnp.float32) + recv_ref[...].astype(jnp.float32)
    piece = total.shape[0] // (halves * pairs)
    parts = [total[(h * pairs + p) * piece :][:piece] for p in range(pairs) for h in range(halves)]
    refs[-1][...] = jnp.concatenate(parts, axis=0).astype(refs[-1].dtype)


def join_kernel(choice_ref, own_ref, recv_ref, *refs):
    out_ref = refs[-1]
    upper = choice_ref[0] == 1
    own, recv = own_ref[...], recv_ref[...]
    rows = own.shape[0]
    if rows % 16:
        own, recv = own.astype(jnp.float32), recv.astype(jnp.float32)
        out = jnp.concatenate([jnp.where(upper, recv, own), jnp.where(upper, own, recv)], axis=0)
        out_ref[...] = out.astype(out_ref.dtype)
    else:
        out_ref[:rows] = jnp.where(upper, recv, own)
        out_ref[rows:] = jnp.where(upper, own, recv)


def place_kernel(start, choice_ref, own_ref, recv_ref, *refs):
    key_hbm, value_hbm, token_ref, key_ref, value_ref, sems = refs[-6:]
    token_ref[...] = jnp.zeros_like(token_ref)
    swapped = choice_ref[0] == 1
    own, recv = own_ref[...].astype(jnp.float32), recv_ref[...].astype(jnp.float32)
    columns = pl.ds(start, own.shape[1])
    key_ref[...] = jnp.where(swapped, recv, own)
    key_out = pltpu.make_async_copy(key_ref, key_hbm.at[:, columns], sems.at[0])
    key_out.start()
    value_ref[...] = jnp.where(swapped, own, recv)
    value_out = pltpu.make_async_copy(value_ref, value_hbm.at[:, columns], sems.at[1])
    value_out.start()
    key_out.wait()
    value_out.wait()


def small(kernel, name, scalars, arrays, outs, after, alias_in=(), out_specs=None, scratch=()):
    vmem = pl.BlockSpec(memory_space=pltpu.VMEM)
    extra = list(alias_in) + list(after)
    first = len(scalars) + len(arrays)
    return pl.pallas_call(
        kernel,
        out_shape=outs,
        in_specs=[pl.BlockSpec(memory_space=pltpu.SMEM)] * len(scalars)
        + [vmem] * len(arrays)
        + [hbm_spec()] * len(alias_in)
        + [any_spec()] * len(after),
        out_specs=out_specs or [vmem] * len(outs),
        scratch_shapes=list(scratch),
        input_output_aliases={first + i: i for i in range(len(alias_in))},
        compiler_params=pltpu.CompilerParams(vmem_limit_bytes=SMALL_GRANT),
        cost_estimate=CHEAP,
        name=name,
    )(*scalars, *arrays, *extra)


class Sum:
    def __init__(self, order, choices, start, enc, width):
        self.choices, self.start, self.enc, self.width = choices, start, enc, width
        self.count = len(order)
        self.steps = list(order) + list(reversed(order))
        self.at = 0

    def begin(self, keep, send):
        self.keep = keep
        self.moving = swap(send, "dp", self.steps[0])

    def load(self, step):
        return self.enc >> (step if step < self.count else 2 * self.count - 1 - step)

    def advance(self, after, outs):
        count, at = self.count, self.at
        self.at += 1
        rows = self.load(at)
        shape = lambda rows, dtype: jax.ShapeDtypeStruct((rows, self.width), dtype)
        if at < count - 1:
            choice = self.choices[self.steps[at + 1]]
            self.keep, send = small(
                halve_kernel, "halve", [choice], [self.keep, self.moving],
                [shape(rows // 2, jnp.float32), shape(rows // 2, jnp.bfloat16)], after,
            )
        elif at == count - 1:
            (send,) = small(add_kernel, "add", [], [self.keep, self.moving], [shape(rows, jnp.bfloat16)], after)
        elif at < 2 * count - 1:
            choice = self.choices[self.steps[at]]
            (send,) = small(
                join_kernel, "join", [choice], [self.own, self.moving], [shape(2 * rows, jnp.bfloat16)], after
            )
        else:
            choice = self.choices[self.steps[at]]
            full = pltpu.HBM(self.full, jnp.float32)
            block = pltpu.VMEM((self.enc, self.width), jnp.float32)
            token = jax.ShapeDtypeStruct((8, 128), jnp.float32)
            *outs, done = small(
                functools.partial(place_kernel, self.start), "place", [choice], [self.own, self.moving],
                [full, full, token], after, alias_in=outs,
                out_specs=[hbm_spec()] * 2 + [pl.BlockSpec(memory_space=pltpu.VMEM)],
                scratch=[block, block, pltpu.SemaphoreType.DMA((2,))],
            )
            return done, outs
        self.own = send
        self.moving = swap(send, "dp", self.steps[at + 1])
        return send, outs


def wavefront(chunks, steps, rest):
    order, done = [], [0] * chunks

    def step(j):
        order.append(f"sum{j}")
        done[j] += 1

    for j in range(chunks):
        order.append(f"heads{j}")
        for earlier in range(j):
            if done[earlier] < steps - 1:
                step(earlier)
    order.append("state")
    for j in [0] + list(range(chunks - 1, 0, -1)):
        step(j)
    period, left, launched = 0, rest, False
    while min(done) < steps or left:
        turn = list(done)
        for j in range(chunks):
            if turn[j] < steps - 1 - (j == chunks - 1):
                step(j)
        if left > 1 and period != 1:
            order.append("rest")
            left -= 1
        for j in range(chunks):
            if turn[j] == steps - 1:
                step(j)
        if turn[-1] == steps - 2:
            step(chunks - 1)
        if left == 1 and not launched and done[-1] >= steps - 1:
            order.append("launch")
            launched = True
        if left == 1 and launched and min(done) == steps:
            order.append("rest")
            left = 0
        period += 1
    return order


def body(queries, states, key_weight, value_weight, nbr_shard, nbr_row, out_grad):
    shards = lax.axis_size("dp")
    groups = lax.axis_size("mp")
    dp_bits, mp_bits = bits_of(shards), bits_of(groups)
    dp_index = lax.axis_index("dp")
    spans, neighbours = nbr_shard.shape
    pair_count = spans * neighbours
    tokens, local_width = queries.shape
    stored, slab_len, enc_width = states.shape
    head_dim = D // H
    capacity = max(2, (pair_count + shards - 1) // shards)
    slot_count = shards * capacity

    owners = nbr_shard.reshape(pair_count)
    row_index = nbr_row.reshape(pair_count)
    pair_ids = jnp.arange(pair_count, dtype=jnp.int32)
    before = (owners[:, None] == owners[None, :]) & (pair_ids[None, :] < pair_ids[:, None])
    slot_index = owners * capacity + jnp.sum(before.astype(jnp.int32), axis=1)
    matched = slot_index[:, None] == jnp.arange(slot_count, dtype=jnp.int32)[None, :]
    asked = stored + jnp.sum(jnp.where(matched, row_index[:, None] - stored, 0), axis=0)
    slot_pair = jnp.sum(jnp.where(matched, pair_ids[:, None], 0), axis=0)
    incoming = lax.all_to_all(
        asked.reshape(shards, capacity), "dp", split_axis=0, concat_axis=0, tiled=True
    ).reshape(slot_count)
    slab_rows = jnp.take(states, jnp.minimum(incoming, stored - 1), axis=0, mode="clip")
    halves = 2
    piece = slab_len // halves
    came = []
    for h in range(halves):
        out = slab_rows[:, h * piece : (h + 1) * piece].reshape(shards, capacity, piece, enc_width)
        came.append(lax.all_to_all(out, "dp", split_axis=0, concat_axis=0, tiled=True))
    blocks = {}
    for h in range(halves):
        if h:
            first = (1 << (mp_bits - 1), h - 1)
            came[h], blocks[first] = lax.optimization_barrier((came[h], blocks[first]))
        back = came[h].reshape(slot_count, piece, enc_width)
        picked = jnp.take(back, slot_index, axis=0, mode="clip").reshape(pair_count * piece, enc_width)
        blocks[0, h] = picked
        for bit in reversed(range(mp_bits)):
            for r in [r for r, k in blocks if k == h]:
                blocks[r | (1 << bit), h] = swap(blocks[r, h], "mp", bit)
    slabs = [blocks[r, h] for r in range(groups) for h in range(halves)]

    heads = local_width // head_dim
    counts = [min(2, heads - first) for first in range(0, heads, 2)]
    bits = list(range(dp_bits))
    choices = [((dp_index >> bit) & 1).astype(jnp.int32).reshape(1) for bit in bits]
    sums = []
    for j, count in enumerate(counts):
        sums.append(Sum(bits, choices, sum(counts[:j]) * head_dim, enc_width, count * head_dim))
        sums[j].full = key_weight.shape

    after, chain, outs, dk, dv = [], [], [], [], []
    rest_bit, pending, held_for = 0, None, 0
    for name in wavefront(len(sums), len(sums[0].steps), mp_bits + 1):
        kind = name.rstrip("0123456789")
        number = int(name[len(kind) :] or 0)
        if kind == "heads":
            part = sums[number]
            chain, dk_part, dv_part, (keep, send) = run_heads(
                part.start, part.width, choices[0], slabs, key_weight, value_weight, queries, out_grad,
                chain, after, spans, head_dim,
            )
            dk.append(dk_part)
            dv.append(dv_part)
            part.begin(keep, send)
            after = [send]
        elif kind == "sum":
            done, outs = sums[number].advance(after, outs)
            after = [done]
            held_for -= 1
            if pending is not None and not held_for:
                pending, _ = lax.optimization_barrier((pending, done))
                moving, pending = swap(pending, "mp", 0), None
        elif kind == "state":
            keep, send = run_state(groups, dk, dv, key_weight, value_weight, after)
            pending, after, held_for = send, [send], len(sums)
        elif kind == "launch":
            outgoing, _ = lax.optimization_barrier((outgoing, after))
            returned = lax.all_to_all(outgoing, "dp", split_axis=0, concat_axis=0, tiled=True)
        elif rest_bit < mp_bits - 1:
            half = keep.shape[0] // 2
            keep, send = small(
                split_kernel, "split", [], [keep, moving],
                [jax.ShapeDtypeStruct((half, enc_width), t) for t in (jnp.float32, jnp.bfloat16)], after,
            )
            moving = swap(send, "mp", mp_bits - 1 - rest_bit)
            after = [send]
            rest_bit += 1
        elif rest_bit == mp_bits - 1:
            (pair_grad,) = small(
                functools.partial(order_kernel, halves, pair_count), "add", [], [keep, moving],
                [jax.ShapeDtypeStruct(keep.shape, jnp.bfloat16)], after,
            )
            after = [pair_grad]
            outgoing = jnp.take(
                pair_grad.reshape(pair_count, slab_len, enc_width), slot_pair, axis=0, mode="clip"
            ).reshape(shards, capacity, slab_len, enc_width)
            after = [outgoing]
            rest_bit += 1
        else:
            (state_total,) = small(
                fold_kernel, "fold", [incoming], [returned.reshape(slot_count, slab_len, enc_width)],
                [pltpu.HBM(states.shape, jnp.float32)], after, out_specs=[hbm_spec()],
                scratch=[pltpu.VMEM(states.shape, jnp.float32), pltpu.SemaphoreType.DMA],
            )
    return (chain[0], chain[1], state_total, outs[0], outs[1])


def solution(mesh):
    placed = (
        P("dp", "mp"),
        P("dp", "mp", None),
        P(None, "mp"),
        P(None, "mp"),
        P("dp", None),
        P("dp", None),
        P("dp", "mp"),
    )
    return jax.shard_map(
        body,
        mesh=mesh,
        in_specs=placed,
        out_specs=(P("dp", "mp"), P("dp", "mp"), P("dp", "mp", None), P(None, "mp"), P(None, "mp")),
        check_vma=False,
    )
```

```python
import functools

import jax
import jax.numpy as jnp
from jax import lax
from jax.experimental import pallas as pl
from jax.experimental.pallas import tpu as pltpu
from jax.sharding import PartitionSpec as P

D = 4096
H = 32
VMEM_GRANT = 28 * 1024 * 1024
SMALL_GRANT = 12 * 1024 * 1024
CHEAP = pl.CostEstimate(flops=1, bytes_accessed=1, transcendentals=0)


def bits_of(count):
    return count.bit_length() - 1


def swap(value, axis, bit):
    count = lax.axis_size(axis)
    return lax.ppermute(value, axis, [(i, i ^ (1 << bit)) for i in range(count)])


def any_spec():
    return pl.BlockSpec(memory_space=pl.ANY)


def in_hbm(arrays):
    return [pltpu.with_memory_space_constraint(x, pltpu.HBM) for x in arrays]


def hbm_spec():
    return pl.BlockSpec(memory_space=pltpu.HBM)


def head_kernel(groups, spans, head_dim, start, extra, *refs):
    flag_ref = refs[0]
    slabs = refs[1 : 1 + groups]
    wk_hbm, wv_hbm, q_hbm, g_hbm = refs[1 + groups : 5 + groups]
    att_hbm, dq_hbm, dk_hbm, dv_hbm, keep_ref, send_ref = refs[5 + groups + extra : 11 + groups + extra]
    rows, wk, wv, q_ref, g_ref, keys, values, att_ref, dq_ref, dk_ref, dv_ref, grads, sems = refs[11 + groups + extra :]
    tokens, width = q_ref.shape
    span_len = tokens // spans
    block = rows.shape[0] // groups
    part = block // spans
    scale = 1.0 / head_dim**0.5
    columns = pl.ds(start, width)

    def begin(source, target, sem):
        copy = pltpu.make_async_copy(source, target, sems.at[sem])
        copy.start()
        return copy

    weights_in = [begin(wk_hbm.at[:, columns], wk, groups), begin(wv_hbm.at[:, columns], wv, groups + 1)]
    rows_in = [begin(slabs[r], rows.at[pl.ds(r * block, block)], r) for r in range(groups)]
    tokens_in = [begin(q_hbm.at[:, columns], q_ref, groups + 2), begin(g_hbm.at[:, columns], g_ref, groups + 3)]
    for copy in weights_in:
        copy.wait()
    for r in range(0, groups, 2):
        rows_in[r].wait()
        rows_in[r + 1].wait()
        at = pl.ds(r * block, 2 * block)
        keys[at, :] = jnp.dot(rows[at, :], wk[...], preferred_element_type=jnp.float32).astype(jnp.bfloat16)
        values[at, :] = jnp.dot(rows[at, :], wv[...], preferred_element_type=jnp.float32).astype(jnp.bfloat16)
    for copy in tokens_in:
        copy.wait()

    def spread(x):
        heads = x.shape[1] // head_dim
        lane_head = lax.broadcasted_iota(jnp.int32, x.shape, 1) // head_dim
        zero = jnp.zeros_like(x)
        return jnp.concatenate([jnp.where(lane_head == h, x, zero) for h in range(heads)], axis=0)

    def collect(x):
        out = x[0:span_len]
        lane_head = lax.broadcasted_iota(jnp.int32, out.shape, 1) // head_dim
        for h in range(1, x.shape[1] // head_dim):
            out = jnp.where(lane_head == h, x[h * span_len : (h + 1) * span_len], out)
        return out

    def span_rows(ref, c, cols):
        return jnp.concatenate([ref[pl.ds(r * block + c * part, part), cols] for r in range(groups)], axis=0)

    contract_last = (((1,), (1,)), ((), ()))
    contract_first = (((0,), (0,)), ((), ()))
    at = [pl.ds(c * span_len, span_len) for c in range(spans)]
    swapped = flag_ref[0] == 1
    pair = 2 * head_dim
    for first in range(0, width, pair):
        cols = slice(first, min(first + pair, width))
        send_cols = slice(width + cols.start, width + cols.stop)
        every = range(spans)
        scores = [
            lax.dot_general(
                span_rows(keys, c, cols), spread(q_ref[at[c], cols]), contract_last,
                preferred_element_type=jnp.float32,
            )
            * scale
            for c in every
        ]
        prob_grad = [
            lax.dot_general(
                span_rows(values, c, cols), spread(g_ref[at[c], cols]), contract_last,
                preferred_element_type=jnp.float32,
            )
            for c in every
        ]
        weights = [jnp.exp(x - jnp.max(x, axis=0, keepdims=True)) for x in scores]
        probs = [x * (1.0 / jnp.sum(x, axis=0, keepdims=True)) for x in weights]
        low = [x.astype(jnp.bfloat16) for x in probs]
        row_dot = [jnp.sum(p * d, axis=0, keepdims=True) for p, d in zip(probs, prob_grad)]
        score_grad = [(scale * p * (d - t)).astype(jnp.bfloat16) for p, d, t in zip(probs, prob_grad, row_dot)]
        for c in every:
            dk = jnp.dot(score_grad[c], spread(q_ref[at[c], cols]), preferred_element_type=jnp.float32)
            dv = jnp.dot(low[c], spread(g_ref[at[c], cols]), preferred_element_type=jnp.float32)
            dk, dv = dk.astype(jnp.bfloat16), dv.astype(jnp.bfloat16)
            for r in range(groups):
                to = pl.ds(r * block + c * part, part)
                piece = slice(r * part, (r + 1) * part)
                dk_ref[to, cols] = dk[piece]
                dv_ref[to, cols] = dv[piece]
                grads[to, cols] = jnp.where(swapped, dv[piece], dk[piece])
                grads[to, send_cols] = jnp.where(swapped, dk[piece], dv[piece])
        for c in every:
            att = lax.dot_general(
                low[c], span_rows(values, c, cols), contract_first, preferred_element_type=jnp.float32
            )
            att_ref[at[c], cols] = collect(att).astype(jnp.bfloat16)
            dq = lax.dot_general(
                score_grad[c], span_rows(keys, c, cols), contract_first, preferred_element_type=jnp.float32
            )
            dq_ref[at[c], cols] = collect(dq).astype(jnp.bfloat16)
    results = [
        begin(att_ref, att_hbm.at[:, columns], 0),
        begin(dq_ref, dq_hbm.at[:, columns], 1),
        begin(dk_ref, dk_hbm, 2),
        begin(dv_ref, dv_hbm, 3),
    ]
    tile = 128
    for first in range(0, rows.shape[1], tile):
        to = slice(first, first + tile)
        both = lax.dot_general(rows[:, to], grads[...], contract_first, preferred_element_type=jnp.float32)
        keep_ref[to, :] = both[:, :width]
        send_ref[to, :] = both[:, width:].astype(jnp.bfloat16)
    for copy in results:
        copy.wait()


def run_heads(start, chunk, flag, slabs, key_weight, value_weight, queries, out_grad, chain, after, spans, head_dim):
    groups = len(slabs)
    tokens, local_width = queries.shape
    block, enc = slabs[0].shape
    total = groups * block
    bf = jnp.bfloat16
    extra = list(chain) + list(after)
    outs = pl.pallas_call(
        functools.partial(head_kernel, groups, spans, head_dim, start, len(extra)),
        out_shape=[
            pltpu.HBM((tokens, local_width), bf),
            pltpu.HBM((tokens, local_width), bf),
            pltpu.HBM((total, chunk), bf),
            pltpu.HBM((total, chunk), bf),
            jax.ShapeDtypeStruct((enc, chunk), jnp.float32),
            jax.ShapeDtypeStruct((enc, chunk), bf),
        ],
        in_specs=[pl.BlockSpec(memory_space=pltpu.SMEM)]
        + [any_spec()] * groups
        + [hbm_spec()] * (4 + len(chain))
        + [any_spec()] * len(after),
        out_specs=[hbm_spec()] * 4 + [pl.BlockSpec(memory_space=pltpu.VMEM)] * 2,
        scratch_shapes=[
            pltpu.VMEM((total, enc), bf),
            pltpu.VMEM((enc, chunk), bf),
            pltpu.VMEM((enc, chunk), bf),
            pltpu.VMEM((tokens, chunk), bf),
            pltpu.VMEM((tokens, chunk), bf),
            pltpu.VMEM((total, chunk), bf),
            pltpu.VMEM((total, chunk), bf),
            pltpu.VMEM((tokens, chunk), bf),
            pltpu.VMEM((tokens, chunk), bf),
            pltpu.VMEM((total, chunk), bf),
            pltpu.VMEM((total, chunk), bf),
            pltpu.VMEM((total, 2 * chunk), bf),
            pltpu.SemaphoreType.DMA((groups + 4,)),
        ],
        input_output_aliases={5 + groups + i: i for i in range(len(chain))},
        compiler_params=pltpu.CompilerParams(vmem_limit_bytes=VMEM_GRANT),
        cost_estimate=pl.CostEstimate(
            flops=2 * total * enc * chunk * 8, bytes_accessed=4 * total * enc, transcendentals=total * tokens
        ),
        name="heads",
    )(flag, *slabs, *in_hbm([key_weight, value_weight, queries, out_grad, *chain]), *after)
    return outs[:2], outs[2], outs[3], outs[4:]


def state_kernel(groups, widths, extra, *refs):
    count = len(widths)
    dk_hbm, dv_hbm = refs[:count], refs[count : 2 * count]
    wk_hbm, wv_hbm = refs[2 * count : 2 * count + 2]
    keep_ref, send_ref, grads, weights, sems = refs[2 * count + 2 + extra :]
    half = weights.shape[1] // 2
    block = grads.shape[0] // groups

    copies = [
        pltpu.make_async_copy(wk_hbm, weights.at[:, pl.ds(0, half)], sems.at[0, 0]),
        pltpu.make_async_copy(wv_hbm, weights.at[:, pl.ds(half, half)], sems.at[0, 1]),
    ]
    blocks = []
    for r in range(groups):
        rows = pl.ds(r * block, block)
        parts = []
        for j in range(count):
            first = sum(widths[:j])
            for k, source in enumerate((dk_hbm[j], dv_hbm[j])):
                target = grads.at[rows, pl.ds(k * half + first, widths[j])]
                parts.append(pltpu.make_async_copy(source.at[rows, :], target, sems.at[1 + r, 2 * j + k]))
        blocks.append(parts)
    for copy in copies:
        copy.start()
    for parts in blocks:
        for copy in parts:
            copy.start()
    for copy in copies:
        copy.wait()
    for r in range(groups):
        for copy in blocks[r]:
            copy.wait()
        to = pl.ds((r // 2) * block, block)
        for first in range(0, weights.shape[0], 256):
            cols = slice(first, min(first + 256, weights.shape[0]))
            term = lax.dot_general(
                grads[pl.ds(r * block, block), :], weights[cols, :], (((1,), (1,)), ((), ())),
                preferred_element_type=jnp.float32,
            )
            (send_ref if r % 2 else keep_ref)[to, cols] = term.astype(jnp.bfloat16)


def run_state(groups, dk, dv, key_weight, value_weight, after):
    total = dk[0].shape[0]
    enc, local_width = key_weight.shape
    widths = [x.shape[1] for x in dk]
    vmem = pl.BlockSpec(memory_space=pltpu.VMEM)
    return pl.pallas_call(
        functools.partial(state_kernel, groups, widths, len(after)),
        out_shape=[
            jax.ShapeDtypeStruct((total // 2, enc), jnp.bfloat16),
            jax.ShapeDtypeStruct((total // 2, enc), jnp.bfloat16),
        ],
        in_specs=[hbm_spec()] * (2 * len(dk) + 2) + [any_spec()] * len(after),
        out_specs=[vmem, vmem],
        scratch_shapes=[
            pltpu.VMEM((total, 2 * local_width), jnp.bfloat16),
            pltpu.VMEM((enc, 2 * local_width), jnp.bfloat16),
            pltpu.SemaphoreType.DMA((groups + 1, max(2, 2 * len(dk)))),
        ],
        compiler_params=pltpu.CompilerParams(vmem_limit_bytes=VMEM_GRANT),
        cost_estimate=pl.CostEstimate(
            flops=8 * total * enc * local_width, bytes_accessed=8 * total * enc, transcendentals=0
        ),
        name="state_terms",
    )(*in_hbm([*dk, *dv, key_weight, value_weight]), *after)


def fold_kernel(rows_ref, returned_ref, *refs):
    out_hbm, out_ref, sem = refs[-3:]
    out_ref[...] = jnp.zeros_like(out_ref)
    count = out_ref.shape[0]
    for s in range(returned_ref.shape[0]):
        row = rows_ref[s]

        @pl.when(row < count)
        def _():
            out_ref[row] += returned_ref[s].astype(jnp.float32)

    copy = pltpu.make_async_copy(out_ref, out_hbm, sem)
    copy.start()
    copy.wait()


def halve_kernel(choice_ref, keep_ref, recv_ref, *refs):
    stay_ref, send_ref = refs[-2:]
    total = keep_ref[...] + recv_ref[...].astype(jnp.float32)
    half = stay_ref.shape[0]
    upper = choice_ref[0] == 1
    stay_ref[...] = jnp.where(upper, total[half:], total[:half])
    send_ref[...] = jnp.where(upper, total[:half], total[half:]).astype(jnp.bfloat16)


def split_kernel(keep_ref, recv_ref, *refs):
    stay_ref, send_ref = refs[-2:]
    half = stay_ref.shape[0]
    total = keep_ref[...].astype(jnp.float32) + recv_ref[...].astype(jnp.float32)
    stay_ref[...] = total[:half]
    send_ref[...] = total[half:].astype(jnp.bfloat16)


def add_kernel(keep_ref, recv_ref, *refs):
    total = keep_ref[...].astype(jnp.float32) + recv_ref[...].astype(jnp.float32)
    refs[-1][...] = total.astype(refs[-1].dtype)


def order_kernel(halves, pairs, keep_ref, recv_ref, *refs):
    total = keep_ref[...].astype(jnp.float32) + recv_ref[...].astype(jnp.float32)
    piece = total.shape[0] // (halves * pairs)
    parts = [total[(h * pairs + p) * piece :][:piece] for p in range(pairs) for h in range(halves)]
    refs[-1][...] = jnp.concatenate(parts, axis=0).astype(refs[-1].dtype)


def join_kernel(choice_ref, own_ref, recv_ref, *refs):
    out_ref = refs[-1]
    upper = choice_ref[0] == 1
    own, recv = own_ref[...], recv_ref[...]
    rows = own.shape[0]
    if rows % 16:
        own, recv = own.astype(jnp.float32), recv.astype(jnp.float32)
        out = jnp.concatenate([jnp.where(upper, recv, own), jnp.where(upper, own, recv)], axis=0)
        out_ref[...] = out.astype(out_ref.dtype)
    else:
        out_ref[:rows] = jnp.where(upper, recv, own)
        out_ref[rows:] = jnp.where(upper, own, recv)


def place_kernel(start, choice_ref, own_ref, recv_ref, *refs):
    key_hbm, value_hbm, token_ref, key_ref, value_ref, sems = refs[-6:]
    token_ref[...] = jnp.zeros_like(token_ref)
    swapped = choice_ref[0] == 1
    own, recv = own_ref[...].astype(jnp.float32), recv_ref[...].astype(jnp.float32)
    columns = pl.ds(start, own.shape[1])
    key_ref[...] = jnp.where(swapped, recv, own)
    key_out = pltpu.make_async_copy(key_ref, key_hbm.at[:, columns], sems.at[0])
    key_out.start()
    value_ref[...] = jnp.where(swapped, own, recv)
    value_out = pltpu.make_async_copy(value_ref, value_hbm.at[:, columns], sems.at[1])
    value_out.start()
    key_out.wait()
    value_out.wait()


def small(kernel, name, scalars, arrays, outs, after, alias_in=(), out_specs=None, scratch=()):
    vmem = pl.BlockSpec(memory_space=pltpu.VMEM)
    extra = list(alias_in) + list(after)
    first = len(scalars) + len(arrays)
    return pl.pallas_call(
        kernel,
        out_shape=outs,
        in_specs=[pl.BlockSpec(memory_space=pltpu.SMEM)] * len(scalars)
        + [vmem] * len(arrays)
        + [hbm_spec()] * len(alias_in)
        + [any_spec()] * len(after),
        out_specs=out_specs or [vmem] * len(outs),
        scratch_shapes=list(scratch),
        input_output_aliases={first + i: i for i in range(len(alias_in))},
        compiler_params=pltpu.CompilerParams(vmem_limit_bytes=SMALL_GRANT),
        cost_estimate=CHEAP,
        name=name,
    )(*scalars, *arrays, *extra)


class Sum:
    def __init__(self, order, choices, start, enc, width):
        self.choices, self.start, self.enc, self.width = choices, start, enc, width
        self.count = len(order)
        self.steps = list(order) + list(reversed(order))
        self.at = 0

    def begin(self, keep, send):
        self.keep = keep
        self.moving = swap(send, "dp", self.steps[0])

    def load(self, step):
        return self.enc >> (step if step < self.count else 2 * self.count - 1 - step)

    def advance(self, after, outs):
        count, at = self.count, self.at
        self.at += 1
        rows = self.load(at)
        shape = lambda rows, dtype: jax.ShapeDtypeStruct((rows, self.width), dtype)
        if at < count - 1:
            choice = self.choices[self.steps[at + 1]]
            self.keep, send = small(
                halve_kernel, "halve", [choice], [self.keep, self.moving],
                [shape(rows // 2, jnp.float32), shape(rows // 2, jnp.bfloat16)], after,
            )
        elif at == count - 1:
            (send,) = small(add_kernel, "add", [], [self.keep, self.moving], [shape(rows, jnp.bfloat16)], after)
        elif at < 2 * count - 1:
            choice = self.choices[self.steps[at]]
            (send,) = small(
                join_kernel, "join", [choice], [self.own, self.moving], [shape(2 * rows, jnp.bfloat16)], after
            )
        else:
            choice = self.choices[self.steps[at]]
            full = pltpu.HBM(self.full, jnp.float32)
            block = pltpu.VMEM((self.enc, self.width), jnp.float32)
            token = jax.ShapeDtypeStruct((8, 128), jnp.float32)
            *outs, done = small(
                functools.partial(place_kernel, self.start), "place", [choice], [self.own, self.moving],
                [full, full, token], after, alias_in=outs,
                out_specs=[hbm_spec()] * 2 + [pl.BlockSpec(memory_space=pltpu.VMEM)],
                scratch=[block, block, pltpu.SemaphoreType.DMA((2,))],
            )
            return done, outs
        self.own = send
        self.moving = swap(send, "dp", self.steps[at + 1])
        return send, outs


def wavefront(chunks, steps, rest):
    order, done = [], [0] * chunks

    def step(j):
        order.append(f"sum{j}")
        done[j] += 1

    for j in range(chunks):
        order.append(f"heads{j}")
        for earlier in range(j):
            if done[earlier] < steps - 1:
                step(earlier)
    order.append("state")
    for j in [0] + list(range(chunks - 1, 0, -1)):
        step(j)
    period, left, launched = 0, rest, False
    while min(done) < steps or left:
        turn = list(done)
        for j in range(chunks):
            if turn[j] < steps - 1 - (j == chunks - 1):
                step(j)
        if left > 1 and period != 1:
            order.append("rest")
            left -= 1
        for j in range(chunks):
            if turn[j] == steps - 1:
                step(j)
        if turn[-1] == steps - 2:
            step(chunks - 1)
        if left == 1 and not launched and done[-1] >= steps - 1:
            order.append("launch")
            launched = True
        if left == 1 and launched and min(done) == steps:
            order.append("rest")
            left = 0
        period += 1
    return order


def body(queries, states, key_weight, value_weight, nbr_shard, nbr_row, out_grad):
    shards = lax.axis_size("dp")
    groups = lax.axis_size("mp")
    dp_bits, mp_bits = bits_of(shards), bits_of(groups)
    dp_index = lax.axis_index("dp")
    spans, neighbours = nbr_shard.shape
    pair_count = spans * neighbours
    tokens, local_width = queries.shape
    stored, slab_len, enc_width = states.shape
    head_dim = D // H
    capacity = max(2, (pair_count + shards - 1) // shards)
    slot_count = shards * capacity

    owners = nbr_shard.reshape(pair_count)
    row_index = nbr_row.reshape(pair_count)
    pair_ids = jnp.arange(pair_count, dtype=jnp.int32)
    before = (owners[:, None] == owners[None, :]) & (pair_ids[None, :] < pair_ids[:, None])
    slot_index = owners * capacity + jnp.sum(before.astype(jnp.int32), axis=1)
    matched = slot_index[:, None] == jnp.arange(slot_count, dtype=jnp.int32)[None, :]
    asked = stored + jnp.sum(jnp.where(matched, row_index[:, None] - stored, 0), axis=0)
    slot_pair = jnp.sum(jnp.where(matched, pair_ids[:, None], 0), axis=0)
    incoming = lax.all_to_all(
        asked.reshape(shards, capacity), "dp", split_axis=0, concat_axis=0, tiled=True
    ).reshape(slot_count)
    slab_rows = jnp.take(states, jnp.minimum(incoming, stored - 1), axis=0, mode="clip")
    halves = 2
    piece = slab_len // halves
    came = []
    for h in range(halves):
        out = slab_rows[:, h * piece : (h + 1) * piece].reshape(shards, capacity, piece, enc_width)
        came.append(lax.all_to_all(out, "dp", split_axis=0, concat_axis=0, tiled=True))
    blocks = {}
    for h in range(halves):
        if h:
            first = (1 << (mp_bits - 1), h - 1)
            came[h], blocks[first] = lax.optimization_barrier((came[h], blocks[first]))
        back = came[h].reshape(slot_count, piece, enc_width)
        picked = jnp.take(back, slot_index, axis=0, mode="clip").reshape(pair_count * piece, enc_width)
        blocks[0, h] = picked
        for bit in reversed(range(mp_bits)):
            for r in [r for r, k in blocks if k == h]:
                blocks[r | (1 << bit), h] = swap(blocks[r, h], "mp", bit)
    slabs = [blocks[r, h] for r in range(groups) for h in range(halves)]

    heads = local_width // head_dim
    counts = [min(2, heads - first) for first in range(0, heads, 2)]
    if len(counts) > 2 and counts[-1] == 2:
        counts[-1:] = [1, 1]
    bits = list(range(dp_bits))
    choices = [((dp_index >> bit) & 1).astype(jnp.int32).reshape(1) for bit in bits]
    sums = []
    for j, count in enumerate(counts):
        sums.append(Sum(bits, choices, sum(counts[:j]) * head_dim, enc_width, count * head_dim))
        sums[j].full = key_weight.shape

    after, chain, outs, dk, dv = [], [], [], [], []
    rest_bit, pending, held_for = 0, None, 0
    for name in wavefront(len(sums), len(sums[0].steps), mp_bits + 1):
        kind = name.rstrip("0123456789")
        number = int(name[len(kind) :] or 0)
        if kind == "heads":
            part = sums[number]
            chain, dk_part, dv_part, (keep, send) = run_heads(
                part.start, part.width, choices[0], slabs, key_weight, value_weight, queries, out_grad,
                chain, after, spans, head_dim,
            )
            dk.append(dk_part)
            dv.append(dv_part)
            part.begin(keep, send)
            after = [send]
        elif kind == "sum":
            done, outs = sums[number].advance(after, outs)
            after = [done]
            held_for -= 1
            if pending is not None and not held_for:
                pending, _ = lax.optimization_barrier((pending, done))
                moving, pending = swap(pending, "mp", 0), None
        elif kind == "state":
            keep, send = run_state(groups, dk, dv, key_weight, value_weight, after)
            pending, after, held_for = send, [send], len(sums)
        elif kind == "launch":
            outgoing, _ = lax.optimization_barrier((outgoing, after))
            returned = lax.all_to_all(outgoing, "dp", split_axis=0, concat_axis=0, tiled=True)
        elif rest_bit < mp_bits - 1:
            half = keep.shape[0] // 2
            keep, send = small(
                split_kernel, "split", [], [keep, moving],
                [jax.ShapeDtypeStruct((half, enc_width), t) for t in (jnp.float32, jnp.bfloat16)], after,
            )
            moving = swap(send, "mp", mp_bits - 1 - rest_bit)
            after = [send]
            rest_bit += 1
        elif rest_bit == mp_bits - 1:
            (pair_grad,) = small(
                functools.partial(order_kernel, halves, pair_count), "add", [], [keep, moving],
                [jax.ShapeDtypeStruct(keep.shape, jnp.bfloat16)], after,
            )
            after = [pair_grad]
            outgoing = jnp.take(
                pair_grad.reshape(pair_count, slab_len, enc_width), slot_pair, axis=0, mode="clip"
            ).reshape(shards, capacity, slab_len, enc_width)
            after = [outgoing]
            rest_bit += 1
        else:
            (state_total,) = small(
                fold_kernel, "fold", [incoming], [returned.reshape(slot_count, slab_len, enc_width)],
                [pltpu.HBM(states.shape, jnp.float32)], after, out_specs=[hbm_spec()],
                scratch=[pltpu.VMEM(states.shape, jnp.float32), pltpu.SemaphoreType.DMA],
            )
    return (chain[0], chain[1], state_total, outs[0], outs[1])


def solution(mesh):
    placed = (
        P("dp", "mp"),
        P("dp", "mp", None),
        P(None, "mp"),
        P(None, "mp"),
        P("dp", None),
        P("dp", None),
        P("dp", "mp"),
    )
    return jax.shard_map(
        body,
        mesh=mesh,
        in_specs=placed,
        out_specs=(P("dp", "mp"), P("dp", "mp"), P("dp", "mp", None), P(None, "mp"), P(None, "mp")),
        check_vma=False,
    )
```

```python
import functools

import jax
import jax.numpy as jnp
from jax import lax
from jax.experimental import pallas as pl
from jax.experimental.pallas import tpu as pltpu
from jax.sharding import PartitionSpec as P

D = 4096
H = 32
VMEM_GRANT = 28 * 1024 * 1024
SMALL_GRANT = 12 * 1024 * 1024
CHEAP = pl.CostEstimate(flops=1, bytes_accessed=1, transcendentals=0)


def bits_of(count):
    return count.bit_length() - 1


def swap(value, axis, bit):
    count = lax.axis_size(axis)
    return lax.ppermute(value, axis, [(i, i ^ (1 << bit)) for i in range(count)])


def any_spec():
    return pl.BlockSpec(memory_space=pl.ANY)


def in_hbm(arrays):
    return [pltpu.with_memory_space_constraint(x, pltpu.HBM) for x in arrays]


def hbm_spec():
    return pl.BlockSpec(memory_space=pltpu.HBM)


def head_kernel(groups, spans, head_dim, start, extra, *refs):
    flag_ref = refs[0]
    slabs = refs[1 : 1 + groups]
    wk_hbm, wv_hbm, q_hbm, g_hbm = refs[1 + groups : 5 + groups]
    att_hbm, dq_hbm, dk_hbm, dv_hbm, keep_ref, send_ref = refs[5 + groups + extra : 11 + groups + extra]
    rows, wk, wv, q_ref, g_ref, keys, values, att_ref, dq_ref, dk_ref, dv_ref, grads, sems = refs[11 + groups + extra :]
    tokens, width = q_ref.shape
    span_len = tokens // spans
    block = rows.shape[0] // groups
    part = block // spans
    scale = 1.0 / head_dim**0.5
    columns = pl.ds(start, width)

    def begin(source, target, sem):
        copy = pltpu.make_async_copy(source, target, sems.at[sem])
        copy.start()
        return copy

    weights_in = [begin(wk_hbm.at[:, columns], wk, groups), begin(wv_hbm.at[:, columns], wv, groups + 1)]
    rows_in = [begin(slabs[r], rows.at[pl.ds(r * block, block)], r) for r in range(groups)]
    tokens_in = [begin(q_hbm.at[:, columns], q_ref, groups + 2), begin(g_hbm.at[:, columns], g_ref, groups + 3)]
    for copy in weights_in:
        copy.wait()
    for r in range(0, groups, 2):
        rows_in[r].wait()
        rows_in[r + 1].wait()
        at = pl.ds(r * block, 2 * block)
        keys[at, :] = jnp.dot(rows[at, :], wk[...], preferred_element_type=jnp.float32).astype(jnp.bfloat16)
        values[at, :] = jnp.dot(rows[at, :], wv[...], preferred_element_type=jnp.float32).astype(jnp.bfloat16)
    for copy in tokens_in:
        copy.wait()

    def spread(x):
        heads = x.shape[1] // head_dim
        lane_head = lax.broadcasted_iota(jnp.int32, x.shape, 1) // head_dim
        zero = jnp.zeros_like(x)
        return jnp.concatenate([jnp.where(lane_head == h, x, zero) for h in range(heads)], axis=0)

    def collect(x):
        out = x[0:span_len]
        lane_head = lax.broadcasted_iota(jnp.int32, out.shape, 1) // head_dim
        for h in range(1, x.shape[1] // head_dim):
            out = jnp.where(lane_head == h, x[h * span_len : (h + 1) * span_len], out)
        return out

    def span_rows(ref, c, cols):
        return jnp.concatenate([ref[pl.ds(r * block + c * part, part), cols] for r in range(groups)], axis=0)

    contract_last = (((1,), (1,)), ((), ()))
    contract_first = (((0,), (0,)), ((), ()))
    at = [pl.ds(c * span_len, span_len) for c in range(spans)]
    swapped = flag_ref[0] == 1
    pair = 2 * head_dim
    for first in range(0, width, pair):
        cols = slice(first, min(first + pair, width))
        send_cols = slice(width + cols.start, width + cols.stop)
        every = range(spans)
        scores = [
            lax.dot_general(
                span_rows(keys, c, cols), spread(q_ref[at[c], cols]), contract_last,
                preferred_element_type=jnp.float32,
            )
            * scale
            for c in every
        ]
        prob_grad = [
            lax.dot_general(
                span_rows(values, c, cols), spread(g_ref[at[c], cols]), contract_last,
                preferred_element_type=jnp.float32,
            )
            for c in every
        ]
        weights = [jnp.exp(x - jnp.max(x, axis=0, keepdims=True)) for x in scores]
        probs = [x * (1.0 / jnp.sum(x, axis=0, keepdims=True)) for x in weights]
        low = [x.astype(jnp.bfloat16) for x in probs]
        row_dot = [jnp.sum(p * d, axis=0, keepdims=True) for p, d in zip(probs, prob_grad)]
        score_grad = [(scale * p * (d - t)).astype(jnp.bfloat16) for p, d, t in zip(probs, prob_grad, row_dot)]
        for c in every:
            dk = jnp.dot(score_grad[c], spread(q_ref[at[c], cols]), preferred_element_type=jnp.float32)
            dv = jnp.dot(low[c], spread(g_ref[at[c], cols]), preferred_element_type=jnp.float32)
            dk, dv = dk.astype(jnp.bfloat16), dv.astype(jnp.bfloat16)
            for r in range(groups):
                to = pl.ds(r * block + c * part, part)
                piece = slice(r * part, (r + 1) * part)
                dk_ref[to, cols] = dk[piece]
                dv_ref[to, cols] = dv[piece]
                grads[to, cols] = jnp.where(swapped, dv[piece], dk[piece])
                grads[to, send_cols] = jnp.where(swapped, dk[piece], dv[piece])
        for c in every:
            att = lax.dot_general(
                low[c], span_rows(values, c, cols), contract_first, preferred_element_type=jnp.float32
            )
            att_ref[at[c], cols] = collect(att).astype(jnp.bfloat16)
            dq = lax.dot_general(
                score_grad[c], span_rows(keys, c, cols), contract_first, preferred_element_type=jnp.float32
            )
            dq_ref[at[c], cols] = collect(dq).astype(jnp.bfloat16)
    results = [
        begin(att_ref, att_hbm.at[:, columns], 0),
        begin(dq_ref, dq_hbm.at[:, columns], 1),
        begin(dk_ref, dk_hbm, 2),
        begin(dv_ref, dv_hbm, 3),
    ]
    tile = 128
    for first in range(0, rows.shape[1], tile):
        to = slice(first, first + tile)
        both = lax.dot_general(rows[:, to], grads[...], contract_first, preferred_element_type=jnp.float32)
        keep_ref[to, :] = both[:, :width]
        send_ref[to, :] = both[:, width:].astype(jnp.bfloat16)
    for copy in results:
        copy.wait()


def run_heads(start, chunk, flag, slabs, key_weight, value_weight, queries, out_grad, chain, after, spans, head_dim):
    groups = len(slabs)
    tokens, local_width = queries.shape
    block, enc = slabs[0].shape
    total = groups * block
    bf = jnp.bfloat16
    extra = list(chain) + list(after)
    outs = pl.pallas_call(
        functools.partial(head_kernel, groups, spans, head_dim, start, len(extra)),
        out_shape=[
            pltpu.HBM((tokens, local_width), bf),
            pltpu.HBM((tokens, local_width), bf),
            pltpu.HBM((total, chunk), bf),
            pltpu.HBM((total, chunk), bf),
            jax.ShapeDtypeStruct((enc, chunk), jnp.float32),
            jax.ShapeDtypeStruct((enc, chunk), bf),
        ],
        in_specs=[pl.BlockSpec(memory_space=pltpu.SMEM)]
        + [any_spec()] * groups
        + [hbm_spec()] * (4 + len(chain))
        + [any_spec()] * len(after),
        out_specs=[hbm_spec()] * 4 + [pl.BlockSpec(memory_space=pltpu.VMEM)] * 2,
        scratch_shapes=[
            pltpu.VMEM((total, enc), bf),
            pltpu.VMEM((enc, chunk), bf),
            pltpu.VMEM((enc, chunk), bf),
            pltpu.VMEM((tokens, chunk), bf),
            pltpu.VMEM((tokens, chunk), bf),
            pltpu.VMEM((total, chunk), bf),
            pltpu.VMEM((total, chunk), bf),
            pltpu.VMEM((tokens, chunk), bf),
            pltpu.VMEM((tokens, chunk), bf),
            pltpu.VMEM((total, chunk), bf),
            pltpu.VMEM((total, chunk), bf),
            pltpu.VMEM((total, 2 * chunk), bf),
            pltpu.SemaphoreType.DMA((groups + 4,)),
        ],
        input_output_aliases={5 + groups + i: i for i in range(len(chain))},
        compiler_params=pltpu.CompilerParams(vmem_limit_bytes=VMEM_GRANT),
        cost_estimate=pl.CostEstimate(
            flops=2 * total * enc * chunk * 8, bytes_accessed=4 * total * enc, transcendentals=total * tokens
        ),
        name="heads",
    )(flag, *slabs, *in_hbm([key_weight, value_weight, queries, out_grad, *chain]), *after)
    return outs[:2], outs[2], outs[3], outs[4:]


def state_kernel(groups, widths, extra, *refs):
    count = len(widths)
    dk_hbm, dv_hbm = refs[:count], refs[count : 2 * count]
    wk_hbm, wv_hbm = refs[2 * count : 2 * count + 2]
    keep_ref, send_ref, grads, weights, sems = refs[2 * count + 2 + extra :]
    half = weights.shape[1] // 2
    block = grads.shape[0] // groups

    copies = [
        pltpu.make_async_copy(wk_hbm, weights.at[:, pl.ds(0, half)], sems.at[0, 0]),
        pltpu.make_async_copy(wv_hbm, weights.at[:, pl.ds(half, half)], sems.at[0, 1]),
    ]
    blocks = []
    for r in range(groups):
        rows = pl.ds(r * block, block)
        parts = []
        for j in range(count):
            first = sum(widths[:j])
            for k, source in enumerate((dk_hbm[j], dv_hbm[j])):
                target = grads.at[rows, pl.ds(k * half + first, widths[j])]
                parts.append(pltpu.make_async_copy(source.at[rows, :], target, sems.at[1 + r, 2 * j + k]))
        blocks.append(parts)
    for copy in copies:
        copy.start()
    for parts in blocks:
        for copy in parts:
            copy.start()
    for copy in copies:
        copy.wait()
    for r in range(groups):
        for copy in blocks[r]:
            copy.wait()
        to = pl.ds((r // 2) * block, block)
        for first in range(0, weights.shape[0], 256):
            cols = slice(first, min(first + 256, weights.shape[0]))
            term = lax.dot_general(
                grads[pl.ds(r * block, block), :], weights[cols, :], (((1,), (1,)), ((), ())),
                preferred_element_type=jnp.float32,
            )
            (send_ref if r % 2 else keep_ref)[to, cols] = term.astype(jnp.bfloat16)


def run_state(groups, dk, dv, key_weight, value_weight, after):
    total = dk[0].shape[0]
    enc, local_width = key_weight.shape
    widths = [x.shape[1] for x in dk]
    vmem = pl.BlockSpec(memory_space=pltpu.VMEM)
    return pl.pallas_call(
        functools.partial(state_kernel, groups, widths, len(after)),
        out_shape=[
            jax.ShapeDtypeStruct((total // 2, enc), jnp.bfloat16),
            jax.ShapeDtypeStruct((total // 2, enc), jnp.bfloat16),
        ],
        in_specs=[hbm_spec()] * (2 * len(dk) + 2) + [any_spec()] * len(after),
        out_specs=[vmem, vmem],
        scratch_shapes=[
            pltpu.VMEM((total, 2 * local_width), jnp.bfloat16),
            pltpu.VMEM((enc, 2 * local_width), jnp.bfloat16),
            pltpu.SemaphoreType.DMA((groups + 1, max(2, 2 * len(dk)))),
        ],
        compiler_params=pltpu.CompilerParams(vmem_limit_bytes=VMEM_GRANT),
        cost_estimate=pl.CostEstimate(
            flops=8 * total * enc * local_width, bytes_accessed=8 * total * enc, transcendentals=0
        ),
        name="state_terms",
    )(*in_hbm([*dk, *dv, key_weight, value_weight]), *after)


def fold_kernel(rows_ref, returned_ref, *refs):
    out_hbm, out_ref, sem = refs[-3:]
    out_ref[...] = jnp.zeros_like(out_ref)
    count = out_ref.shape[0]
    for s in range(returned_ref.shape[0]):
        row = rows_ref[s]

        @pl.when(row < count)
        def _():
            out_ref[row] += returned_ref[s].astype(jnp.float32)

    copy = pltpu.make_async_copy(out_ref, out_hbm, sem)
    copy.start()
    copy.wait()


def halve_kernel(choice_ref, keep_ref, recv_ref, *refs):
    stay_ref, send_ref = refs[-2:]
    total = keep_ref[...] + recv_ref[...].astype(jnp.float32)
    half = stay_ref.shape[0]
    upper = choice_ref[0] == 1
    stay_ref[...] = jnp.where(upper, total[half:], total[:half])
    send_ref[...] = jnp.where(upper, total[:half], total[half:]).astype(jnp.bfloat16)


def split_kernel(keep_ref, recv_ref, *refs):
    stay_ref, send_ref = refs[-2:]
    half = stay_ref.shape[0]
    total = keep_ref[...].astype(jnp.float32) + recv_ref[...].astype(jnp.float32)
    stay_ref[...] = total[:half]
    send_ref[...] = total[half:].astype(jnp.bfloat16)


def add_kernel(keep_ref, recv_ref, *refs):
    total = keep_ref[...].astype(jnp.float32) + recv_ref[...].astype(jnp.float32)
    refs[-1][...] = total.astype(refs[-1].dtype)


def order_kernel(halves, pairs, keep_ref, recv_ref, *refs):
    total = keep_ref[...].astype(jnp.float32) + recv_ref[...].astype(jnp.float32)
    piece = total.shape[0] // (halves * pairs)
    parts = [total[(h * pairs + p) * piece :][:piece] for p in range(pairs) for h in range(halves)]
    refs[-1][...] = jnp.concatenate(parts, axis=0).astype(refs[-1].dtype)


def join_kernel(choice_ref, own_ref, recv_ref, *refs):
    out_ref = refs[-1]
    upper = choice_ref[0] == 1
    own, recv = own_ref[...], recv_ref[...]
    rows = own.shape[0]
    if rows % 16:
        own, recv = own.astype(jnp.float32), recv.astype(jnp.float32)
        out = jnp.concatenate([jnp.where(upper, recv, own), jnp.where(upper, own, recv)], axis=0)
        out_ref[...] = out.astype(out_ref.dtype)
    else:
        out_ref[:rows] = jnp.where(upper, recv, own)
        out_ref[rows:] = jnp.where(upper, own, recv)


def place_kernel(start, choice_ref, own_ref, recv_ref, *refs):
    key_hbm, value_hbm, token_ref, key_ref, value_ref, sems = refs[-6:]
    token_ref[...] = jnp.zeros_like(token_ref)
    swapped = choice_ref[0] == 1
    own, recv = own_ref[...].astype(jnp.float32), recv_ref[...].astype(jnp.float32)
    columns = pl.ds(start, own.shape[1])
    key_ref[...] = jnp.where(swapped, recv, own)
    key_out = pltpu.make_async_copy(key_ref, key_hbm.at[:, columns], sems.at[0])
    key_out.start()
    value_ref[...] = jnp.where(swapped, own, recv)
    value_out = pltpu.make_async_copy(value_ref, value_hbm.at[:, columns], sems.at[1])
    value_out.start()
    key_out.wait()
    value_out.wait()


def small(kernel, name, scalars, arrays, outs, after, alias_in=(), out_specs=None, scratch=()):
    vmem = pl.BlockSpec(memory_space=pltpu.VMEM)
    extra = list(alias_in) + list(after)
    first = len(scalars) + len(arrays)
    return pl.pallas_call(
        kernel,
        out_shape=outs,
        in_specs=[pl.BlockSpec(memory_space=pltpu.SMEM)] * len(scalars)
        + [vmem] * len(arrays)
        + [hbm_spec()] * len(alias_in)
        + [any_spec()] * len(after),
        out_specs=out_specs or [vmem] * len(outs),
        scratch_shapes=list(scratch),
        input_output_aliases={first + i: i for i in range(len(alias_in))},
        compiler_params=pltpu.CompilerParams(vmem_limit_bytes=SMALL_GRANT),
        cost_estimate=CHEAP,
        name=name,
    )(*scalars, *arrays, *extra)


class Sum:
    def __init__(self, order, choices, start, enc, width):
        self.choices, self.start, self.enc, self.width = choices, start, enc, width
        self.count = len(order)
        self.steps = list(order) + list(reversed(order))
        self.at = 0

    def begin(self, keep, send):
        self.keep = keep
        self.moving = swap(send, "dp", self.steps[0])

    def load(self, step):
        return self.enc >> (step if step < self.count else 2 * self.count - 1 - step)

    def advance(self, after, outs):
        count, at = self.count, self.at
        self.at += 1
        rows = self.load(at)
        shape = lambda rows, dtype: jax.ShapeDtypeStruct((rows, self.width), dtype)
        if at < count - 1:
            choice = self.choices[self.steps[at + 1]]
            self.keep, send = small(
                halve_kernel, "halve", [choice], [self.keep, self.moving],
                [shape(rows // 2, jnp.float32), shape(rows // 2, jnp.bfloat16)], after,
            )
        elif at == count - 1:
            (send,) = small(add_kernel, "add", [], [self.keep, self.moving], [shape(rows, jnp.bfloat16)], after)
        elif at < 2 * count - 1:
            choice = self.choices[self.steps[at]]
            (send,) = small(
                join_kernel, "join", [choice], [self.own, self.moving], [shape(2 * rows, jnp.bfloat16)], after
            )
        else:
            choice = self.choices[self.steps[at]]
            full = pltpu.HBM(self.full, jnp.float32)
            block = pltpu.VMEM((self.enc, self.width), jnp.float32)
            token = jax.ShapeDtypeStruct((8, 128), jnp.float32)
            *outs, done = small(
                functools.partial(place_kernel, self.start), "place", [choice], [self.own, self.moving],
                [full, full, token], after, alias_in=outs,
                out_specs=[hbm_spec()] * 2 + [pl.BlockSpec(memory_space=pltpu.VMEM)],
                scratch=[block, block, pltpu.SemaphoreType.DMA((2,))],
            )
            return done, outs
        self.own = send
        self.moving = swap(send, "dp", self.steps[at + 1])
        return send, outs


def wavefront(chunks, steps, rest):
    order, done = [], [0] * chunks

    def step(j):
        order.append(f"sum{j}")
        done[j] += 1

    for j in range(chunks):
        order.append(f"heads{j}")
        for earlier in range(j):
            if done[earlier] < steps - 1:
                step(earlier)
    order.append("state")
    for j in [0] + list(range(chunks - 1, 0, -1)):
        step(j)
    period, left, launched = 0, rest, False
    while min(done) < steps or left:
        turn = list(done)
        for j in [chunks - 1, *range(chunks - 1)] if period == 1 else range(chunks):
            if turn[j] < steps - 1 - (j == chunks - 1):
                step(j)
        if left > 1 and period != 1:
            order.append("rest")
            left -= 1
        for j in range(chunks):
            if turn[j] == steps - 1:
                step(j)
        if turn[-1] == steps - 2:
            step(chunks - 1)
        if left == 1 and not launched and done[-1] >= steps - 1:
            order.append("launch")
            launched = True
        if left == 1 and launched and min(done) == steps:
            order.append("rest")
            left = 0
        period += 1
    return order


def body(queries, states, key_weight, value_weight, nbr_shard, nbr_row, out_grad):
    shards = lax.axis_size("dp")
    groups = lax.axis_size("mp")
    dp_bits, mp_bits = bits_of(shards), bits_of(groups)
    dp_index = lax.axis_index("dp")
    spans, neighbours = nbr_shard.shape
    pair_count = spans * neighbours
    tokens, local_width = queries.shape
    stored, slab_len, enc_width = states.shape
    head_dim = D // H
    capacity = max(2, (pair_count + shards - 1) // shards)
    slot_count = shards * capacity

    owners = nbr_shard.reshape(pair_count)
    row_index = nbr_row.reshape(pair_count)
    pair_ids = jnp.arange(pair_count, dtype=jnp.int32)
    before = (owners[:, None] == owners[None, :]) & (pair_ids[None, :] < pair_ids[:, None])
    slot_index = owners * capacity + jnp.sum(before.astype(jnp.int32), axis=1)
    matched = slot_index[:, None] == jnp.arange(slot_count, dtype=jnp.int32)[None, :]
    asked = stored + jnp.sum(jnp.where(matched, row_index[:, None] - stored, 0), axis=0)
    slot_pair = jnp.sum(jnp.where(matched, pair_ids[:, None], 0), axis=0)
    incoming = lax.all_to_all(
        asked.reshape(shards, capacity), "dp", split_axis=0, concat_axis=0, tiled=True
    ).reshape(slot_count)
    slab_rows = jnp.take(states, jnp.minimum(incoming, stored - 1), axis=0, mode="clip")
    halves = 2
    piece = slab_len // halves
    came = []
    for h in range(halves):
        out = slab_rows[:, h * piece : (h + 1) * piece].reshape(shards, capacity, piece, enc_width)
        came.append(lax.all_to_all(out, "dp", split_axis=0, concat_axis=0, tiled=True))
    blocks = {}
    for h in range(halves):
        if h:
            first = (1 << (mp_bits - 1), h - 1)
            came[h], blocks[first] = lax.optimization_barrier((came[h], blocks[first]))
        back = came[h].reshape(slot_count, piece, enc_width)
        picked = jnp.take(back, slot_index, axis=0, mode="clip").reshape(pair_count * piece, enc_width)
        blocks[0, h] = picked
        for bit in reversed(range(mp_bits)):
            for r in [r for r, k in blocks if k == h]:
                blocks[r | (1 << bit), h] = swap(blocks[r, h], "mp", bit)
    slabs = [blocks[r, h] for r in range(groups) for h in range(halves)]

    heads = local_width // head_dim
    counts = [min(2, heads - first) for first in range(0, heads, 2)]
    bits = list(range(dp_bits))
    choices = [((dp_index >> bit) & 1).astype(jnp.int32).reshape(1) for bit in bits]
    sums = []
    for j, count in enumerate(counts):
        sums.append(Sum(bits, choices, sum(counts[:j]) * head_dim, enc_width, count * head_dim))
        sums[j].full = key_weight.shape

    after, chain, outs, dk, dv = [], [], [], [], []
    rest_bit, pending, held_for = 0, None, 0
    for name in wavefront(len(sums), len(sums[0].steps), mp_bits + 1):
        kind = name.rstrip("0123456789")
        number = int(name[len(kind) :] or 0)
        if kind == "heads":
            part = sums[number]
            chain, dk_part, dv_part, (keep, send) = run_heads(
                part.start, part.width, choices[0], slabs, key_weight, value_weight, queries, out_grad,
                chain, after, spans, head_dim,
            )
            dk.append(dk_part)
            dv.append(dv_part)
            part.begin(keep, send)
            after = [send]
        elif kind == "sum":
            done, outs = sums[number].advance(after, outs)
            after = [done]
            held_for -= 1
            if pending is not None and not held_for:
                pending, _ = lax.optimization_barrier((pending, done))
                moving, pending = swap(pending, "mp", 0), None
        elif kind == "state":
            keep, send = run_state(groups, dk, dv, key_weight, value_weight, after)
            pending, after, held_for = send, [send], len(sums)
        elif kind == "launch":
            outgoing, _ = lax.optimization_barrier((outgoing, after))
            returned = lax.all_to_all(outgoing, "dp", split_axis=0, concat_axis=0, tiled=True)
        elif rest_bit < mp_bits - 1:
            half = keep.shape[0] // 2
            keep, send = small(
                split_kernel, "split", [], [keep, moving],
                [jax.ShapeDtypeStruct((half, enc_width), t) for t in (jnp.float32, jnp.bfloat16)], after,
            )
            moving = swap(send, "mp", mp_bits - 1 - rest_bit)
            after = [send]
            rest_bit += 1
        elif rest_bit == mp_bits - 1:
            (pair_grad,) = small(
                functools.partial(order_kernel, halves, pair_count), "add", [], [keep, moving],
                [jax.ShapeDtypeStruct(keep.shape, jnp.bfloat16)], after,
            )
            after = [pair_grad]
            outgoing = jnp.take(
                pair_grad.reshape(pair_count, slab_len, enc_width), slot_pair, axis=0, mode="clip"
            ).reshape(shards, capacity, slab_len, enc_width)
            after = [outgoing]
            rest_bit += 1
        else:
            (state_total,) = small(
                fold_kernel, "fold", [incoming], [returned.reshape(slot_count, slab_len, enc_width)],
                [pltpu.HBM(states.shape, jnp.float32)], after, out_specs=[hbm_spec()],
                scratch=[pltpu.VMEM(states.shape, jnp.float32), pltpu.SemaphoreType.DMA],
            )
    return (chain[0], chain[1], state_total, outs[0], outs[1])


def solution(mesh):
    placed = (
        P("dp", "mp"),
        P("dp", "mp", None),
        P(None, "mp"),
        P(None, "mp"),
        P("dp", None),
        P("dp", None),
        P("dp", "mp"),
    )
    return jax.shard_map(
        body,
        mesh=mesh,
        in_specs=placed,
        out_specs=(P("dp", "mp"), P("dp", "mp"), P("dp", "mp", None), P(None, "mp"), P(None, "mp")),
        check_vma=False,
    )
```

```python
import functools

import jax
import jax.numpy as jnp
from jax import lax
from jax.experimental import pallas as pl
from jax.experimental.pallas import tpu as pltpu
from jax.sharding import PartitionSpec as P

D = 4096
H = 32
VMEM_GRANT = 28 * 1024 * 1024
SMALL_GRANT = 12 * 1024 * 1024
CHEAP = pl.CostEstimate(flops=1, bytes_accessed=1, transcendentals=0)


def bits_of(count):
    return count.bit_length() - 1


def swap(value, axis, bit):
    count = lax.axis_size(axis)
    return lax.ppermute(value, axis, [(i, i ^ (1 << bit)) for i in range(count)])


def any_spec():
    return pl.BlockSpec(memory_space=pl.ANY)


def in_hbm(arrays):
    return [pltpu.with_memory_space_constraint(x, pltpu.HBM) for x in arrays]


def hbm_spec():
    return pl.BlockSpec(memory_space=pltpu.HBM)


def head_kernel(groups, spans, head_dim, start, extra, *refs):
    flag_ref = refs[0]
    slabs = refs[1 : 1 + groups]
    wk_hbm, wv_hbm, q_hbm, g_hbm = refs[1 + groups : 5 + groups]
    att_hbm, dq_hbm, dk_hbm, dv_hbm, keep_ref, send_ref = refs[5 + groups + extra : 11 + groups + extra]
    rows, wk, wv, q_ref, g_ref, keys, values, att_ref, dq_ref, dk_ref, dv_ref, grads, sems = refs[11 + groups + extra :]
    tokens, width = q_ref.shape
    span_len = tokens // spans
    block = rows.shape[0] // groups
    part = block // spans
    scale = 1.0 / head_dim**0.5
    columns = pl.ds(start, width)

    def begin(source, target, sem):
        copy = pltpu.make_async_copy(source, target, sems.at[sem])
        copy.start()
        return copy

    weights_in = [begin(wk_hbm.at[:, columns], wk, groups), begin(wv_hbm.at[:, columns], wv, groups + 1)]
    rows_in = [begin(slabs[r], rows.at[pl.ds(r * block, block)], r) for r in range(groups)]
    tokens_in = [begin(q_hbm.at[:, columns], q_ref, groups + 2), begin(g_hbm.at[:, columns], g_ref, groups + 3)]
    for copy in weights_in:
        copy.wait()
    for r in range(0, groups, 2):
        rows_in[r].wait()
        rows_in[r + 1].wait()
        at = pl.ds(r * block, 2 * block)
        keys[at, :] = jnp.dot(rows[at, :], wk[...], preferred_element_type=jnp.float32).astype(jnp.bfloat16)
        values[at, :] = jnp.dot(rows[at, :], wv[...], preferred_element_type=jnp.float32).astype(jnp.bfloat16)
    for copy in tokens_in:
        copy.wait()

    def spread(x):
        heads = x.shape[1] // head_dim
        lane_head = lax.broadcasted_iota(jnp.int32, x.shape, 1) // head_dim
        zero = jnp.zeros_like(x)
        return jnp.concatenate([jnp.where(lane_head == h, x, zero) for h in range(heads)], axis=0)

    def collect(x):
        out = x[0:span_len]
        lane_head = lax.broadcasted_iota(jnp.int32, out.shape, 1) // head_dim
        for h in range(1, x.shape[1] // head_dim):
            out = jnp.where(lane_head == h, x[h * span_len : (h + 1) * span_len], out)
        return out

    def span_rows(ref, c, cols):
        return jnp.concatenate([ref[pl.ds(r * block + c * part, part), cols] for r in range(groups)], axis=0)

    contract_last = (((1,), (1,)), ((), ()))
    contract_first = (((0,), (0,)), ((), ()))
    at = [pl.ds(c * span_len, span_len) for c in range(spans)]
    swapped = flag_ref[0] == 1
    pair = 2 * head_dim
    for first in range(0, width, pair):
        cols = slice(first, min(first + pair, width))
        send_cols = slice(width + cols.start, width + cols.stop)
        every = range(spans)
        scores = [
            lax.dot_general(
                span_rows(keys, c, cols), spread(q_ref[at[c], cols]), contract_last,
                preferred_element_type=jnp.float32,
            )
            * scale
            for c in every
        ]
        prob_grad = [
            lax.dot_general(
                span_rows(values, c, cols), spread(g_ref[at[c], cols]), contract_last,
                preferred_element_type=jnp.float32,
            )
            for c in every
        ]
        weights = [jnp.exp(x - jnp.max(x, axis=0, keepdims=True)) for x in scores]
        probs = [x * (1.0 / jnp.sum(x, axis=0, keepdims=True)) for x in weights]
        low = [x.astype(jnp.bfloat16) for x in probs]
        row_dot = [jnp.sum(p * d, axis=0, keepdims=True) for p, d in zip(probs, prob_grad)]
        score_grad = [(scale * p * (d - t)).astype(jnp.bfloat16) for p, d, t in zip(probs, prob_grad, row_dot)]
        for c in every:
            dk = jnp.dot(score_grad[c], spread(q_ref[at[c], cols]), preferred_element_type=jnp.float32)
            dv = jnp.dot(low[c], spread(g_ref[at[c], cols]), preferred_element_type=jnp.float32)
            dk, dv = dk.astype(jnp.bfloat16), dv.astype(jnp.bfloat16)
            for r in range(groups):
                to = pl.ds(r * block + c * part, part)
                piece = slice(r * part, (r + 1) * part)
                dk_ref[to, cols] = dk[piece]
                dv_ref[to, cols] = dv[piece]
                grads[to, cols] = jnp.where(swapped, dv[piece], dk[piece])
                grads[to, send_cols] = jnp.where(swapped, dk[piece], dv[piece])
        for c in every:
            att = lax.dot_general(
                low[c], span_rows(values, c, cols), contract_first, preferred_element_type=jnp.float32
            )
            att_ref[at[c], cols] = collect(att).astype(jnp.bfloat16)
            dq = lax.dot_general(
                score_grad[c], span_rows(keys, c, cols), contract_first, preferred_element_type=jnp.float32
            )
            dq_ref[at[c], cols] = collect(dq).astype(jnp.bfloat16)
    results = [
        begin(att_ref, att_hbm.at[:, columns], 0),
        begin(dq_ref, dq_hbm.at[:, columns], 1),
        begin(dk_ref, dk_hbm, 2),
        begin(dv_ref, dv_hbm, 3),
    ]
    tile = 128
    for first in range(0, rows.shape[1], tile):
        to = slice(first, first + tile)
        both = lax.dot_general(rows[:, to], grads[...], contract_first, preferred_element_type=jnp.float32)
        keep_ref[to, :] = both[:, :width]
        send_ref[to, :] = both[:, width:].astype(jnp.bfloat16)
    for copy in results:
        copy.wait()


def run_heads(start, chunk, flag, slabs, key_weight, value_weight, queries, out_grad, chain, after, spans, head_dim):
    groups = len(slabs)
    tokens, local_width = queries.shape
    block, enc = slabs[0].shape
    total = groups * block
    bf = jnp.bfloat16
    extra = list(chain) + list(after)
    outs = pl.pallas_call(
        functools.partial(head_kernel, groups, spans, head_dim, start, len(extra)),
        out_shape=[
            pltpu.HBM((tokens, local_width), bf),
            pltpu.HBM((tokens, local_width), bf),
            pltpu.HBM((total, chunk), bf),
            pltpu.HBM((total, chunk), bf),
            jax.ShapeDtypeStruct((enc, chunk), jnp.float32),
            jax.ShapeDtypeStruct((enc, chunk), bf),
        ],
        in_specs=[pl.BlockSpec(memory_space=pltpu.SMEM)]
        + [any_spec()] * groups
        + [hbm_spec()] * (4 + len(chain))
        + [any_spec()] * len(after),
        out_specs=[hbm_spec()] * 4 + [pl.BlockSpec(memory_space=pltpu.VMEM)] * 2,
        scratch_shapes=[
            pltpu.VMEM((total, enc), bf),
            pltpu.VMEM((enc, chunk), bf),
            pltpu.VMEM((enc, chunk), bf),
            pltpu.VMEM((tokens, chunk), bf),
            pltpu.VMEM((tokens, chunk), bf),
            pltpu.VMEM((total, chunk), bf),
            pltpu.VMEM((total, chunk), bf),
            pltpu.VMEM((tokens, chunk), bf),
            pltpu.VMEM((tokens, chunk), bf),
            pltpu.VMEM((total, chunk), bf),
            pltpu.VMEM((total, chunk), bf),
            pltpu.VMEM((total, 2 * chunk), bf),
            pltpu.SemaphoreType.DMA((groups + 4,)),
        ],
        input_output_aliases={5 + groups + i: i for i in range(len(chain))},
        compiler_params=pltpu.CompilerParams(vmem_limit_bytes=VMEM_GRANT),
        cost_estimate=pl.CostEstimate(
            flops=2 * total * enc * chunk * 8, bytes_accessed=4 * total * enc, transcendentals=total * tokens
        ),
        name="heads",
    )(flag, *slabs, *in_hbm([key_weight, value_weight, queries, out_grad, *chain]), *after)
    return outs[:2], outs[2], outs[3], outs[4:]


def state_kernel(groups, widths, extra, *refs):
    count = len(widths)
    dk_hbm, dv_hbm = refs[:count], refs[count : 2 * count]
    wk_hbm, wv_hbm = refs[2 * count : 2 * count + 2]
    keep_ref, send_ref, grads, weights, sems = refs[2 * count + 2 + extra :]
    half = weights.shape[1] // 2
    block = grads.shape[0] // groups

    copies = [
        pltpu.make_async_copy(wk_hbm, weights.at[:, pl.ds(0, half)], sems.at[0, 0]),
        pltpu.make_async_copy(wv_hbm, weights.at[:, pl.ds(half, half)], sems.at[0, 1]),
    ]
    blocks = []
    for r in range(groups):
        rows = pl.ds(r * block, block)
        parts = []
        for j in range(count):
            first = sum(widths[:j])
            for k, source in enumerate((dk_hbm[j], dv_hbm[j])):
                target = grads.at[rows, pl.ds(k * half + first, widths[j])]
                parts.append(pltpu.make_async_copy(source.at[rows, :], target, sems.at[1 + r, 2 * j + k]))
        blocks.append(parts)
    for copy in copies:
        copy.start()
    for parts in blocks:
        for copy in parts:
            copy.start()
    for copy in copies:
        copy.wait()
    for r in range(groups):
        for copy in blocks[r]:
            copy.wait()
        to = pl.ds((r // 2) * block, block)
        for first in range(0, weights.shape[0], 256):
            cols = slice(first, min(first + 256, weights.shape[0]))
            term = lax.dot_general(
                grads[pl.ds(r * block, block), :], weights[cols, :], (((1,), (1,)), ((), ())),
                preferred_element_type=jnp.float32,
            )
            (send_ref if r % 2 else keep_ref)[to, cols] = term.astype(jnp.bfloat16)


def run_state(groups, dk, dv, key_weight, value_weight, after):
    total = dk[0].shape[0]
    enc, local_width = key_weight.shape
    widths = [x.shape[1] for x in dk]
    vmem = pl.BlockSpec(memory_space=pltpu.VMEM)
    return pl.pallas_call(
        functools.partial(state_kernel, groups, widths, len(after)),
        out_shape=[
            jax.ShapeDtypeStruct((total // 2, enc), jnp.bfloat16),
            jax.ShapeDtypeStruct((total // 2, enc), jnp.bfloat16),
        ],
        in_specs=[hbm_spec()] * (2 * len(dk) + 2) + [any_spec()] * len(after),
        out_specs=[vmem, vmem],
        scratch_shapes=[
            pltpu.VMEM((total, 2 * local_width), jnp.bfloat16),
            pltpu.VMEM((enc, 2 * local_width), jnp.bfloat16),
            pltpu.SemaphoreType.DMA((groups + 1, max(2, 2 * len(dk)))),
        ],
        compiler_params=pltpu.CompilerParams(vmem_limit_bytes=VMEM_GRANT),
        cost_estimate=pl.CostEstimate(
            flops=8 * total * enc * local_width, bytes_accessed=8 * total * enc, transcendentals=0
        ),
        name="state_terms",
    )(*in_hbm([*dk, *dv, key_weight, value_weight]), *after)


def fold_kernel(rows_ref, returned_ref, *refs):
    out_hbm, out_ref, sem = refs[-3:]
    out_ref[...] = jnp.zeros_like(out_ref)
    count = out_ref.shape[0]
    for s in range(returned_ref.shape[0]):
        row = rows_ref[s]

        @pl.when(row < count)
        def _():
            out_ref[row] += returned_ref[s].astype(jnp.float32)

    copy = pltpu.make_async_copy(out_ref, out_hbm, sem)
    copy.start()
    copy.wait()


def halve_kernel(choice_ref, keep_ref, recv_ref, *refs):
    stay_ref, send_ref = refs[-2:]
    total = keep_ref[...] + recv_ref[...].astype(jnp.float32)
    half = stay_ref.shape[0]
    upper = choice_ref[0] == 1
    stay_ref[...] = jnp.where(upper, total[half:], total[:half])
    send_ref[...] = jnp.where(upper, total[:half], total[half:]).astype(jnp.bfloat16)


def split_kernel(keep_ref, recv_ref, *refs):
    stay_ref, send_ref = refs[-2:]
    half = stay_ref.shape[0]
    total = keep_ref[...].astype(jnp.float32) + recv_ref[...].astype(jnp.float32)
    stay_ref[...] = total[:half]
    send_ref[...] = total[half:].astype(jnp.bfloat16)


def add_kernel(keep_ref, recv_ref, *refs):
    total = keep_ref[...].astype(jnp.float32) + recv_ref[...].astype(jnp.float32)
    refs[-1][...] = total.astype(refs[-1].dtype)


def order_kernel(halves, pairs, keep_ref, recv_ref, *refs):
    total = keep_ref[...].astype(jnp.float32) + recv_ref[...].astype(jnp.float32)
    piece = total.shape[0] // (halves * pairs)
    parts = [total[(h * pairs + p) * piece :][:piece] for p in range(pairs) for h in range(halves)]
    refs[-1][...] = jnp.concatenate(parts, axis=0).astype(refs[-1].dtype)


def join_kernel(choice_ref, own_ref, recv_ref, *refs):
    out_ref = refs[-1]
    upper = choice_ref[0] == 1
    own, recv = own_ref[...], recv_ref[...]
    rows = own.shape[0]
    if rows % 16:
        own, recv = own.astype(jnp.float32), recv.astype(jnp.float32)
        out = jnp.concatenate([jnp.where(upper, recv, own), jnp.where(upper, own, recv)], axis=0)
        out_ref[...] = out.astype(out_ref.dtype)
    else:
        out_ref[:rows] = jnp.where(upper, recv, own)
        out_ref[rows:] = jnp.where(upper, own, recv)


def place_kernel(start, choice_ref, own_ref, recv_ref, *refs):
    key_hbm, value_hbm, token_ref, key_ref, value_ref, sems = refs[-6:]
    token_ref[...] = jnp.zeros_like(token_ref)
    swapped = choice_ref[0] == 1
    own, recv = own_ref[...].astype(jnp.float32), recv_ref[...].astype(jnp.float32)
    columns = pl.ds(start, own.shape[1])
    key_ref[...] = jnp.where(swapped, recv, own)
    key_out = pltpu.make_async_copy(key_ref, key_hbm.at[:, columns], sems.at[0])
    key_out.start()
    value_ref[...] = jnp.where(swapped, own, recv)
    value_out = pltpu.make_async_copy(value_ref, value_hbm.at[:, columns], sems.at[1])
    value_out.start()
    key_out.wait()
    value_out.wait()


def small(kernel, name, scalars, arrays, outs, after, alias_in=(), out_specs=None, scratch=()):
    vmem = pl.BlockSpec(memory_space=pltpu.VMEM)
    extra = list(alias_in) + list(after)
    first = len(scalars) + len(arrays)
    return pl.pallas_call(
        kernel,
        out_shape=outs,
        in_specs=[pl.BlockSpec(memory_space=pltpu.SMEM)] * len(scalars)
        + [vmem] * len(arrays)
        + [hbm_spec()] * len(alias_in)
        + [any_spec()] * len(after),
        out_specs=out_specs or [vmem] * len(outs),
        scratch_shapes=list(scratch),
        input_output_aliases={first + i: i for i in range(len(alias_in))},
        compiler_params=pltpu.CompilerParams(vmem_limit_bytes=SMALL_GRANT),
        cost_estimate=CHEAP,
        name=name,
    )(*scalars, *arrays, *extra)


class Sum:
    def __init__(self, order, choices, start, enc, width):
        self.choices, self.start, self.enc, self.width = choices, start, enc, width
        self.count = len(order)
        self.steps = list(order) + list(reversed(order))
        self.at = 0

    def begin(self, keep, send):
        self.keep = keep
        self.moving = swap(send, "dp", self.steps[0])

    def load(self, step):
        return self.enc >> (step if step < self.count else 2 * self.count - 1 - step)

    def advance(self, after, outs):
        count, at = self.count, self.at
        self.at += 1
        rows = self.load(at)
        shape = lambda rows, dtype: jax.ShapeDtypeStruct((rows, self.width), dtype)
        if at < count - 1:
            choice = self.choices[self.steps[at + 1]]
            self.keep, send = small(
                halve_kernel, "halve", [choice], [self.keep, self.moving],
                [shape(rows // 2, jnp.float32), shape(rows // 2, jnp.bfloat16)], after,
            )
        elif at == count - 1:
            (send,) = small(add_kernel, "add", [], [self.keep, self.moving], [shape(rows, jnp.bfloat16)], after)
        elif at < 2 * count - 1:
            choice = self.choices[self.steps[at]]
            (send,) = small(
                join_kernel, "join", [choice], [self.own, self.moving], [shape(2 * rows, jnp.bfloat16)], after
            )
        else:
            choice = self.choices[self.steps[at]]
            full = pltpu.HBM(self.full, jnp.float32)
            block = pltpu.VMEM((self.enc, self.width), jnp.float32)
            token = jax.ShapeDtypeStruct((8, 128), jnp.float32)
            *outs, done = small(
                functools.partial(place_kernel, self.start), "place", [choice], [self.own, self.moving],
                [full, full, token], after, alias_in=outs,
                out_specs=[hbm_spec()] * 2 + [pl.BlockSpec(memory_space=pltpu.VMEM)],
                scratch=[block, block, pltpu.SemaphoreType.DMA((2,))],
            )
            return done, outs
        self.own = send
        self.moving = swap(send, "dp", self.steps[at + 1])
        return send, outs


def wavefront(chunks, steps, rest):
    order, done = [], [0] * chunks

    def step(j):
        order.append(f"sum{j}")
        done[j] += 1

    for j in range(chunks):
        order.append(f"heads{j}")
        for earlier in range(j):
            if done[earlier] < steps - 1:
                step(earlier)
    order.append("state")
    for j in [0] + list(range(chunks - 1, 0, -1)):
        step(j)
    period, left, launched = 0, rest, False
    while min(done) < steps or left:
        turn = list(done)
        for j in range(chunks):
            if turn[j] < steps - 1 - (j == chunks - 1):
                step(j)
        if left > 1 and period != 1:
            order.append("rest")
            left -= 1
        for j in range(chunks):
            if turn[j] == steps - 1:
                step(j)
        if turn[-1] == steps - 2:
            step(chunks - 1)
        if left == 1 and not launched and done[-1] >= steps - 1:
            order.append("launch")
            launched = True
        if left == 1 and launched and min(done) == steps:
            order.append("rest")
            left = 0
        period += 1
    return order


def body(queries, states, key_weight, value_weight, nbr_shard, nbr_row, out_grad):
    shards = lax.axis_size("dp")
    groups = lax.axis_size("mp")
    dp_bits, mp_bits = bits_of(shards), bits_of(groups)
    dp_index = lax.axis_index("dp")
    spans, neighbours = nbr_shard.shape
    pair_count = spans * neighbours
    tokens, local_width = queries.shape
    stored, slab_len, enc_width = states.shape
    head_dim = D // H
    capacity = max(2, (pair_count + shards - 1) // shards)
    slot_count = shards * capacity

    owners = nbr_shard.reshape(pair_count)
    row_index = nbr_row.reshape(pair_count)
    pair_ids = jnp.arange(pair_count, dtype=jnp.int32)
    before = (owners[:, None] == owners[None, :]) & (pair_ids[None, :] < pair_ids[:, None])
    slot_index = owners * capacity + jnp.sum(before.astype(jnp.int32), axis=1)
    matched = slot_index[:, None] == jnp.arange(slot_count, dtype=jnp.int32)[None, :]
    asked = stored + jnp.sum(jnp.where(matched, row_index[:, None] - stored, 0), axis=0)
    slot_pair = jnp.sum(jnp.where(matched, pair_ids[:, None], 0), axis=0)
    incoming = lax.all_to_all(
        asked.reshape(shards, capacity), "dp", split_axis=0, concat_axis=0, tiled=True
    ).reshape(slot_count)
    wanted = jnp.minimum(incoming, stored - 1)
    halves = 2
    piece = slab_len // halves
    came = []
    for h in range(halves):
        out = jnp.take(states[:, h * piece : (h + 1) * piece], wanted, axis=0, mode="clip")
        out = out.reshape(shards, capacity, piece, enc_width)
        came.append(lax.all_to_all(out, "dp", split_axis=0, concat_axis=0, tiled=True))
    blocks = {}
    for h in range(halves):
        if h:
            first = (1 << (mp_bits - 1), h - 1)
            came[h], blocks[first] = lax.optimization_barrier((came[h], blocks[first]))
        back = came[h].reshape(slot_count, piece, enc_width)
        picked = jnp.take(back, slot_index, axis=0, mode="clip").reshape(pair_count * piece, enc_width)
        blocks[0, h] = picked
        for bit in reversed(range(mp_bits)):
            for r in [r for r, k in blocks if k == h]:
                blocks[r | (1 << bit), h] = swap(blocks[r, h], "mp", bit)
    slabs = [blocks[r, h] for r in range(groups) for h in range(halves)]

    heads = local_width // head_dim
    counts = [min(2, heads - first) for first in range(0, heads, 2)]
    bits = list(range(dp_bits))
    choices = [((dp_index >> bit) & 1).astype(jnp.int32).reshape(1) for bit in bits]
    sums = []
    for j, count in enumerate(counts):
        sums.append(Sum(bits, choices, sum(counts[:j]) * head_dim, enc_width, count * head_dim))
        sums[j].full = key_weight.shape

    after, chain, outs, dk, dv = [], [], [], [], []
    rest_bit, pending, held_for = 0, None, 0
    for name in wavefront(len(sums), len(sums[0].steps), mp_bits + 1):
        kind = name.rstrip("0123456789")
        number = int(name[len(kind) :] or 0)
        if kind == "heads":
            part = sums[number]
            chain, dk_part, dv_part, (keep, send) = run_heads(
                part.start, part.width, choices[0], slabs, key_weight, value_weight, queries, out_grad,
                chain, after, spans, head_dim,
            )
            dk.append(dk_part)
            dv.append(dv_part)
            part.begin(keep, send)
            after = [send]
        elif kind == "sum":
            done, outs = sums[number].advance(after, outs)
            after = [done]
            held_for -= 1
            if pending is not None and not held_for:
                pending, _ = lax.optimization_barrier((pending, done))
                moving, pending = swap(pending, "mp", 0), None
        elif kind == "state":
            keep, send = run_state(groups, dk, dv, key_weight, value_weight, after)
            pending, after, held_for = send, [send], len(sums)
        elif kind == "launch":
            outgoing, _ = lax.optimization_barrier((outgoing, after))
            returned = lax.all_to_all(outgoing, "dp", split_axis=0, concat_axis=0, tiled=True)
        elif rest_bit < mp_bits - 1:
            half = keep.shape[0] // 2
            keep, send = small(
                split_kernel, "split", [], [keep, moving],
                [jax.ShapeDtypeStruct((half, enc_width), t) for t in (jnp.float32, jnp.bfloat16)], after,
            )
            moving = swap(send, "mp", mp_bits - 1 - rest_bit)
            after = [send]
            rest_bit += 1
        elif rest_bit == mp_bits - 1:
            (pair_grad,) = small(
                functools.partial(order_kernel, halves, pair_count), "add", [], [keep, moving],
                [jax.ShapeDtypeStruct(keep.shape, jnp.bfloat16)], after,
            )
            after = [pair_grad]
            outgoing = jnp.take(
                pair_grad.reshape(pair_count, slab_len, enc_width), slot_pair, axis=0, mode="clip"
            ).reshape(shards, capacity, slab_len, enc_width)
            after = [outgoing]
            rest_bit += 1
        else:
            (state_total,) = small(
                fold_kernel, "fold", [incoming], [returned.reshape(slot_count, slab_len, enc_width)],
                [pltpu.HBM(states.shape, jnp.float32)], after, out_specs=[hbm_spec()],
                scratch=[pltpu.VMEM(states.shape, jnp.float32), pltpu.SemaphoreType.DMA],
            )
    return (chain[0], chain[1], state_total, outs[0], outs[1])


def solution(mesh):
    placed = (
        P("dp", "mp"),
        P("dp", "mp", None),
        P(None, "mp"),
        P(None, "mp"),
        P("dp", None),
        P("dp", None),
        P("dp", "mp"),
    )
    return jax.shard_map(
        body,
        mesh=mesh,
        in_specs=placed,
        out_specs=(P("dp", "mp"), P("dp", "mp"), P("dp", "mp", None), P(None, "mp"), P(None, "mp")),
        check_vma=False,
    )
```
